32 devices in a mesh: dp: 8 (over z, y), mp: 4 (over x, core).
Axes of the slice: x: 2, y: 2, z: 4, core: 2. Of those that a mesh axis runs over, the one named last changes fastest.
Arguments:
- inputs: bfloat16 [7840, 768], P('dp'), may hold values from -6 to 6
- image_of_row: int32 [7840], P('dp'), may hold values from 0 to 4, as said below
- gain_first: bfloat16 [768], replicated, may hold values from 0.5 to 1.5
- shift_first: bfloat16 [768], replicated, may hold values from -3 to 3
- qkv_weight: bfloat16 [3, 768, 768], P(None, None, 'mp'), may hold values from -0.21875 to 0.21875
- qv_bias: bfloat16 [2, 768], P(None, 'mp'), may hold values from -3 to 3
- out_weight: bfloat16 [768, 768], P('mp'), may hold values from -1.75 to 1.75
- out_bias: bfloat16 [768], replicated, may hold values from -3 to 3
- gain_second: bfloat16 [768], replicated, may hold values from 0.5 to 1.5
- shift_second: bfloat16 [768], replicated, may hold values from -3 to 3
- up_weight: bfloat16 [768, 3072], P(None, 'mp'), may hold values from -0.21875 to 0.21875
- up_bias: bfloat16 [3072], P('mp'), may hold values from -3 to 3
- down_weight: bfloat16 [3072, 768], P('mp'), may hold values from -0.15625 to 0.15625
- down_bias: bfloat16 [768], replicated, may hold values from -3 to 3
- cotangent: bfloat16 [7840, 768], P(('dp', 'mp')), may hold values from -6 to 6
Outputs:
- block_out: float32 [7840, 768], P(('dp', 'mp'))
- input_grad: float32 [7840, 768], P(('dp', 'mp'))
- grad_gain_first: float32 [768], replicated
- grad_shift_first: float32 [768], replicated
- grad_qkv: float32 [3, 768, 768], P(None, None, 'mp')
- grad_qv: float32 [2, 768], P(None, 'mp')
- grad_out: float32 [768, 768], P('mp')
- grad_out_bias: float32 [768], replicated
- grad_gain_second: float32 [768], replicated
- grad_shift_second: float32 [768], replicated
- grad_up: float32 [768, 3072], P(None, 'mp')
- grad_up_bias: float32 [3072], P('mp')
- grad_down: float32 [3072, 768], P('mp')
- grad_down_bias: float32 [768], replicated
The draws below stay inside these ranges and needn't reach their ends.
Inputs may be any that keep to these rules, and one draw needn't show every extreme that they name: `image_of_row`: each index of dp holds 980 patches as 1 group of 980 rows in order; a group is either one image of 784 patches followed by one of 196, or five images of 196. Entries number the images of an index of dp from 0 upward in row order. In every draw some index of dp holds only five-image groups and some only two-image groups.
All inputs are finite; a program needn't handle non-finite values.
Results may differ from the reference program's by a relative error of at most 0.018.
Values may be sent and summed in bfloat16 or wider, within the bound.
A program may use at most 128 MiB of HBM per device.

```python
import jax
import jax.numpy as jnp
from jax import lax

D = 768
HD = 64
FF = 3072
P_LO = 196
GROUPS_DEV = 1
TOK_DEV = 980
TOKENS = 7840
N_DP = 8


def draw_image_of_row(key, part):
    devices = TOKENS // TOK_DEV
    group_kinds = jax.random.randint(jax.random.fold_in(key, 11), (devices, GROUPS_DEV), 0, 2)
    shuffled = jax.random.permutation(jax.random.fold_in(key, 12), devices)
    device_ids = jnp.arange(devices)
    group_kinds = jnp.where((device_ids == shuffled[0])[:, None], 0, group_kinds)
    group_kinds = jnp.where((device_ids == shuffled[1])[:, None], 1, group_kinds)
    counts = jnp.where(group_kinds == 1, 2, 5)
    offsets = jnp.cumsum(counts, axis=1) - counts
    position = jnp.arange(5 * P_LO)
    five_ids = position // P_LO
    two_ids = (position >= 4 * P_LO).astype(jnp.int32)
    local_ids = jnp.where(group_kinds[:, :, None] == 1, two_ids[None, None, :], five_ids[None, None, :])
    return (offsets[:, :, None] + local_ids).reshape(TOKENS).astype(jnp.int32)


def shard_levels(key, shape, shards, low, top_value):
    factor_of = 1.0
    for dim, parts in shards:
        draws = jax.random.uniform(jax.random.fold_in(jax.random.fold_in(key, 6), dim), (parts,), jnp.float32, low / len(shards), top_value / len(shards))
        factor_of = factor_of * jnp.repeat(jnp.exp(draws), shape[dim] // parts).reshape((-1,) + (1,) * (len(shape) - 1 - dim))
    return factor_of


def centred(key, extent, scale, bound, shards=(), dtype=jnp.bfloat16):
    drawn = scale * jax.random.normal(key, extent, jnp.float32)
    if shards:
        drawn = drawn * shard_levels(key, extent, shards, -0.22, 0.18)
    return jnp.clip(drawn, -bound, bound).astype(dtype)


def setup_inputs(seed: int = 0) -> dict:
    seeds = jax.random.split(jax.random.key(seed), 16)
    inputs = centred(seeds[0], (TOKENS, D), 1.0, 6.0, ((0, 8),))
    image_of_row = draw_image_of_row(jax.random.fold_in(seeds[15], 71), 0)
    gain_first = jnp.clip(1.0 + 0.1 * jax.random.normal(seeds[2], (D,), jnp.float32), 0.5, 1.5).astype(jnp.bfloat16)
    shift_first = centred(seeds[3], (D,), 0.3, 3.0)
    qkv_weight = centred(seeds[4], (3, D, D), D ** -0.5, 0.21875, ((2, 4),))
    qv_bias = centred(seeds[5], (2, D), 0.3, 3.0, ((1, 4),))
    out_weight = centred(seeds[6], (D, D), (max(D // 64, 4)) ** -0.5, 1.75, ((0, 4),))
    out_bias = centred(seeds[7], (D,), 0.3, 3.0)
    gain_second = jnp.clip(1.0 + 0.1 * jax.random.normal(seeds[8], (D,), jnp.float32), 0.5, 1.5).astype(jnp.bfloat16)
    shift_second = centred(seeds[9], (D,), 0.3, 3.0)
    up_weight = centred(seeds[10], (D, FF), D ** -0.5, 0.21875, ((1, 4),))
    up_bias = centred(seeds[11], (FF,), 0.3, 3.0, ((0, 4),))
    down_weight = centred(seeds[12], (FF, D), (FF // 2) ** -0.5, 0.15625, ((0, 4),))
    down_bias = centred(seeds[13], (D,), 0.3, 3.0)
    cotangent = centred(seeds[14], (TOKENS, D), 1.0, 6.0, ((0, 32),))
    return dict(inputs=inputs, image_of_row=image_of_row, gain_first=gain_first, shift_first=shift_first, qkv_weight=qkv_weight, qv_bias=qv_bias, out_weight=out_weight, out_bias=out_bias, gain_second=gain_second, shift_second=shift_second, up_weight=up_weight, up_bias=up_bias, down_weight=down_weight, down_bias=down_bias, cotangent=cotangent)


EPSILON = 1e-06
HIGH = lax.Precision.HIGHEST

@jax.custom_vjp
def low(v):
    return lax.optimization_barrier(v.astype(jnp.bfloat16)).astype(jnp.float32)

@jax.custom_vjp
def low_back(v):
    return v

def low_keep(v):
    return (low(v), None)

def low_pass(kept, grad):
    return (grad,)

def back_keep(v):
    return (v, None)

def back_low(kept, grad):
    return (low(grad),)
low.defvjp(low_keep, low_pass)
low_back.defvjp(back_keep, back_low)

def product(left, right):
    return jnp.dot(left, right, precision=HIGH, preferred_element_type=jnp.float32)

def layer_norm(values, gain, shift):
    center = values - lax.optimization_barrier(jnp.mean(values, axis=1, keepdims=True))
    factor = lax.rsqrt(lax.optimization_barrier(jnp.mean(center * center, axis=1, keepdims=True)) + EPSILON)
    return center * factor * gain + shift

def block_rows(rows_in, image_ids, weights):
    gain_a, shift_a, qkv, biases_qv, weight_out, bias_out, gain_b, shift_b, weight_up, bias_up, weight_down, bias_down = weights
    act_first = low(layer_norm(rows_in, gain_a, shift_a))
    queries = low_back(low(product(act_first, qkv[0]) + biases_qv[0]))
    keys_all = low_back(low(product(act_first, qkv[1])))
    values_all = low_back(low(product(act_first, qkv[2]) + biases_qv[1]))
    head_count = D // HD
    queries = queries.reshape(TOK_DEV, head_count, HD)
    keys_all = keys_all.reshape(TOK_DEV, head_count, HD)
    values_all = values_all.reshape(TOK_DEV, head_count, HD)
    scores = jnp.einsum('lhe,mhe->hlm', queries, keys_all, precision=HIGH) * HD ** (-0.5)
    scores = low_back(scores)
    same_image = image_ids[:, None] == image_ids[None, :]
    scores = jnp.where(same_image[None], scores, -1e+30)
    probs = jax.nn.softmax(scores, axis=-1)
    context = jnp.einsum('hlm,mhe->lhe', low(probs), values_all, precision=HIGH).reshape(TOK_DEV, D)
    context = low_back(low(context))
    branch = low_back(product(context, weight_out) + bias_out)
    resid = rows_in + branch
    act_second = low(layer_norm(resid, gain_b, shift_b))
    preact = low_back(product(act_second, weight_up) + bias_up)
    hidden = low(jax.nn.gelu(preact, approximate=False))
    return resid + low_back(product(hidden, weight_down) + bias_down)

def reference(inputs, image_of_row, gain_first, shift_first, qkv_weight, qv_bias, out_weight, out_bias, gain_second, shift_second, up_weight, up_bias, down_weight, down_bias, cotangent):
    params = tuple((item.astype(jnp.float32) for item in (gain_first, shift_first, qkv_weight, qv_bias, out_weight, out_bias, gain_second, shift_second, up_weight, up_bias, down_weight, down_bias)))
    checked = jax.checkpoint(block_rows)
    image_blocks = image_of_row.reshape(N_DP, TOK_DEV).astype(jnp.int32)

    def forward(rows_all, weights):
        blocks = rows_all.reshape(N_DP, TOK_DEV, D)

        def scan_step(carry, packed):
            return (carry, checked(packed[0], packed[1], weights))
        unused, results = lax.scan(scan_step, jnp.zeros((), jnp.float32), (blocks, image_blocks))
        return results.reshape(TOKENS, D)
    block_out, pullback = jax.vjp(forward, inputs.astype(jnp.float32), params)
    input_grad, grads = pullback(cotangent.astype(jnp.float32))
    grad_gain_first, grad_shift_first, grad_qkv, grad_qv, grad_out, grad_out_bias, grad_gain_second, grad_shift_second, grad_up, grad_up_bias, grad_down, grad_down_bias = grads
    return (block_out, input_grad, grad_gain_first, grad_shift_first, grad_qkv, grad_qv, grad_out, grad_out_bias, grad_gain_second, grad_shift_second, grad_up, grad_up_bias, grad_down, grad_down_bias)
```

```python
import functools

import jax
import jax.numpy as jnp
from jax import lax
from jax.experimental import pallas as pl
from jax.experimental.pallas import tpu as pltpu
from jax.sharding import PartitionSpec as P

f32, bf16, i32 = jnp.float32, jnp.bfloat16, jnp.int32
MESH = pl.DeviceIdType.MESH
NN = (((1,), (0,)), ((), ()))
NT = (((1,), (1,)), ((), ()))
TN = (((0,), (0,)), ((), ()))
HD = 64
P_LO = 196
EPSILON = 1e-06
B = 256
TOP = 832
BIG = 4 * P_LO


def dot(left, right, dims):
    return lax.dot_general(left, right, dims, preferred_element_type=f32)


def rows(start, size=B):
    return pl.ds(pl.multiple_of(start * size, size), size)


def layer_hat(values):
    center = values - jnp.mean(values, axis=1, keepdims=True)
    factor = lax.rsqrt(jnp.mean(center * center, axis=1, keepdims=True) + EPSILON)
    return center * factor, factor


def layer_back(grad_hat, normed, factor):
    first = jnp.mean(grad_hat, axis=1, keepdims=True)
    second = jnp.mean(grad_hat * normed, axis=1, keepdims=True)
    return factor * (grad_hat - first - normed * second)


def column_sum(values):
    return jnp.sum(values, axis=0, keepdims=True)


def remote(src, dst, send, recv, device):
    return pltpu.make_async_remote_copy(
        src_ref=src, dst_ref=dst, send_sem=send, recv_sem=recv, device_id=device, device_id_type=MESH
    )


class Gather:
    def __init__(self, place, view, send, recv):
        self.me, self.core, self.across = place
        self.view, self.send, self.recv = view, send, recv

    def copy(self, slot, k, device):
        return remote(self.view(slot), self.view(slot), self.send(k), self.recv(k), device)

    def start(self):
        self.copy(self.me, 1, self.across).start()
        self.copy(self.me, 0, self.core).start()

    def forward(self):
        slot = self.me ^ 2
        self.copy(slot, 1, self.across).wait_recv()
        self.copy(slot, 2, self.core).start()

    def land_core(self):
        self.copy(self.me ^ 1, 0, self.core).wait_recv()

    def land_far(self):
        self.copy(self.me ^ 3, 2, self.core).wait_recv()

    def close(self):
        for k in range(3):
            self.copy(self.me, k, self.core).wait_send()


class Scatter:
    def __init__(self, place, out, both, far, own, send, recv):
        self.me, self.core, self.across = place
        self.out, self.both, self.far, self.own = out, both, far, own
        self.send, self.recv = send, recv

    def copy(self, k):
        src = self.out.at[k]
        dst = self.far if k == 1 else self.both.at[k // 2]
        return remote(src, dst, self.send.at[k], self.recv.at[k], self.across if k == 1 else self.core)

    def step(self, i, value):
        @pl.when(i == 0)
        def _():
            self.out[0] = value().astype(bf16)
            self.copy(0).start()

        @pl.when(i == 1)
        def _():
            self.copy(0).wait_recv()
            self.out[1] = (value() + self.both[0].astype(f32)).astype(bf16)
            self.copy(1).start()

        @pl.when(i == 2)
        def _():
            self.out[2] = value().astype(bf16)
            self.copy(2).start()

        @pl.when(i == 3)
        def _():
            self.own[...] = value()

    def finish(self):
        self.copy(2).wait_recv()
        self.copy(1).wait_recv()
        total = self.own[...] + self.both[1].astype(f32) + self.far[...].astype(f32)
        for k in range(3):
            self.copy(k).wait_send()
        return total


class Reduce:
    def __init__(self, spot, part, ybuf, zbuf, whole, send, recv):
        self.zi, self.yi, self.ypeer, self.zpeers = spot
        self.part, self.ybuf, self.zbuf, self.whole = part, ybuf, zbuf, whole
        self.send, self.recv = send, recv
        self.quarter = part.shape[1] // 4

    def piece(self, ref, half, quarter):
        return ref.at[half, pl.ds(pl.multiple_of(quarter * self.quarter, 16), self.quarter)]

    def copy_y(self):
        return remote(self.part.at[1 - self.yi], self.ybuf, self.send.at[0], self.recv.at[0], self.ypeer)

    def copy_z(self, j):
        src = self.piece(self.part, self.yi, self.zi ^ j)
        return remote(src, self.zbuf.at[j - 1], self.send.at[j], self.recv.at[j], self.zpeers[j - 1])

    def copy_back(self, j, quarter):
        view = self.piece(self.whole, self.yi, quarter)
        return remote(view, view, self.send.at[3 + j], self.recv.at[3 + j], self.zpeers[j - 1])

    def copy_over(self, j, half):
        view = self.piece(self.whole, half, self.zi ^ j)
        return remote(view, view, self.send.at[7 + j], self.recv.at[7 + j], self.ypeer)

    def one(self):
        self.copy_y().start()

    def two(self):
        self.copy_y().wait_recv()

        def add(q, carry):
            span = pl.ds(pl.multiple_of(q * self.quarter, 16), self.quarter)
            total = self.part[self.yi, span].astype(f32) + self.ybuf[span].astype(f32)
            self.part[self.yi, span] = total.astype(bf16)
            return carry

        lax.fori_loop(0, 4, add, 0)
        for j in (3, 2, 1):
            self.copy_z(j).start()

    def three(self):
        span = pl.ds(pl.multiple_of(self.zi * self.quarter, 16), self.quarter)
        total = self.part[self.yi, span].astype(f32)
        for j in (1, 2, 3):
            self.copy_z(j).wait_recv()
            total = total + self.zbuf[j - 1].astype(f32)
        self.whole[self.yi, span] = total.astype(bf16)
        for j in (3, 2, 1):
            self.copy_back(j, self.zi).start()
        self.copy_over(0, self.yi).start()

    def four(self):
        for j in (1, 2, 3):
            self.copy_back(j, self.zi ^ j).wait_recv()
            self.copy_over(j, self.yi).start()

    def five(self):
        for j in range(4):
            self.copy_over(j, 1 - self.yi).wait_recv()

    def close(self):
        self.copy_y().wait_send()
        for j in (1, 2, 3):
            self.copy_z(j).wait_send()
            self.copy_back(j, self.zi).wait_send()
        for j in range(4):
            self.copy_over(j, self.yi).wait_send()


def layer_kernel(
    x_ref, ids_ref, vec_ref, wqkv_ref, wo_ref, wup_ref, wdn_ref, cot_ref,
    block_ref, input_ref, sums_ref, down_hbm, up_hbm, out_hbm, qkv_hbm,
    xp, stage, a1, keys, values, keys_t, values_t, qz_t, qz, kid, qid, probs, probs_last, rinv, ctx_t, ctx_all,
    wo_all, cot_all, a2, gate, du, do_all, dcz_t, dcz, delta, dq, dk, dv, dkb, dvb, own,
    rs_out, rs_both, rs_far, ms_out, ms_both, ms_far, m_own,
    gd_part, gd_y, gd_z, gd_all, gu_part, gu_y, gu_z, gu_all,
    go_part, go_y, go_z, go_all, gq_part, gq_y, gq_z, gq_all,
    acc, v_mp, v_y, v_z,
    wo_send, wo_recv, cot_send, cot_recv, ctx_send, ctx_recv, do_send, do_recv,
    rs_send, rs_recv, ms_send, ms_recv, rt_send, rt_recv,
    gd_send, gd_recv, gu_send, gu_recv, go_send, go_recv, gq_send, gq_recv,
    v_send, v_recv, local_sem,
):
    dp, me = lax.axis_index("dp"), lax.axis_index("mp")
    core, across, diagonal = (dp, me ^ 1), (dp, me ^ 2), (dp, me ^ 3)
    yi, zi = dp & 1, (dp >> 1) & 3
    ypeer = (dp ^ 1, me)
    zpeers = [(dp ^ (2 * j), me) for j in (1, 2, 3)]
    place = (me, core, across)
    spot = (zi, yi, ypeer, zpeers)
    share = cot_ref.shape[0]

    barrier = pltpu.get_barrier_semaphore()
    partners = [core, across, diagonal, ypeer] + zpeers
    for partner in partners:
        pl.semaphore_signal(barrier, inc=1, device_id=partner, device_id_type=MESH)

    def vec(r, width=None):
        return vec_ref[r : r + 1, :] if width is None else vec_ref[r : r + 1, width[0] : width[1]]

    stage[240:256, :] = jnp.zeros((16, 768), f32)
    stage[0:share, :] = cot_ref[...].astype(f32)
    cot_all[rows(me), :] = stage[0:B, :].astype(bf16)
    wo_all[me] = wo_ref[...]
    acc[...] = jnp.zeros(acc.shape, f32)
    pl.semaphore_wait(barrier, len(partners))

    gather_wo = Gather(place, lambda s: wo_all.at[s], lambda k: wo_send.at[k], lambda k: wo_recv.at[k])
    gather_cot = Gather(place, lambda s: cot_all.at[rows(s)], lambda k: cot_send.at[k], lambda k: cot_recv.at[k])
    gather_wo.start()
    gather_cot.start()

    row_in = lax.broadcasted_iota(i32, (B, 768), 0)
    for s in range(4):
        first = s * share // 16 * 16
        last = min(first + 272, 4 * share)
        stage[0 : last - first, :] = x_ref[first:last, :].astype(f32)
        moved = stage[s * share - first : s * share - first + B, :]
        xp[s * B : (s + 1) * B, :] = jnp.where(row_in < share, moved, 0.0).astype(bf16)

    two_images = (ids_ref[0] == ids_ref[BIG - 1]).astype(i32)

    def image_of(index, shard, pad):
        place_of = index + shard * share
        small = jnp.zeros_like(index)
        for k in range(1, 5):
            small = small + (place_of >= k * P_LO).astype(i32)
        large = (place_of >= BIG).astype(i32)
        image = small * (1 - two_images) + large * two_images
        return jnp.where(index < share, image, pad)

    def images(s, carry):
        kid[rows(s), :] = image_of(lax.broadcasted_iota(i32, (B, B), 0), s, -1)
        qid[s] = image_of(lax.broadcasted_iota(i32, (8, B), 1), s, -2)
        qz_t[s] = jnp.zeros(qz_t.shape[1:], bf16)
        return carry

    lax.fori_loop(0, 4, images, 0)

    lane_head = lax.broadcasted_iota(i32, (B, 192), 1) // HD

    def project(s, carry):
        span = rows(s)
        hat, _ = layer_hat(xp[span, :].astype(f32))
        act = (hat * vec(0) + vec(1)).astype(bf16)
        a1[span, :] = act
        q = (dot(act, wqkv_ref[0], NN) + vec(7, (0, 192))).astype(bf16)
        k = dot(act, wqkv_ref[1], NN).astype(bf16)
        v = (dot(act, wqkv_ref[2], NN) + vec(7, (256, 448))).astype(bf16)
        keys[span, :] = k
        values[span, :] = v
        keys_t[:, span] = k.T
        values_t[:, span] = v.T
        q = q.astype(f32) * HD**-0.5
        qt = q.astype(bf16).T
        for h in range(3):
            qz_t[s, h * HD : (h + 1) * HD, h * B : (h + 1) * B] = qt[h * HD : (h + 1) * HD, :]
            qz[s, h * B : (h + 1) * B, :] = jnp.where(lane_head == h, q, 0.0).astype(bf16)
        return carry

    lax.fori_loop(0, 4, project, 0)

    def gather_ctx(s):
        return Gather(
            place, lambda j: ctx_all.at[j, s], lambda k: ctx_send.at[s, k], lambda k: ctx_recv.at[s, k]
        )

    def attend(s, h, low, high, qlow, qhigh, store):
        lanes = pl.ds(pl.multiple_of(h * B + qlow, 128), qhigh - qlow)
        scores = dot(keys[low:high, :], qz_t[s, :, lanes], NN)
        same = kid[low:high, qlow:qhigh] == qid[s, 0:1, qlow:qhigh]
        scores = jnp.where(same, scores, -1e30)
        top = jnp.max(scores, axis=0, keepdims=True)
        weights = jnp.exp(scores - top)
        inverse = 1.0 / jnp.sum(weights, axis=0, keepdims=True)
        weights = weights.astype(bf16)
        store(lanes, weights)
        rinv[s, h, 0:1, qlow:qhigh] = inverse
        head = pl.ds(pl.multiple_of(h * HD, HD), HD)
        return (dot(values_t[head, low:high], weights, NN) * inverse).astype(bf16)

    def send_ctx(s):
        span = rows(s)
        block = ctx_t[:, span]
        ctx_all[me, s, 0:B, :] = block[0:128, :].T
        last = jnp.concatenate([block[128:192, 0:128], block[128:192, 128:256]], axis=0)
        ctx_all[me, s, B : B + 128, :] = last.T
        gather_ctx(s).start()

    def attend_top(s, carry):
        def head(h, inner):
            def store(lanes, weights):
                probs[s, :, lanes] = weights

            here = pl.ds(pl.multiple_of(h * HD, HD), HD)
            ctx_t[here, rows(s)] = attend(s, h, 0, TOP, 0, B, store)
            return inner

        lax.fori_loop(0, 3, head, 0)
        send_ctx(s)

        @pl.when(s == 1)
        def _():
            gather_wo.forward()

        @pl.when(s == 2)
        def _():
            gather_cot.forward()

        return carry

    lax.fori_loop(0, 3, attend_top, 0)

    def attend_last(h, carry):
        here = pl.ds(pl.multiple_of(h * HD, HD), HD)

        def store_left(lanes, weights):
            probs_last[:, lanes] = weights

        def store_right(lanes, weights):
            probs_last[0:768, lanes] = jnp.zeros((768, 128), bf16)
            probs_last[768:1024, lanes] = weights

        ctx_t[here, 768:896] = attend(3, h, 0, 1024, 0, 128, store_left)
        ctx_t[here, 896:1024] = attend(3, h, 768, 1024, 128, 256, store_right)
        return carry

    lax.fori_loop(0, 3, attend_last, 0)
    send_ctx(3)

    gather_wo.land_core()
    gather_wo.land_far()
    gather_cot.land_core()
    gather_cot.land_far()
    for s in range(4):
        gather_ctx(s).forward()

    sum_in = Scatter(place, rs_out, rs_both, rs_far, own, rs_send, rs_recv)
    zeros_w = jnp.zeros((HD, 768), bf16)

    def middle(i, carry):
        s = me ^ (3 - i)
        span = rows(s)
        ctx = gather_ctx(s)
        ctx.land_core()
        ctx.land_far()
        left = jnp.concatenate([ctx_all[j, s, 0:B, :] for j in range(4)], axis=1)
        last = jnp.concatenate([ctx_all[j, s, B : B + 128, :] for j in range(4)], axis=1)
        w_left = jnp.concatenate([wo_all[j, 0:128, :] for j in range(4)], axis=0)
        w_tail = [wo_all[j, 128:192, :] for j in range(4)]
        w_upper = jnp.concatenate([piece for w in w_tail for piece in (w, zeros_w)], axis=0)
        w_lower = jnp.concatenate([piece for w in w_tail for piece in (zeros_w, w)], axis=0)
        branch = dot(left, w_left, NN) + jnp.concatenate(
            [dot(last, w_upper, NN), dot(last, w_lower, NN)], axis=0
        )
        h = xp[span, :].astype(f32) + (branch + vec(2))

        @pl.when(i == 3)
        def _():
            block_ref[...] = h

        hat, _ = layer_hat(h)
        stage[0:B, :] = hat
        act = (hat * vec(3) + vec(4)).astype(bf16)
        a2[span, :] = act
        u = dot(act, wup_ref[...], NN) + vec(5)
        cdf = 0.5 * (1.0 + lax.erf(u * 0.7071067811865476))
        gate[span, :] = (u * cdf).astype(bf16)
        slope = cdf + u * (0.3989422804014327 * jnp.exp(-0.5 * (u * u)))
        grad_u = (dot(cot_all[span, :], wdn_ref[...], NT) * slope).astype(bf16)
        du[span, :] = grad_u
        acc[8:9, :] += column_sum(grad_u.astype(f32))
        grad_act = dot(grad_u, wup_ref[...], NT)
        acc[2:3, :] += column_sum(grad_act * stage[0:B, :])
        acc[3:4, :] += column_sum(grad_act)
        own[...] = grad_act
        sum_in.step(i, lambda: own[...])
        return carry

    lax.fori_loop(0, 4, middle, 0)

    def grad_tiles(part, left, right, width):
        def tile(i, carry):
            piece = dot(left[:, rows(i, width)], right[...], TN).astype(bf16)
            part[0, rows(i, width), :] = piece[:, 0:384]
            part[1, rows(i, width), :] = piece[:, 384:768]
            return carry

        lax.fori_loop(0, 768 // width, tile, 0)

    reduce_down = Reduce(spot, gd_part, gd_y, gd_z, gd_all, gd_send, gd_recv)
    reduce_up = Reduce(spot, gu_part, gu_y, gu_z, gu_all, gu_send, gu_recv)
    reduce_out = Reduce(spot, go_part, go_y, go_z, go_all, go_send, go_recv)
    reduce_qkv = Reduce(spot, gq_part, gq_y, gq_z, gq_all, gq_send, gq_recv)

    grad_tiles(gd_part, gate, cot_all, B)
    reduce_down.one()
    grad_tiles(gu_part, a2, du, B)
    reduce_up.one()

    grad_act = sum_in.finish()
    hat, factor = layer_hat(block_ref[...])
    cot_own = cot_all[rows(me), :].astype(f32)
    grad_h = cot_own + layer_back(grad_act * vec(3), hat, factor)
    input_ref[...] = grad_h
    grad_branch = grad_h.astype(bf16)
    do_all[rows(me), :] = grad_branch
    gather_do = Gather(place, lambda s: do_all.at[rows(s)], lambda k: do_send.at[k], lambda k: do_recv.at[k])
    gather_do.start()
    acc[4:5, :] = column_sum(grad_branch.astype(f32))
    acc[5:6, :] = column_sum(cot_own)

    sum_out = Scatter(place, ms_out, ms_both, ms_far, m_own, ms_send, ms_recv)

    def project_down(i, carry):
        s = me ^ (3 - i)
        m_own[...] = dot(gate[rows(s), :], wdn_ref[...], NN)
        sum_out.step(i, lambda: m_own[...])
        return carry

    lax.fori_loop(0, 4, project_down, 0)
    reduce_down.two()

    dk[...] = jnp.zeros(dk.shape, f32)
    dv[...] = jnp.zeros(dv.shape, f32)

    def back_head(s, h, low, high, qlow, qhigh, ref):
        lanes = pl.ds(pl.multiple_of(h * B + qlow, 128), qhigh - qlow)
        head = pl.ds(pl.multiple_of(h * HD, HD), HD)
        weights = ref[low:high, lanes]
        grad_probs = dot(values[low:high, :], dcz_t[:, lanes], NN)
        grad_scores = weights.astype(f32) * (grad_probs - delta[h, 0:1, qlow:qhigh])
        grad_scores = grad_scores.astype(bf16)
        ref[low:high, lanes] = grad_scores
        return dot(keys_t[head, low:high], grad_scores, NN)

    def back_block(i, carry):
        s = me ^ i
        span = rows(s)

        @pl.when(i == 1)
        def _():
            gather_do.land_core()

        @pl.when(i == 2)
        def _():
            gather_do.forward()
            reduce_up.two()

        @pl.when(i == 3)
        def _():
            gather_do.land_far()
            reduce_down.three()

        grad_ctx = dot(wo_ref[...], do_all[span, :], NT).astype(bf16).astype(f32)
        for h in range(3):
            here = slice(h * HD, (h + 1) * HD)
            scaled = (grad_ctx[here, :] * rinv[s, h, 0:1, :]).astype(bf16)
            delta[h, 0:1, :] = column_sum(scaled.astype(f32) * ctx_t[here, span].astype(f32))
            dcz_t[here, h * B : (h + 1) * B] = scaled
            turned = jnp.concatenate([scaled, jnp.zeros((HD, B), bf16)], axis=0).T.astype(f32)
            wide = jnp.concatenate([turned, turned], axis=1)[:, 0:192]
            if h == 1:
                wide = pltpu.roll(jnp.concatenate([turned, jnp.zeros((B, 128), f32)], axis=1), HD, 1)[:, 0:192]
            dcz[h * B : (h + 1) * B, :] = jnp.where(lane_head == h, wide, 0.0).astype(bf16)

        @pl.when(s != 3)
        def _():
            dv[0:TOP, :] += dot(probs[s], dcz[...], NN)
            ref = probs.at[s]

            def head(h, inner):
                grad = back_head(s, h, 0, TOP, 0, B, ref)
                stage[pl.ds(pl.multiple_of(h * HD, HD), HD), 0:B] = grad
                return inner

            lax.fori_loop(0, 3, head, 0)
            dk[0:TOP, :] += dot(probs[s], qz[s], NN)

        @pl.when(s == 3)
        def _():
            dv[...] += dot(probs_last[...], dcz[...], NN)

            def head(h, inner):
                here = pl.ds(pl.multiple_of(h * HD, HD), HD)
                stage[here, 0:128] = back_head(s, h, 0, 1024, 0, 128, probs_last)
                stage[here, 128:256] = back_head(s, h, 768, 1024, 128, 256, probs_last)
                return inner

            lax.fori_loop(0, 3, head, 0)
            dk[...] += dot(probs_last[...], qz[s], NN)

        dq[span, :] = (stage[0:192, 0:B] * HD**-0.5).T.astype(bf16)
        return carry

    dcz_t[...] = jnp.zeros(dcz_t.shape, bf16)
    lax.fori_loop(0, 4, back_block, 0)

    grad_out = dot(ctx_t[...], do_all[...], NN).astype(bf16)
    go_part[0] = grad_out[:, 0:384]
    go_part[1] = grad_out[:, 384:768]
    reduce_out.one()
    reduce_up.three()

    dkb[...] = dk[...].astype(bf16)
    dvb[...] = dv[...].astype(bf16)
    for t, ref in enumerate((dq, dkb, dvb)):
        piece = dot(ref[...], a1[...], TN).astype(bf16)
        gq_part[0, t * 192 : (t + 1) * 192, :] = piece[:, 0:384]
        gq_part[1, t * 192 : (t + 1) * 192, :] = piece[:, 384:768]
    reduce_qkv.one()
    acc[9:10, 0:192] = column_sum(dq[...].astype(f32))
    acc[9:10, 256:448] = column_sum(dvb[...].astype(f32))

    sum_first = Scatter(place, rs_out, rs_both, rs_far, own, rt_send, rt_recv)

    def project_back(i, carry):
        s = me ^ (3 - i)
        span = rows(s)
        grad = dot(dq[span, :], wqkv_ref[0], NT)
        grad = grad + dot(dkb[span, :], wqkv_ref[1], NT)
        grad = grad + dot(dvb[span, :], wqkv_ref[2], NT)
        hat, _ = layer_hat(xp[span, :].astype(f32))
        acc[0:1, :] += column_sum(grad * hat)
        acc[1:2, :] += column_sum(grad)
        own[...] = grad
        sum_first.step(i, lambda: own[...])
        return carry

    lax.fori_loop(0, 4, project_back, 0)

    v_mp[me] = acc[...]
    v_copies = [remote(v_mp.at[me], v_mp.at[me], v_send.at[j - 1], v_recv.at[j - 1], (dp, me ^ j)) for j in (1, 2, 3)]
    v_lands = [remote(v_mp.at[me ^ j], v_mp.at[me ^ j], v_send.at[j - 1], v_recv.at[j - 1], (dp, me ^ j)) for j in (1, 2, 3)]
    for copy in v_copies:
        copy.start()
    reduce_out.two()
    reduce_qkv.two()
    for copy in v_lands:
        copy.wait_recv()
    acc[0:8, :] = v_mp[0, 0:8, :] + v_mp[1, 0:8, :] + v_mp[2, 0:8, :] + v_mp[3, 0:8, :]
    vy_copy = remote(acc, v_y, v_send.at[3], v_recv.at[3], ypeer)
    vy_copy.start()
    reduce_down.four()
    reduce_up.four()
    reduce_out.three()
    vy_copy.wait_recv()
    v_z[zi] = acc[...] + v_y[...]
    vz_copies = [remote(v_z.at[zi], v_z.at[zi], v_send.at[3 + j], v_recv.at[3 + j], zpeers[j - 1]) for j in (1, 2, 3)]
    vz_lands = [remote(v_z.at[zi ^ j], v_z.at[zi ^ j], v_send.at[3 + j], v_recv.at[3 + j], zpeers[j - 1]) for j in (1, 2, 3)]
    for copy in vz_copies:
        copy.start()
    reduce_qkv.three()

    block_ref[...] = block_ref[...] + (sum_out.finish() + vec(6))
    reduce_down.five()
    save_down = pltpu.make_async_copy(gd_all, down_hbm, local_sem.at[0])
    save_down.start()
    reduce_up.five()
    save_up = pltpu.make_async_copy(gu_all, up_hbm, local_sem.at[1])
    save_up.start()
    reduce_out.four()
    for copy in vz_lands:
        copy.wait_recv()
    sums_ref[...] = v_z[0] + v_z[1] + v_z[2] + v_z[3]

    grad_act = sum_first.finish()
    hat, factor = layer_hat(xp[rows(me), :].astype(f32))
    input_ref[...] = input_ref[...] + layer_back(grad_act * vec(0), hat, factor)

    reduce_out.five()
    save_out = pltpu.make_async_copy(go_all, out_hbm, local_sem.at[2])
    save_out.start()
    reduce_qkv.four()
    reduce_qkv.five()
    save_qkv = pltpu.make_async_copy(gq_all, qkv_hbm, local_sem.at[3])
    save_qkv.start()

    for copy in v_copies + [vy_copy] + vz_copies:
        copy.wait_send()
    for gather in [gather_wo, gather_cot, gather_do] + [gather_ctx(s) for s in range(4)]:
        gather.close()
    for reduce in (reduce_down, reduce_up, reduce_out, reduce_qkv):
        reduce.close()
    for save in (save_down, save_up, save_out, save_qkv):
        save.wait()


def finish_kernel(
    block_ref, input_ref, sums_ref, down_ref, up_ref, out_ref, qkv_ref,
    block_out, input_grad, gain_first, shift_first, grad_qkv, grad_qv, grad_out, out_bias, gain_second, shift_second,
    grad_up, up_bias, grad_down, down_bias,
):
    share = block_out.shape[0]
    block_out[...] = block_ref[0:share, :]
    input_grad[...] = input_ref[0:share, :]
    for r, ref in enumerate((gain_first, shift_first, gain_second, shift_second, out_bias, down_bias)):
        ref[...] = sums_ref[r, :]
    up_bias[...] = sums_ref[8, :]
    grad_qv[0:1, :] = sums_ref[9:10, 0:192]
    grad_qv[1:2, :] = sums_ref[9:10, 256:448]
    for source, target in ((down_ref, grad_down), (up_ref, grad_up), (out_ref, grad_out)):
        for half in range(2):
            target[:, half * 384 : (half + 1) * 384] = source[half].astype(f32)
    for t in range(3):
        for half in range(2):
            turned = qkv_ref[half, t * 192 : (t + 1) * 192, :].astype(f32).T
            grad_qkv[t, half * 384 : (half + 1) * 384, :] = turned


def per_device(
    inputs, image_of_row, gain_first, shift_first, qkv_weight, qv_bias, out_weight, out_bias, gain_second,
    shift_second, up_weight, up_bias, down_weight, down_bias, cotangent,
):
    qv_row = jnp.concatenate([jnp.pad(qv_bias[0], (0, 64)), jnp.pad(qv_bias[1], (0, 320))])
    packed = jnp.stack(
        [gain_first, shift_first, out_bias, gain_second, shift_second, up_bias, down_bias, qv_row]
    ).astype(f32)
    share = cotangent.shape[0]
    vmem, smem, anyspace = (pl.BlockSpec(memory_space=m) for m in (pltpu.VMEM, pltpu.SMEM, pl.ANY))

    def shape(*dims, dtype=bf16):
        return pltpu.VMEM(dims, dtype)

    def job(n):
        return [shape(2, n, 384), shape(n, 384), shape(3, n // 4, 384), shape(2, n, 384)]

    scratch = [
        shape(1024, 768), shape(272, 768, dtype=f32), shape(1024, 768),
        shape(1024, 192), shape(1024, 192), shape(192, 1024), shape(192, 1024),
        shape(4, 192, 768), shape(4, 768, 192),
        shape(1024, B, dtype=i32), shape(4, 8, B, dtype=i32),
        shape(3, TOP, 768), shape(1024, 768), shape(4, 3, 8, B, dtype=f32),
        shape(192, 1024), shape(4, 4, 384, 128), shape(4, 192, 768), shape(1024, 768),
        shape(1024, 768), shape(1024, 768), shape(1024, 768), shape(1024, 768),
        shape(192, 768), shape(768, 192), shape(3, 8, B, dtype=f32),
        shape(1024, 192), shape(1024, 192, dtype=f32), shape(1024, 192, dtype=f32),
        shape(1024, 192), shape(1024, 192), shape(B, 768, dtype=f32),
        shape(3, B, 768), shape(2, B, 768), shape(B, 768),
        shape(3, B, 768), shape(2, B, 768), shape(B, 768), shape(B, 768, dtype=f32),
        *job(768), *job(768), *job(192), *job(576),
        shape(16, 768, dtype=f32), shape(4, 16, 768, dtype=f32), shape(16, 768, dtype=f32), shape(4, 16, 768, dtype=f32),
    ]
    dma = pltpu.SemaphoreType.DMA
    scratch += [dma((3,))] * 4 + [dma((4, 3))] * 2 + [dma((3,))] * 8 + [dma((11,))] * 8 + [dma((7,))] * 2 + [dma((4,))]
    results = pl.pallas_call(
        layer_kernel,
        out_shape=[
            jax.ShapeDtypeStruct((B, 768), f32),
            jax.ShapeDtypeStruct((B, 768), f32),
            jax.ShapeDtypeStruct((16, 768), f32),
            jax.ShapeDtypeStruct((2, 768, 384), bf16),
            jax.ShapeDtypeStruct((2, 768, 384), bf16),
            jax.ShapeDtypeStruct((2, 192, 384), bf16),
            jax.ShapeDtypeStruct((2, 576, 384), bf16),
        ],
        in_specs=[vmem, smem] + [vmem] * 6,
        out_specs=[vmem] * 3 + [anyspace] * 4,
        scratch_shapes=scratch,
        compiler_params=pltpu.CompilerParams(
            collective_id=0, has_side_effects=True, vmem_limit_bytes=60 * 2**20
        ),
        name="layer",
    )(inputs, image_of_row, packed, qkv_weight, out_weight, up_weight, down_weight, cotangent)

    def out(*dims):
        return jax.ShapeDtypeStruct(dims, f32)

    return tuple(
        pl.pallas_call(
            finish_kernel,
            out_shape=[
                out(share, 768), out(share, 768), out(768), out(768), out(3, 768, 192), out(2, 192), out(192, 768),
                out(768), out(768), out(768), out(768, 768), out(768), out(768, 768), out(768),
            ],
            in_specs=[vmem] * 7,
            out_specs=[vmem] * 14,
            compiler_params=pltpu.CompilerParams(vmem_limit_bytes=32 * 2**20),
            name="finish",
        )(*results)
    )


def solution(mesh):
    return jax.shard_map(
        per_device,
        mesh=mesh,
        in_specs=(
            P("dp", None),
            P("dp"),
            P(),
            P(),
            P(None, None, "mp"),
            P(None, "mp"),
            P("mp", None),
            P(),
            P(),
            P(),
            P(None, "mp"),
            P("mp"),
            P("mp", None),
            P(),
            P(("dp", "mp"), None),
        ),
        out_specs=(
            P(("dp", "mp"), None),
            P(("dp", "mp"), None),
            P(),
            P(),
            P(None, None, "mp"),
            P(None, "mp"),
            P("mp", None),
            P(),
            P(),
            P(),
            P(None, "mp"),
            P("mp"),
            P("mp", None),
            P(),
        ),
        check_vma=False,
    )
```

```python
import functools

import jax
import jax.numpy as jnp
from jax import lax
from jax.experimental import pallas as pl
from jax.experimental.pallas import tpu as pltpu
from jax.sharding import PartitionSpec as P

f32, bf16, i32 = jnp.float32, jnp.bfloat16, jnp.int32
MESH = pl.DeviceIdType.MESH
NN = (((1,), (0,)), ((), ()))
NT = (((1,), (1,)), ((), ()))
TN = (((0,), (0,)), ((), ()))
HD = 64
P_LO = 196
EPSILON = 1e-06
B = 256
TOP = 832
BIG = 4 * P_LO


def dot(left, right, dims):
    return lax.dot_general(left, right, dims, preferred_element_type=f32)


def rows(start, size=B):
    return pl.ds(pl.multiple_of(start * size, size), size)


def layer_hat(values):
    center = values - jnp.mean(values, axis=1, keepdims=True)
    factor = lax.rsqrt(jnp.mean(center * center, axis=1, keepdims=True) + EPSILON)
    return center * factor, factor


def layer_back(grad_hat, normed, factor):
    first = jnp.mean(grad_hat, axis=1, keepdims=True)
    second = jnp.mean(grad_hat * normed, axis=1, keepdims=True)
    return factor * (grad_hat - first - normed * second)


def column_sum(values):
    return jnp.sum(values, axis=0, keepdims=True)


def remote(src, dst, send, recv, device):
    return pltpu.make_async_remote_copy(
        src_ref=src, dst_ref=dst, send_sem=send, recv_sem=recv, device_id=device, device_id_type=MESH
    )


class Gather:
    def __init__(self, place, view, send, recv):
        self.me, self.core, self.across = place
        self.view, self.send, self.recv = view, send, recv

    def copy(self, slot, k, device):
        return remote(self.view(slot), self.view(slot), self.send(k), self.recv(k), device)

    def start(self):
        self.copy(self.me, 1, self.across).start()
        self.copy(self.me, 0, self.core).start()

    def forward(self):
        slot = self.me ^ 2
        self.copy(slot, 1, self.across).wait_recv()
        self.copy(slot, 2, self.core).start()

    def land_core(self):
        self.copy(self.me ^ 1, 0, self.core).wait_recv()

    def land_far(self):
        self.copy(self.me ^ 3, 2, self.core).wait_recv()

    def close(self):
        for k in range(3):
            self.copy(self.me, k, self.core).wait_send()


class Scatter:
    def __init__(self, place, out, both, far, own, send, recv):
        self.me, self.core, self.across = place
        self.out, self.both, self.far, self.own = out, both, far, own
        self.send, self.recv = send, recv

    def copy(self, k):
        src = self.out.at[k]
        dst = self.far if k == 1 else self.both.at[k // 2]
        return remote(src, dst, self.send.at[k], self.recv.at[k], self.across if k == 1 else self.core)

    def step(self, i, value):
        @pl.when(i == 0)
        def _():
            self.out[0] = value().astype(bf16)
            self.copy(0).start()

        @pl.when(i == 1)
        def _():
            self.copy(0).wait_recv()
            self.out[1] = (value() + self.both[0].astype(f32)).astype(bf16)
            self.copy(1).start()

        @pl.when(i == 2)
        def _():
            self.out[2] = value().astype(bf16)
            self.copy(2).start()

        @pl.when(i == 3)
        def _():
            self.own[...] = value()

    def finish(self):
        self.copy(2).wait_recv()
        self.copy(1).wait_recv()
        total = self.own[...] + self.both[1].astype(f32) + self.far[...].astype(f32)
        for k in range(3):
            self.copy(k).wait_send()
        return total


class Reduce:
    def __init__(self, spot, first_y, refs):
        self.zi, self.yi, self.over, self.above, self.below = spot
        self.first_y = first_y
        self.part, self.ybuf, self.up, self.down, self.whole, self.send, self.recv = refs
        self.sent = []

    def copy(self, src, dst, k, device):
        return remote(src, dst, self.send.at[k], self.recv.at[k], device)

    def begin(self, condition, make):
        self.sent.append((condition, make))
        if condition is None:
            make().start()
        else:
            pl.when(condition())(lambda: make().start())

    def close(self):
        for condition, make in self.sent:
            if condition is None:
                make().wait_send()
            else:
                pl.when(condition())(lambda make=make: make().wait_send())

    def chunks(self, first, count):
        return self.part.at[self.yi if self.first_y else slice(None), pl.ds(first, count)]

    def rising(self, first, count):
        span = pl.ds(first - 1, count)
        return self.up.at[span] if self.first_y else self.up.at[:, span]

    def falling(self, first, count):
        span = pl.ds(first, count)
        return self.down.at[span] if self.first_y else self.down.at[:, span]

    def result(self, chunk):
        return self.whole.at[self.yi if self.first_y else slice(None), chunk]

    def copy_up(self, first, count, src):
        return self.copy(src, self.rising(first, count), 1, self.above)

    def copy_down(self, first, count, src):
        return self.copy(src, self.falling(first, count), 2, self.below)

    def at(self, z):
        return lambda: self.zi == z

    def hop(self, n):
        up_first, down_count = n, 4 - n

        def up_view():
            return self.chunks(n, 4 - n) if n == 1 else self.rising(n, 4 - n)

        def down_view():
            return self.chunks(0, 4 - n) if n == 1 else self.falling(0, 4 - n)

        if n > 1:

            @pl.when(self.zi == n - 1)
            def _():
                came = self.rising(n - 1, 5 - n)
                self.copy_up(n - 1, 5 - n, came).wait_recv()
                view, own = self.rising(n, 4 - n), self.chunks(n, 4 - n)
                view[...] = (view[...].astype(f32) + own[...].astype(f32)).astype(bf16)

            @pl.when(self.zi == 4 - n)
            def _():
                came = self.falling(0, 5 - n)
                self.copy_down(0, 5 - n, came).wait_recv()
                view, own = self.falling(0, 4 - n), self.chunks(0, 4 - n)
                view[...] = (view[...].astype(f32) + own[...].astype(f32)).astype(bf16)

        self.begin(self.at(n - 1), lambda: self.copy_up(up_first, 4 - n, up_view()))
        self.begin(self.at(4 - n), lambda: self.copy_down(0, down_count, down_view()))

    def total(self, store):
        def plain(view):
            return view[...].astype(f32)

        @pl.when(self.zi == 0)
        def _():
            self.copy_down(0, 1, self.falling(0, 1)).wait_recv()
            store(0, plain(self.chunks(0, 1)) + plain(self.falling(0, 1)))

        @pl.when(self.zi == 3)
        def _():
            self.copy_up(3, 1, self.rising(3, 1)).wait_recv()
            store(3, plain(self.chunks(3, 1)) + plain(self.rising(3, 1)))

        for z in (1, 2):

            @pl.when(self.zi == z)
            def _(z=z):
                value = plain(self.chunks(z, 1)) + plain(self.rising(z, 1)) + plain(self.falling(z, 1))
                store(z, value)

    def back(self, d):
        for sign, base, ahead, room in ((-1, 3, self.above, lambda: self.zi < 3), (1, 6, self.below, lambda: self.zi > 0)):

            def here(sign=sign):
                return self.zi >= d if sign < 0 else self.zi <= 3 - d

            def view(sign=sign):
                return self.result(self.zi + sign * d)

            if d > 0:

                @pl.when(here())
                def _():
                    self.copy(view(), view(), base + d - 1, ahead).wait_recv()

            if d < 3:
                self.begin(
                    lambda room=room, here=here: room() & here(),
                    lambda view=view, base=base, ahead=ahead: self.copy(view(), view(), base + d, ahead),
                )
            if self.first_y and (d > 0 or sign < 0):
                self.begin(
                    here, lambda view=view, sign=sign: self.copy_over(self.yi, self.zi + sign * d)
                )

    def copy_over(self, half, chunk):
        view = self.whole.at[half, chunk]
        return self.copy(view, view, 9 + (chunk if self.first_y else 0), self.over)

    def sum_over(self):
        if self.first_y:
            return self.copy(self.part.at[1 - self.yi], self.ybuf, 0, self.over)
        return self.copy(self.part.at[1 - self.yi, self.zi], self.ybuf, 0, self.over)

    def stage(self, k):
        if self.first_y:
            if k == 0:
                self.begin(None, self.sum_over)
            elif k == 1:
                self.sum_over().wait_recv()

                def add(c, carry):
                    value = self.part[self.yi, c].astype(f32) + self.ybuf[c].astype(f32)
                    self.part[self.yi, c] = value.astype(bf16)
                    return carry

                lax.fori_loop(0, 4, add, 0)
                self.hop(1)
            elif k in (2, 3):
                self.hop(k)
            elif k == 4:

                def store(z, value):
                    self.whole[self.yi, z] = value[0].astype(bf16)

                self.total(store)
                self.back(0)
            elif k in (5, 6, 7):
                self.back(k - 4)
            else:
                for c in range(4):
                    self.copy_over(1 - self.yi, c).wait_recv()
        else:
            if k in (0, 1, 2):
                self.hop(k + 1)
            elif k == 3:

                def store(z, value):
                    self.part[:, z] = value[:, 0].astype(bf16)

                self.total(store)
                self.begin(None, self.sum_over)
            elif k == 4:
                self.sum_over().wait_recv()
                value = self.part[self.yi, self.zi].astype(f32) + self.ybuf[...].astype(f32)
                self.whole[self.yi, self.zi] = value.astype(bf16)
                self.begin(None, lambda: self.copy_over(self.yi, self.zi))
            elif k == 5:
                self.copy_over(1 - self.yi, self.zi).wait_recv()
                self.back(0)
            else:
                self.back(k - 5)


FIRST_Y = (False, True, True, True, True, False, True, True, True, True)
QUARTER = (64,) * 6 + (48,) * 4
STAGES = 9

POLLS = {
    "down1": ((0, 0),),
    "down2": ((1, 0),),
    "up0": ((2, 0),),
    "up1": ((3, 0),),
    "up2": ((4, 0),),
    "own": ((5, 0),),
    "mlp2": ((1, 1),),
    "mlp3": ((0, 1),),
    "attend1": ((2, 1),),
    "attend4": ((0, 2), (5, 1),),
    "attend5": ((3, 1),),
    "attend6": ((1, 2),),
    "attend7": ((0, 3),),
    "attend8": ((4, 1),),
    "attend9": ((2, 2), (5, 2), (0, 4),),
    "attend10": ((1, 3),),
    "attend11": ((3, 2),),
    "out": ((0, 5),),
    "qkv0": ((2, 3), (5, 3), (6, 0),),
    "qkv1": ((1, 4), (4, 2), (7, 0),),
    "qkv2": ((8, 0),),
    "first0": ((5, 4), (3, 3), (9, 0),),
    "first2": ((0, 6), (2, 4),),
    "first3": ((1, 5), (6, 1), (3, 4),),
    "sums1": ((4, 3),),
    "sums2": ((0, 7), (2, 5), (6, 2), (7, 1),),
    "tail": ((1, 6), (3, 5), (5, 5), (4, 4), (0, 8), (6, 3), (7, 2), (8, 1), (2, 6), (1, 7), (9, 1), (3, 6), (5, 6), (4, 5), (8, 2), (7, 3), (6, 4), (2, 7), (9, 2), (3, 7), (5, 7), (8, 3), (1, 8), (4, 6), (7, 4), (6, 5), (9, 3), (2, 8), (5, 8), (3, 8), (8, 4), (4, 7), (7, 5), (6, 6), (9, 4), (8, 5), (4, 8), (7, 6), (6, 7), (9, 5), (8, 6), (7, 7), (9, 6), (6, 8), (8, 7), (9, 7), (7, 8), (8, 8), (9, 8),),
}


def layer_kernel(
    x_ref, ids_ref, gain_a, shift_a, bias_qv, bias_out, gain_b, shift_b, bias_up, bias_down,
    wqkv_ref, wo_ref, wup_ref, wdn_ref, cot_ref,
    block_ref, input_ref, sums_ref, down_hbm, up_hbm, out_hbm, qkv_hbm,
    xp, stage, a1, keys, values, keys_t, values_t, qz_t, qz, kid, qid, probs, probs_last, rinv, ctx_t, ctx_all,
    wo_all, cot_all, a2, gate, du, do_all, dcz_t, dcz, delta, dq, dk, dv, dkb, dvb, own,
    rs_out, rs_both, rs_far, ms_out, ms_both, ms_far, m_own,
    vec_ref, acc, v_mp, v_y, v_z,
    wo_send, wo_recv, cot_send, cot_recv, ctx_send, ctx_recv, do_send, do_recv,
    rs_send, rs_recv, ms_send, ms_recv, rt_send, rt_recv,
    v_send, v_recv, local_sem, block_refs,
):
    dp, me = lax.axis_index("dp"), lax.axis_index("mp")
    core, across, diagonal = (dp, me ^ 1), (dp, me ^ 2), (dp, me ^ 3)
    yi, zi = dp & 1, (dp >> 1) & 3
    ypeer = (dp ^ 1, me)
    zpeers = [(dp ^ (2 * j), me) for j in (1, 2, 3)]
    place = (me, core, across)
    base = dp & ~7
    above, below = (base + (((zi + 1) & 3) << 1) + yi, me), (base + (((zi + 3) & 3) << 1) + yi, me)
    spot = (zi, yi, ypeer, above, below)
    share = cot_ref.shape[0]

    barrier = pltpu.get_barrier_semaphore()
    partners = [core, across, diagonal, ypeer] + zpeers
    for partner in partners:
        pl.semaphore_signal(barrier, inc=1, device_id=partner, device_id_type=MESH)

    def vec(r, width=None):
        return vec_ref[r : r + 1, :] if width is None else vec_ref[r : r + 1, width[0] : width[1]]

    for r, ref in enumerate((gain_a, shift_a, bias_out, gain_b, shift_b, bias_up, bias_down)):
        vec_ref[r : r + 1, :] = ref[...].astype(f32).reshape(1, 768)
    vec_ref[7:8, 0:192] = bias_qv[0:1, :].astype(f32)
    vec_ref[7:8, 256:448] = bias_qv[1:2, :].astype(f32)

    stage[240:256, :] = jnp.zeros((16, 768), f32)
    stage[0:share, :] = cot_ref[...].astype(f32)
    cot_all[rows(me), :] = stage[0:B, :].astype(bf16)
    wo_all[me] = wo_ref[...]
    acc[...] = jnp.zeros(acc.shape, f32)
    pl.semaphore_wait(barrier, len(partners))

    gather_wo = Gather(place, lambda s: wo_all.at[s], lambda k: wo_send.at[k], lambda k: wo_recv.at[k])
    gather_cot = Gather(place, lambda s: cot_all.at[rows(s)], lambda k: cot_send.at[k], lambda k: cot_recv.at[k])
    gather_wo.start()
    gather_cot.start()

    row_in = lax.broadcasted_iota(i32, (B, 768), 0)
    for s in range(4):
        first = s * share // 16 * 16
        last = min(first + 272, 4 * share)
        stage[0 : last - first, :] = x_ref[first:last, :].astype(f32)
        moved = stage[s * share - first : s * share - first + B, :]
        xp[s * B : (s + 1) * B, :] = jnp.where(row_in < share, moved, 0.0).astype(bf16)

    two_images = (ids_ref[0] == ids_ref[BIG - 1]).astype(i32)

    def image_of(index, shard, pad):
        place_of = index + shard * share
        small = jnp.zeros_like(index)
        for k in range(1, 5):
            small = small + (place_of >= k * P_LO).astype(i32)
        large = (place_of >= BIG).astype(i32)
        image = small * (1 - two_images) + large * two_images
        return jnp.where(index < share, image, pad)

    def images(s, carry):
        kid[rows(s), :] = image_of(lax.broadcasted_iota(i32, (B, B), 0), s, -1)
        qid[s] = image_of(lax.broadcasted_iota(i32, (8, B), 1), s, -2)
        qz_t[s] = jnp.zeros(qz_t.shape[1:], bf16)
        return carry

    lax.fori_loop(0, 4, images, 0)

    lane_head = lax.broadcasted_iota(i32, (B, 192), 1) // HD

    def project(s, carry):
        span = rows(s)
        hat, _ = layer_hat(xp[span, :].astype(f32))
        act = (hat * vec(0) + vec(1)).astype(bf16)
        a1[span, :] = act
        q = (dot(act, wqkv_ref[0], NT) + vec(7, (0, 192))).astype(bf16)
        k = dot(act, wqkv_ref[1], NT).astype(bf16)
        v = (dot(act, wqkv_ref[2], NT) + vec(7, (256, 448))).astype(bf16)
        keys[span, :] = k
        values[span, :] = v
        keys_t[:, span] = k.T
        values_t[:, span] = v.T
        q = q.astype(f32) * HD**-0.5
        qt = q.astype(bf16).T
        for h in range(3):
            qz_t[s, h * HD : (h + 1) * HD, h * B : (h + 1) * B] = qt[h * HD : (h + 1) * HD, :]
            qz[s, h * B : (h + 1) * B, :] = jnp.where(lane_head == h, q, 0.0).astype(bf16)
        return carry

    lax.fori_loop(0, 4, project, 0)

    def gather_ctx(s):
        return Gather(
            place, lambda j: ctx_all.at[j, s], lambda k: ctx_send.at[s, k], lambda k: ctx_recv.at[s, k]
        )

    def attend(s, h, low, high, qlow, qhigh, store):
        lanes = pl.ds(pl.multiple_of(h * B + qlow, 128), qhigh - qlow)
        scores = dot(keys[low:high, :], qz_t[s, :, lanes], NN)
        same = kid[low:high, qlow:qhigh] == qid[s, 0:1, qlow:qhigh]
        scores = jnp.where(same, scores, -1e30)
        top = jnp.max(scores, axis=0, keepdims=True)
        weights = jnp.exp(scores - top)
        inverse = 1.0 / jnp.sum(weights, axis=0, keepdims=True)
        weights = weights.astype(bf16)
        store(lanes, weights)
        rinv[s, h, 0:1, qlow:qhigh] = inverse
        head = pl.ds(pl.multiple_of(h * HD, HD), HD)
        return (dot(values_t[head, low:high], weights, NN) * inverse).astype(bf16)

    def send_ctx(s):
        span = rows(s)
        block = ctx_t[:, span]
        ctx_all[me, s, 0:B, :] = block[0:128, :].T
        last = jnp.concatenate([block[128:192, 0:128], block[128:192, 128:256]], axis=0)
        ctx_all[me, s, B : B + 128, :] = last.T
        gather_ctx(s).start()

    def attend_top(s, carry):
        def head(h, inner):
            def store(lanes, weights):
                probs[s, :, lanes] = weights

            here = pl.ds(pl.multiple_of(h * HD, HD), HD)
            ctx_t[here, rows(s)] = attend(s, h, 0, TOP, 0, B, store)
            return inner

        lax.fori_loop(0, 3, head, 0)
        send_ctx(s)

        @pl.when(s == 1)
        def _():
            gather_wo.forward()

        @pl.when(s == 2)
        def _():
            gather_cot.forward()

        return carry

    lax.fori_loop(0, 3, attend_top, 0)

    def attend_last(h, carry):
        here = pl.ds(pl.multiple_of(h * HD, HD), HD)

        def store_left(lanes, weights):
            probs_last[:, lanes] = weights

        def store_right(lanes, weights):
            probs_last[0:768, lanes] = jnp.zeros((768, 128), bf16)
            probs_last[768:1024, lanes] = weights

        ctx_t[here, 768:896] = attend(3, h, 0, 1024, 0, 128, store_left)
        ctx_t[here, 896:1024] = attend(3, h, 768, 1024, 128, 256, store_right)
        return carry

    lax.fori_loop(0, 3, attend_last, 0)
    send_ctx(3)

    gather_wo.land_core()
    gather_wo.land_far()
    gather_cot.land_core()
    gather_cot.land_far()
    for s in range(4):
        gather_ctx(s).forward()

    sum_in = Scatter(place, rs_out, rs_both, rs_far, own, rs_send, rs_recv)
    zeros_w = jnp.zeros((HD, 768), bf16)

    def middle(i, carry):
        s = me ^ (3 - i)
        span = rows(s)
        ctx = gather_ctx(s)
        ctx.land_core()
        ctx.land_far()
        left = jnp.concatenate([ctx_all[j, s, 0:B, :] for j in range(4)], axis=1)
        last = jnp.concatenate([ctx_all[j, s, B : B + 128, :] for j in range(4)], axis=1)
        w_left = jnp.concatenate([wo_all[j, 0:128, :] for j in range(4)], axis=0)
        w_tail = [wo_all[j, 128:192, :] for j in range(4)]
        w_upper = jnp.concatenate([piece for w in w_tail for piece in (w, zeros_w)], axis=0)
        w_lower = jnp.concatenate([piece for w in w_tail for piece in (zeros_w, w)], axis=0)
        branch = dot(left, w_left, NN) + jnp.concatenate(
            [dot(last, w_upper, NN), dot(last, w_lower, NN)], axis=0
        )
        h = xp[span, :].astype(f32) + (branch + vec(2))

        @pl.when(i == 3)
        def _():
            block_ref[...] = h

        hat, _ = layer_hat(h)
        stage[0:B, :] = hat
        act = (hat * vec(3) + vec(4)).astype(bf16)
        a2[span, :] = act
        u = dot(act, wup_ref[...], NN) + vec(5)
        cdf = 0.5 * (1.0 + lax.erf(u * 0.7071067811865476))
        gate[span, :] = (u * cdf).astype(bf16)
        slope = cdf + u * (0.3989422804014327 * jnp.exp(-0.5 * (u * u)))
        grad_u = (dot(cot_all[span, :], wdn_ref[...], NT) * slope).astype(bf16)
        du[span, :] = grad_u
        acc[8:9, :] += column_sum(grad_u.astype(f32))
        grad_act = dot(grad_u, wup_ref[...], NT)
        acc[2:3, :] += column_sum(grad_act * stage[0:B, :])
        acc[3:4, :] += column_sum(grad_act)
        own[...] = grad_act
        sum_in.step(i, lambda: own[...])
        return carry

    lax.fori_loop(0, 4, middle, 0)

    blocks = [Reduce(spot, first_y, refs) for first_y, refs in zip(FIRST_Y, block_refs)]
    homes = [down_hbm.at[p] for p in range(3)] + [up_hbm.at[p] for p in range(3)]
    homes += [out_hbm.at[0]] + [qkv_hbm.at[p] for p in range(3)]
    saves = [pltpu.make_async_copy(blocks[p].whole, homes[p], local_sem.at[p]) for p in range(10)]

    def poll(name):
        for p, k in POLLS.get(name, ()):
            blocks[p].stage(k)
            if k == STAGES - 1:
                saves[p].start()

    def poll_at(prefix, index, count):
        for n in range(count):
            if POLLS.get(f"{prefix}{n}"):
                pl.when(index == n)(lambda n=n: poll(f"{prefix}{n}"))

    def stage_grad(p, piece):
        quarter = QUARTER[p]
        for h in range(2):
            for c in range(4):
                part = piece[c * quarter : (c + 1) * quarter, h * 384 : (h + 1) * 384]
                blocks[p].part[h, c] = part.astype(bf16)

    for t in range(3):
        stage_grad(t, dot(gate[:, t * B : (t + 1) * B], cot_all[...], TN))
        poll(f"down{t}")
    for t in range(3):
        stage_grad(3 + t, dot(a2[:, t * B : (t + 1) * B], du[...], TN))
        poll(f"up{t}")

    grad_act = sum_in.finish()
    hat, factor = layer_hat(block_ref[...])
    cot_own = cot_all[rows(me), :].astype(f32)
    grad_h = cot_own + layer_back(grad_act * vec(3), hat, factor)
    input_ref[...] = grad_h
    grad_branch = grad_h.astype(bf16)
    do_all[rows(me), :] = grad_branch
    gather_do = Gather(place, lambda s: do_all.at[rows(s)], lambda k: do_send.at[k], lambda k: do_recv.at[k])
    gather_do.start()
    acc[4:5, :] = column_sum(grad_branch.astype(f32))
    acc[5:6, :] = column_sum(cot_own)

    sum_out = Scatter(place, ms_out, ms_both, ms_far, m_own, ms_send, ms_recv)

    def project_down(i, carry):
        s = me ^ (3 - i)
        m_own[...] = dot(gate[rows(s), :], wdn_ref[...], NN)
        sum_out.step(i, lambda: m_own[...])
        poll_at("mlp", i, 4)
        return carry

    poll("own")
    lax.fori_loop(0, 4, project_down, 0)

    dk[...] = jnp.zeros(dk.shape, f32)
    dv[...] = jnp.zeros(dv.shape, f32)

    def back_head(s, h, low, high, qlow, qhigh, ref):
        lanes = pl.ds(pl.multiple_of(h * B + qlow, 128), qhigh - qlow)
        head = pl.ds(pl.multiple_of(h * HD, HD), HD)
        weights = ref[low:high, lanes]
        grad_probs = dot(values[low:high, :], dcz_t[:, lanes], NN)
        grad_scores = weights.astype(f32) * (grad_probs - delta[h, 0:1, qlow:qhigh])
        grad_scores = grad_scores.astype(bf16)
        ref[low:high, lanes] = grad_scores
        return dot(keys_t[head, low:high], grad_scores, NN)

    def back_block(i, carry):
        s = me ^ i
        span = rows(s)

        @pl.when(i == 1)
        def _():
            gather_do.land_core()

        @pl.when(i == 2)
        def _():
            gather_do.forward()

        @pl.when(i == 3)
        def _():
            gather_do.land_far()

        grad_ctx = dot(wo_ref[...], do_all[span, :], NT).astype(bf16).astype(f32)
        for h in range(3):
            here = slice(h * HD, (h + 1) * HD)
            scaled = (grad_ctx[here, :] * rinv[s, h, 0:1, :]).astype(bf16)
            delta[h, 0:1, :] = column_sum(scaled.astype(f32) * ctx_t[here, span].astype(f32))
            dcz_t[here, h * B : (h + 1) * B] = scaled
            turned = jnp.concatenate([scaled, jnp.zeros((HD, B), bf16)], axis=0).T.astype(f32)
            wide = jnp.concatenate([turned, turned], axis=1)[:, 0:192]
            if h == 1:
                wide = pltpu.roll(jnp.concatenate([turned, jnp.zeros((B, 128), f32)], axis=1), HD, 1)[:, 0:192]
            dcz[h * B : (h + 1) * B, :] = jnp.where(lane_head == h, wide, 0.0).astype(bf16)

        @pl.when(s != 3)
        def _():
            dv[0:TOP, :] += dot(probs[s], dcz[...], NN)

        @pl.when(s == 3)
        def _():
            dv[...] += dot(probs_last[...], dcz[...], NN)

        def head(h, inner):
            here = pl.ds(pl.multiple_of(h * HD, HD), HD)

            @pl.when(s != 3)
            def _():
                stage[here, 0:B] = back_head(s, h, 0, TOP, 0, B, probs.at[s])

            @pl.when(s == 3)
            def _():
                stage[here, 0:128] = back_head(s, h, 0, 1024, 0, 128, probs_last)
                stage[here, 128:256] = back_head(s, h, 768, 1024, 128, 256, probs_last)

            poll_at("attend", i * 3 + h, 12)
            return inner

        lax.fori_loop(0, 3, head, 0)

        @pl.when(s != 3)
        def _():
            dk[0:TOP, :] += dot(probs[s], qz[s], NN)

        @pl.when(s == 3)
        def _():
            dk[...] += dot(probs_last[...], qz[s], NN)

        dq[span, :] = (stage[0:192, 0:B] * HD**-0.5).T.astype(bf16)
        return carry

    dcz_t[...] = jnp.zeros(dcz_t.shape, bf16)
    lax.fori_loop(0, 4, back_block, 0)

    stage_grad(6, dot(ctx_t[...], do_all[...], NN))
    poll("out")
    dkb[...] = dk[...].astype(bf16)
    dvb[...] = dv[...].astype(bf16)
    for t, ref in enumerate((dq, dkb, dvb)):
        stage_grad(7 + t, dot(ref[...], a1[...], TN))
        poll(f"qkv{t}")
    acc[9:10, 0:192] = column_sum(dq[...].astype(f32))
    acc[9:10, 256:448] = column_sum(dvb[...].astype(f32))

    sum_first = Scatter(place, rs_out, rs_both, rs_far, own, rt_send, rt_recv)

    def project_back(i, carry):
        s = me ^ (3 - i)
        span = rows(s)
        grad = dot(dq[span, :], wqkv_ref[0], NN)
        grad = grad + dot(dkb[span, :], wqkv_ref[1], NN)
        grad = grad + dot(dvb[span, :], wqkv_ref[2], NN)
        hat, _ = layer_hat(xp[span, :].astype(f32))
        acc[0:1, :] += column_sum(grad * hat)
        acc[1:2, :] += column_sum(grad)
        own[...] = grad
        sum_first.step(i, lambda: own[...])
        poll_at("first", i, 4)
        return carry

    lax.fori_loop(0, 4, project_back, 0)

    v_mp[me] = acc[...]
    v_copies = [remote(v_mp.at[me], v_mp.at[me], v_send.at[j - 1], v_recv.at[j - 1], (dp, me ^ j)) for j in (1, 2, 3)]
    v_lands = [remote(v_mp.at[me ^ j], v_mp.at[me ^ j], v_send.at[j - 1], v_recv.at[j - 1], (dp, me ^ j)) for j in (1, 2, 3)]
    for copy in v_copies:
        copy.start()
    poll("sums0")
    for copy in v_lands:
        copy.wait_recv()
    acc[0:8, :] = v_mp[0, 0:8, :] + v_mp[1, 0:8, :] + v_mp[2, 0:8, :] + v_mp[3, 0:8, :]
    vy_copy = remote(acc, v_y, v_send.at[3], v_recv.at[3], ypeer)
    vy_copy.start()
    poll("sums1")
    vy_copy.wait_recv()
    v_z[zi] = acc[...] + v_y[...]
    vz_copies = [remote(v_z.at[zi], v_z.at[zi], v_send.at[3 + j], v_recv.at[3 + j], zpeers[j - 1]) for j in (1, 2, 3)]
    vz_lands = [remote(v_z.at[zi ^ j], v_z.at[zi ^ j], v_send.at[3 + j], v_recv.at[3 + j], zpeers[j - 1]) for j in (1, 2, 3)]
    for copy in vz_copies:
        copy.start()
    poll("sums2")

    block_ref[...] = block_ref[...] + (sum_out.finish() + vec(6))
    for copy in vz_lands:
        copy.wait_recv()
    sums_ref[...] = v_z[0] + v_z[1] + v_z[2] + v_z[3]

    grad_act = sum_first.finish()
    hat, factor = layer_hat(xp[rows(me), :].astype(f32))
    input_ref[...] = input_ref[...] + layer_back(grad_act * vec(0), hat, factor)

    poll("tail")

    for copy in v_copies + [vy_copy] + vz_copies:
        copy.wait_send()
    for gather in [gather_wo, gather_cot, gather_do] + [gather_ctx(s) for s in range(4)]:
        gather.close()
    for block in blocks:
        block.close()
    for save in saves:
        save.wait()


def finish_kernel(
    block_hbm, input_hbm, sums_hbm, down_hbm, up_hbm, out_hbm, qkv_hbm,
    block_out, input_grad, gain_first, shift_first, grad_qkv, grad_qv, grad_out, out_bias, gain_second, shift_second,
    grad_up, up_bias, grad_down, down_bias,
    block_v, input_v, sums, down_v, up_v, out_v, qkv_v, block_w, input_w, down_w, up_w, out_w, qkv_w,
    in_sem, out_sem,
):
    share = block_out.shape[0]
    pairs = (
        (down_hbm, down_v), (up_hbm, up_v), (qkv_hbm, qkv_v), (block_hbm, block_v), (input_hbm, input_v),
        (out_hbm, out_v), (sums_hbm, sums),
    )
    loads = [pltpu.make_async_copy(src, dst, in_sem.at[k]) for k, (src, dst) in enumerate(pairs)]
    for load in loads:
        load.start()
    stores = []

    def save(src, dst):
        stores.append(pltpu.make_async_copy(src, dst, out_sem.at[len(stores)]))
        stores[-1].start()

    def widen(source, p, put):
        quarter = source.shape[3]
        for h in range(2):
            for c in range(4):
                put(slice(c * quarter, (c + 1) * quarter), slice(h * 384, (h + 1) * 384), source[p, h, c].astype(f32))

    for k, (source, wide, target) in enumerate(((down_v, down_w, grad_down), (up_v, up_w, grad_up))):
        loads[k].wait()
        for p in range(3):

            def put(r, lanes, value):
                wide[p * B + r.start : p * B + r.stop, lanes] = value

            widen(source, p, put)
        save(wide, target)
    loads[2].wait()
    for p in range(3):

        def put(r, lanes, value):
            qkv_w[p, r, lanes] = value

        widen(qkv_v, p, put)
    save(qkv_w, grad_qkv)
    for k, source, wide, target in ((3, block_v, block_w, block_out), (4, input_v, input_w, input_grad)):
        loads[k].wait()
        wide[...] = source[0:share, :]
        save(wide, target)
    loads[5].wait()

    def put(r, lanes, value):
        out_w[r, lanes] = value

    widen(out_v, 0, put)
    save(out_w, grad_out)
    loads[6].wait()
    for r, ref in enumerate((gain_first, shift_first, gain_second, shift_second, out_bias, down_bias)):
        ref[...] = sums[r, :]
    up_bias[...] = sums[8, :]
    grad_qv[0:1, :] = sums[9:10, 0:192]
    grad_qv[1:2, :] = sums[9:10, 256:448]
    for store in stores:
        store.wait()


def per_device(
    inputs, image_of_row, gain_first, shift_first, qkv_weight, qv_bias, out_weight, out_bias, gain_second,
    shift_second, up_weight, up_bias, down_weight, down_bias, cotangent,
):
    share = cotangent.shape[0]
    vmem, smem, anyspace = (pl.BlockSpec(memory_space=m) for m in (pltpu.VMEM, pltpu.SMEM, pl.ANY))

    def shape(*dims, dtype=bf16):
        return pltpu.VMEM(dims, dtype)

    dma = pltpu.SemaphoreType.DMA

    def block_scratch(first_y, r):
        over = shape(4, r, 384) if first_y else shape(r, 384)
        along = shape(3, r, 384) if first_y else shape(2, 3, r, 384)
        return [shape(2, 4, r, 384), over, along, along, shape(2, 4, r, 384), dma((13,)), dma((13,))]

    scratch = [
        shape(1024, 768), shape(272, 768, dtype=f32), shape(1024, 768),
        shape(1024, 192), shape(1024, 192), shape(192, 1024), shape(192, 1024),
        shape(4, 192, 768), shape(4, 768, 192),
        shape(1024, B, dtype=i32), shape(4, 8, B, dtype=i32),
        shape(3, TOP, 768), shape(1024, 768), shape(4, 3, 8, B, dtype=f32),
        shape(192, 1024), shape(4, 4, 384, 128), shape(4, 192, 768), shape(1024, 768),
        shape(1024, 768), shape(1024, 768), shape(1024, 768), shape(1024, 768),
        shape(192, 768), shape(768, 192), shape(3, 8, B, dtype=f32),
        shape(1024, 192), shape(1024, 192, dtype=f32), shape(1024, 192, dtype=f32),
        shape(1024, 192), shape(1024, 192), shape(B, 768, dtype=f32),
        shape(3, B, 768), shape(2, B, 768), shape(B, 768),
        shape(3, B, 768), shape(2, B, 768), shape(B, 768), shape(B, 768, dtype=f32),
        shape(8, 768, dtype=f32),
        shape(16, 768, dtype=f32), shape(4, 16, 768, dtype=f32), shape(16, 768, dtype=f32), shape(4, 16, 768, dtype=f32),
    ]
    scratch += [dma((3,))] * 4 + [dma((4, 3))] * 2 + [dma((3,))] * 8 + [dma((7,))] * 2 + [dma((10,))]
    scratch += [[block_scratch(first_y, r) for first_y, r in zip(FIRST_Y, QUARTER)]]
    results = pl.pallas_call(
        layer_kernel,
        out_shape=[
            jax.ShapeDtypeStruct((B, 768), f32),
            jax.ShapeDtypeStruct((B, 768), f32),
            jax.ShapeDtypeStruct((16, 768), f32),
            jax.ShapeDtypeStruct((3, 2, 4, 64, 384), bf16),
            jax.ShapeDtypeStruct((3, 2, 4, 64, 384), bf16),
            jax.ShapeDtypeStruct((1, 2, 4, 48, 384), bf16),
            jax.ShapeDtypeStruct((3, 2, 4, 48, 384), bf16),
        ],
        in_specs=[vmem, smem] + [vmem] * 13,
        out_specs=[vmem] * 3 + [anyspace] * 4,
        scratch_shapes=scratch,
        compiler_params=pltpu.CompilerParams(
            collective_id=0, has_side_effects=True, vmem_limit_bytes=60 * 2**20
        ),
        name="layer",
    )(
        inputs, image_of_row, gain_first, shift_first, qv_bias, out_bias, gain_second, shift_second, up_bias, down_bias,
        jnp.swapaxes(qkv_weight, 1, 2), out_weight, up_weight, down_weight, cotangent,
    )

    def out(*dims):
        return jax.ShapeDtypeStruct(dims, f32)

    wide = [shape(share, 768, dtype=f32)] * 2 + [shape(768, 768, dtype=f32)] * 2
    outputs = pl.pallas_call(
        finish_kernel,
        out_shape=[
            out(share, 768), out(share, 768), out(768), out(768), out(3, 192, 768), out(2, 192), out(192, 768),
            out(768), out(768), out(768), out(768, 768), out(768), out(768, 768), out(768),
        ],
        in_specs=[anyspace] * 7,
        out_specs=[anyspace if k in (0, 1, 4, 6, 10, 12) else vmem for k in range(14)],
        scratch_shapes=[pltpu.VMEM(r.shape, r.dtype) for r in results]
        + wide + [shape(192, 768, dtype=f32), shape(3, 192, 768, dtype=f32), dma((7,)), dma((6,))],
        compiler_params=pltpu.CompilerParams(vmem_limit_bytes=60 * 2**20),
        name="finish",
    )(*results)
    return (*outputs[:4], jnp.swapaxes(outputs[4], 1, 2), *outputs[5:])


def solution(mesh):
    return jax.shard_map(
        per_device,
        mesh=mesh,
        in_specs=(
            P("dp", None),
            P("dp"),
            P(),
            P(),
            P(None, None, "mp"),
            P(None, "mp"),
            P("mp", None),
            P(),
            P(),
            P(),
            P(None, "mp"),
            P("mp"),
            P("mp", None),
            P(),
            P(("dp", "mp"), None),
        ),
        out_specs=(
            P(("dp", "mp"), None),
            P(("dp", "mp"), None),
            P(),
            P(),
            P(None, None, "mp"),
            P(None, "mp"),
            P("mp", None),
            P(),
            P(),
            P(),
            P(None, "mp"),
            P("mp"),
            P("mp", None),
            P(),
        ),
        check_vma=False,
    )
```

```python
import functools

import jax
import jax.numpy as jnp
from jax import lax
from jax.experimental import pallas as pl
from jax.experimental.pallas import tpu as pltpu
from jax.sharding import PartitionSpec as P

f32, bf16, i32 = jnp.float32, jnp.bfloat16, jnp.int32
MESH = pl.DeviceIdType.MESH
NN = (((1,), (0,)), ((), ()))
NT = (((1,), (1,)), ((), ()))
TN = (((0,), (0,)), ((), ()))
HD = 64
P_LO = 196
EPSILON = 1e-06
B = 256
TOP = 832
BIG = 4 * P_LO


def dot(left, right, dims):
    return lax.dot_general(left, right, dims, preferred_element_type=f32)


def rows(start, size=B):
    return pl.ds(pl.multiple_of(start * size, size), size)


def layer_hat(values):
    center = values - jnp.mean(values, axis=1, keepdims=True)
    factor = lax.rsqrt(jnp.mean(center * center, axis=1, keepdims=True) + EPSILON)
    return center * factor, factor


def layer_back(grad_hat, normed, factor):
    first = jnp.mean(grad_hat, axis=1, keepdims=True)
    second = jnp.mean(grad_hat * normed, axis=1, keepdims=True)
    return factor * (grad_hat - first - normed * second)


def column_sum(values):
    return jnp.sum(values, axis=0, keepdims=True)


def remote(src, dst, send, recv, device):
    return pltpu.make_async_remote_copy(
        src_ref=src, dst_ref=dst, send_sem=send, recv_sem=recv, device_id=device, device_id_type=MESH
    )


class Gather:
    def __init__(self, place, view, send, recv):
        self.me, self.core, self.across = place
        self.view, self.send, self.recv = view, send, recv

    def copy(self, slot, k, device):
        return remote(self.view(slot), self.view(slot), self.send(k), self.recv(k), device)

    def start(self):
        self.copy(self.me, 1, self.across).start()
        self.copy(self.me, 0, self.core).start()

    def forward(self):
        slot = self.me ^ 2
        self.copy(slot, 1, self.across).wait_recv()
        self.copy(slot, 2, self.core).start()

    def land_core(self):
        self.copy(self.me ^ 1, 0, self.core).wait_recv()

    def land_far(self):
        self.copy(self.me ^ 3, 2, self.core).wait_recv()

    def close(self):
        for k in range(3):
            self.copy(self.me, k, self.core).wait_send()


class Scatter:
    def __init__(self, place, out, both, far, own, send, recv):
        self.me, self.core, self.across = place
        self.out, self.both, self.far, self.own = out, both, far, own
        self.send, self.recv = send, recv

    def copy(self, k):
        src = self.out.at[k]
        dst = self.far if k == 1 else self.both.at[k // 2]
        return remote(src, dst, self.send.at[k], self.recv.at[k], self.across if k == 1 else self.core)

    def step(self, i, value, hold=False):
        @pl.when(i == 0)
        def _():
            self.out[0] = value().astype(bf16)
            self.copy(0).start()

        @pl.when(i == 1)
        def _():
            if hold:
                self.out[1] = value().astype(bf16)
            else:
                self.copy(0).wait_recv()
                self.out[1] = (value() + self.both[0].astype(f32)).astype(bf16)
                self.copy(1).start()

        @pl.when(i == 2)
        def _():
            self.out[2] = value().astype(bf16)
            self.copy(2).start()

        @pl.when(i == 3)
        def _():
            self.own[...] = value()

    def release(self):
        self.copy(0).wait_recv()
        self.out[1] = (self.out[1].astype(f32) + self.both[0].astype(f32)).astype(bf16)
        self.copy(1).start()

    def finish(self):
        self.copy(2).wait_recv()
        self.copy(1).wait_recv()
        total = self.own[...] + self.both[1].astype(f32) + self.far[...].astype(f32)
        for k in range(3):
            self.copy(k).wait_send()
        return total


class Reduce:
    def __init__(self, spot, first_y, refs):
        self.zi, self.yi, self.over, self.above, self.below = spot
        self.first_y = first_y
        self.part, self.ybuf, self.up, self.down, self.whole, self.send, self.recv = refs
        self.sent = []

    def copy(self, src, dst, k, device):
        return remote(src, dst, self.send.at[k], self.recv.at[k], device)

    def begin(self, condition, make):
        self.sent.append((condition, make))
        if condition is None:
            make().start()
        else:
            pl.when(condition())(lambda: make().start())

    def close(self):
        for condition, make in self.sent:
            if condition is None:
                make().wait_send()
            else:
                pl.when(condition())(lambda make=make: make().wait_send())

    def chunks(self, first, count):
        return self.part.at[self.yi if self.first_y else slice(None), pl.ds(first, count)]

    def rising(self, first, count):
        span = pl.ds(first - 1, count)
        return self.up.at[span] if self.first_y else self.up.at[:, span]

    def falling(self, first, count):
        span = pl.ds(first, count)
        return self.down.at[span] if self.first_y else self.down.at[:, span]

    def result(self, chunk):
        return self.whole.at[self.yi if self.first_y else slice(None), chunk]

    def copy_up(self, first, count, src):
        return self.copy(src, self.rising(first, count), 1, self.above)

    def copy_down(self, first, count, src):
        return self.copy(src, self.falling(first, count), 2, self.below)

    def at(self, z):
        return lambda: self.zi == z

    def hop(self, n):
        up_first, down_count = n, 4 - n

        def up_view():
            return self.chunks(n, 4 - n) if n == 1 else self.rising(n, 4 - n)

        def down_view():
            return self.chunks(0, 4 - n) if n == 1 else self.falling(0, 4 - n)

        if n > 1:

            @pl.when(self.zi == n - 1)
            def _():
                came = self.rising(n - 1, 5 - n)
                self.copy_up(n - 1, 5 - n, came).wait_recv()
                view, own = self.rising(n, 4 - n), self.chunks(n, 4 - n)
                view[...] = (view[...].astype(f32) + own[...].astype(f32)).astype(bf16)

            @pl.when(self.zi == 4 - n)
            def _():
                came = self.falling(0, 5 - n)
                self.copy_down(0, 5 - n, came).wait_recv()
                view, own = self.falling(0, 4 - n), self.chunks(0, 4 - n)
                view[...] = (view[...].astype(f32) + own[...].astype(f32)).astype(bf16)

        self.begin(self.at(n - 1), lambda: self.copy_up(up_first, 4 - n, up_view()))
        self.begin(self.at(4 - n), lambda: self.copy_down(0, down_count, down_view()))

    def total(self, store):
        def plain(view):
            return view[...].astype(f32)

        @pl.when(self.zi == 0)
        def _():
            self.copy_down(0, 1, self.falling(0, 1)).wait_recv()
            store(0, plain(self.chunks(0, 1)) + plain(self.falling(0, 1)))

        @pl.when(self.zi == 3)
        def _():
            self.copy_up(3, 1, self.rising(3, 1)).wait_recv()
            store(3, plain(self.chunks(3, 1)) + plain(self.rising(3, 1)))

        for z in (1, 2):

            @pl.when(self.zi == z)
            def _(z=z):
                value = plain(self.chunks(z, 1)) + plain(self.rising(z, 1)) + plain(self.falling(z, 1))
                store(z, value)

    def back(self, d):
        for sign, base, ahead, room in ((-1, 3, self.above, lambda: self.zi < 3), (1, 6, self.below, lambda: self.zi > 0)):

            def here(sign=sign):
                return self.zi >= d if sign < 0 else self.zi <= 3 - d

            def view(sign=sign):
                return self.result(self.zi + sign * d)

            if d > 0:

                @pl.when(here())
                def _():
                    self.copy(view(), view(), base + d - 1, ahead).wait_recv()

            if d < 3:
                self.begin(
                    lambda room=room, here=here: room() & here(),
                    lambda view=view, base=base, ahead=ahead: self.copy(view(), view(), base + d, ahead),
                )
            if self.first_y and (d > 0 or sign < 0):
                self.begin(
                    here, lambda view=view, sign=sign: self.copy_over(self.yi, self.zi + sign * d)
                )

    def copy_over(self, half, chunk):
        view = self.whole.at[half, chunk]
        return self.copy(view, view, 9 + (chunk if self.first_y else 0), self.over)

    def sum_over(self):
        if self.first_y:
            return self.copy(self.part.at[1 - self.yi], self.ybuf, 0, self.over)
        return self.copy(self.part.at[1 - self.yi, self.zi], self.ybuf, 0, self.over)

    def stage(self, k):
        if self.first_y:
            if k == 0:
                self.begin(None, self.sum_over)
            elif k == 1:
                self.sum_over().wait_recv()

                def add(c, carry):
                    value = self.part[self.yi, c].astype(f32) + self.ybuf[c].astype(f32)
                    self.part[self.yi, c] = value.astype(bf16)
                    return carry

                lax.fori_loop(0, 4, add, 0)
                self.hop(1)
            elif k in (2, 3):
                self.hop(k)
            elif k == 4:

                def store(z, value):
                    self.whole[self.yi, z] = value[0].astype(bf16)

                self.total(store)
                self.back(0)
            elif k in (5, 6, 7):
                self.back(k - 4)
            else:
                for c in range(4):
                    self.copy_over(1 - self.yi, c).wait_recv()
        else:
            if k in (0, 1, 2):
                self.hop(k + 1)
            elif k == 3:

                def store(z, value):
                    self.part[:, z] = value[:, 0].astype(bf16)

                self.total(store)
                self.begin(None, self.sum_over)
            elif k == 4:
                self.sum_over().wait_recv()
                value = self.part[self.yi, self.zi].astype(f32) + self.ybuf[...].astype(f32)
                self.whole[self.yi, self.zi] = value.astype(bf16)
                self.begin(None, lambda: self.copy_over(self.yi, self.zi))
            elif k == 5:
                self.copy_over(1 - self.yi, self.zi).wait_recv()
                self.back(0)
            else:
                self.back(k - 5)


FIRST_Y = (False, True, True, True, True, True, True, True, True, True)
QUARTER = (64,) * 6 + (48,) * 4
STAGES = 9

POLLS = {
    "down0": ((0, 0),),
    "down1": ((1, 0),),
    "down2": ((2, 0),),
    "up0": ((3, 0), (1, 1),),
    "up1": ((4, 0),),
    "up2": ((0, 1), (5, 0),),
    "rs1": ((2, 1), (1, 2),),
    "own": ((0, 2), (3, 1),),
    "attend0": ((1, 3), (2, 2),),
    "attend3": ((1, 4), (0, 3), (3, 2),),
    "attend4": ((2, 3), (4, 1),),
    "do": ((5, 1), (1, 5),),
    "attend6": ((0, 4), (2, 4), (3, 3),),
    "attend7": ((1, 6), (4, 2),),
    "attend9": ((0, 5), (3, 4), (5, 2),),
    "attend10": ((1, 7), (2, 5), (4, 3),),
    "out": ((6, 0),),
    "qkv0": ((7, 0),),
    "qkv1": ((1, 8), (0, 6), (8, 0),),
    "qkv2": ((9, 0),),
    "first0": ((3, 5),),
    "first2": ((4, 4), (5, 3),),
    "first3": ((2, 6), (6, 1),),
    "tail": ((10, 0), (11, 0), (0, 7), (3, 6), (7, 1), (4, 5), (5, 4), (6, 2), (2, 7), (8, 1), (0, 8), (7, 2), (3, 7), (12, 0), (4, 6), (6, 3), (9, 1), (10, 1), (5, 5), (8, 2), (7, 3), (4, 7), (6, 4), (9, 2), (5, 6), (8, 3), (7, 4), (6, 5), (2, 8), (5, 7), (9, 3), (3, 8), (8, 4), (7, 5), (6, 6), (10, 2), (9, 4), (8, 5), (4, 8), (7, 6), (6, 7), (5, 8), (10, 3), (9, 5), (7, 7), (8, 6), (6, 8), (9, 6), (8, 7), (7, 8), (9, 7), (8, 8), (9, 8),),
}


def layer_kernel(
    x_hbm, ids_ref, gain_a, shift_a, bias_qv, bias_out, gain_b, shift_b, bias_up, bias_down,
    wqkv_hbm, wo_hbm, wup_hbm, wdn_hbm, cot_hbm,
    block_ref, input_ref, sums_ref, down_hbm, up_hbm, out_hbm, qkv_hbm,
    xp, stage, a1, keys, values, keys_t, values_t, qz_t, qz, kid, qid, probs, probs_last, rinv, ctx_t, ctx_all,
    wo_all, cot_all, a2, gate, du, do_all, dcz_t, dcz, delta, dq, dk, dv, dkb, dvb, own,
    rs_out, rs_both, rs_far, ms_out, ms_both, ms_far, m_own,
    vec_ref, acc, v_mp, v_y, v_z,
    wo_send, wo_recv, cot_send, cot_recv, ctx_send, ctx_recv, do_send, do_recv,
    rs_send, rs_recv, ms_send, ms_recv, rt_send, rt_recv,
    v_send, v_recv, local_sem, load_sem, x_ref, wqkv_ref, wup_ref, wdn_ref, cot_ref, vec_raw, qv_raw, block_refs,
):
    dp, me = lax.axis_index("dp"), lax.axis_index("mp")
    core, across, diagonal = (dp, me ^ 1), (dp, me ^ 2), (dp, me ^ 3)
    yi, zi = dp & 1, (dp >> 1) & 3
    ypeer = (dp ^ 1, me)
    zpeers = [(dp ^ (2 * j), me) for j in (1, 2, 3)]
    place = (me, core, across)
    base = dp & ~7
    above, below = (base + (((zi + 1) & 3) << 1) + yi, me), (base + (((zi + 3) & 3) << 1) + yi, me)
    spot = (zi, yi, ypeer, above, below)
    share = cot_hbm.shape[0]

    barrier = pltpu.get_barrier_semaphore()
    partners = [core, across, diagonal, ypeer] + zpeers
    for partner in partners:
        pl.semaphore_signal(barrier, inc=1, device_id=partner, device_id_type=MESH)

    def vec(r, width=None):
        return vec_ref[r : r + 1, :] if width is None else vec_ref[r : r + 1, width[0] : width[1]]

    pairs = [(cot_hbm, cot_ref), (x_hbm, x_ref), (wo_hbm, wo_all.at[me]), (bias_qv, qv_raw)]
    pairs += list(zip((gain_a, shift_a, bias_out, gain_b, shift_b, bias_up, bias_down), vec_raw))
    pairs += [(wqkv_hbm, wqkv_ref), (wup_hbm, wup_ref), (wdn_hbm, wdn_ref)]
    loads = [pltpu.make_async_copy(src, dst, load_sem.at[k]) for k, (src, dst) in enumerate(pairs)]
    for load in loads:
        load.start()
    pl.semaphore_wait(barrier, len(partners))

    gather_wo = Gather(place, lambda s: wo_all.at[s], lambda k: wo_send.at[k], lambda k: wo_recv.at[k])
    loads[2].wait()
    gather_wo.start()

    def gather_cot(q):
        return Gather(
            place,
            lambda s: cot_all.at[pl.ds(pl.multiple_of(s * B + q * 64, 64), 64)],
            lambda k: cot_send.at[q, k],
            lambda k: cot_recv.at[q, k],
        )

    loads[0].wait()
    stage[240:256, :] = jnp.zeros((16, 768), f32)
    stage[0:share, :] = cot_ref[...].astype(f32)
    cot_all[rows(me), :] = stage[0:B, :].astype(bf16)
    gather_cot(0).start()
    acc[...] = jnp.zeros(acc.shape, f32)
    for k in range(3, 11):
        loads[k].wait()
    for r, ref in enumerate(vec_raw):
        vec_ref[r : r + 1, :] = ref[...].astype(f32).reshape(1, 768)
    vec_ref[7:8, 0:192] = qv_raw[0:1, :].astype(f32)
    vec_ref[7:8, 256:448] = qv_raw[1:2, :].astype(f32)
    loads[1].wait()

    row_in = lax.broadcasted_iota(i32, (B, 768), 0)
    for s in range(4):
        first = s * share // 16 * 16
        last = min(first + 272, 4 * share)
        stage[0 : last - first, :] = x_ref[first:last, :].astype(f32)
        moved = stage[s * share - first : s * share - first + B, :]
        xp[s * B : (s + 1) * B, :] = jnp.where(row_in < share, moved, 0.0).astype(bf16)

    two_images = (ids_ref[0] == ids_ref[BIG - 1]).astype(i32)

    def image_of(index, shard, pad):
        place_of = index + shard * share
        small = jnp.zeros_like(index)
        for k in range(1, 5):
            small = small + (place_of >= k * P_LO).astype(i32)
        large = (place_of >= BIG).astype(i32)
        image = small * (1 - two_images) + large * two_images
        return jnp.where(index < share, image, pad)

    def images(s, carry):
        kid[rows(s), :] = image_of(lax.broadcasted_iota(i32, (B, B), 0), s, -1)
        qid[s] = image_of(lax.broadcasted_iota(i32, (8, B), 1), s, -2)
        qz_t[s] = jnp.zeros(qz_t.shape[1:], bf16)
        return carry

    lax.fori_loop(0, 4, images, 0)

    lane_head = lax.broadcasted_iota(i32, (B, 192), 1) // HD

    def project(s, carry):
        span = rows(s)
        hat, _ = layer_hat(xp[span, :].astype(f32))
        act = (hat * vec(0) + vec(1)).astype(bf16)
        a1[span, :] = act
        q = (dot(act, wqkv_ref[0], NT) + vec(7, (0, 192))).astype(bf16)
        k = dot(act, wqkv_ref[1], NT).astype(bf16)
        v = (dot(act, wqkv_ref[2], NT) + vec(7, (256, 448))).astype(bf16)
        keys[span, :] = k
        values[span, :] = v
        keys_t[:, span] = k.T
        values_t[:, span] = v.T
        q = q.astype(f32) * HD**-0.5
        qt = q.astype(bf16).T
        for h in range(3):
            qz_t[s, h * HD : (h + 1) * HD, h * B : (h + 1) * B] = qt[h * HD : (h + 1) * HD, :]
            qz[s, h * B : (h + 1) * B, :] = jnp.where(lane_head == h, q, 0.0).astype(bf16)
        return carry

    loads[11].wait()
    lax.fori_loop(0, 4, project, 0)

    def gather_ctx(s):
        return Gather(
            place, lambda j: ctx_all.at[j, s], lambda k: ctx_send.at[s, k], lambda k: ctx_recv.at[s, k]
        )

    def attend(s, h, low, high, qlow, qhigh, store):
        lanes = pl.ds(pl.multiple_of(h * B + qlow, 128), qhigh - qlow)
        scores = dot(keys[low:high, :], qz_t[s, :, lanes], NN)
        same = kid[low:high, qlow:qhigh] == qid[s, 0:1, qlow:qhigh]
        scores = jnp.where(same, scores, -1e30)
        top = jnp.max(scores, axis=0, keepdims=True)
        weights = jnp.exp(scores - top)
        inverse = 1.0 / jnp.sum(weights, axis=0, keepdims=True)
        weights = weights.astype(bf16)
        store(lanes, weights)
        rinv[s, h, 0:1, qlow:qhigh] = inverse
        head = pl.ds(pl.multiple_of(h * HD, HD), HD)
        return (dot(values_t[head, low:high], weights, NN) * inverse).astype(bf16)

    def send_ctx(s):
        span = rows(s)
        block = ctx_t[:, span]
        ctx_all[me, s, 0:B, :] = block[0:128, :].T
        last = jnp.concatenate([block[128:192, 0:128], block[128:192, 128:256]], axis=0)
        ctx_all[me, s, B : B + 128, :] = last.T
        gather_ctx(s).start()

    def attend_top(s, carry):
        def head(h, inner):
            def store(lanes, weights):
                probs[s, :, lanes] = weights

            here = pl.ds(pl.multiple_of(h * HD, HD), HD)
            ctx_t[here, rows(s)] = attend(s, h, 0, TOP, 0, B, store)
            return inner

        lax.fori_loop(0, 3, head, 0)
        send_ctx(s)

        @pl.when(s == 1)
        def _():
            gather_wo.forward()

        return carry

    lax.fori_loop(0, 3, attend_top, 0)

    def attend_last(h, carry):
        here = pl.ds(pl.multiple_of(h * HD, HD), HD)

        def store_left(lanes, weights):
            probs_last[:, lanes] = weights

        def store_right(lanes, weights):
            probs_last[0:768, lanes] = jnp.zeros((768, 128), bf16)
            probs_last[768:1024, lanes] = weights

        ctx_t[here, 768:896] = attend(3, h, 0, 1024, 0, 128, store_left)
        ctx_t[here, 896:1024] = attend(3, h, 768, 1024, 128, 256, store_right)
        return carry

    lax.fori_loop(0, 3, attend_last, 0)
    send_ctx(3)

    for q in (1, 2, 3):
        gather_cot(q).start()
    gather_wo.land_core()
    gather_wo.land_far()
    for s in range(4):
        gather_ctx(s).forward()
    loads[12].wait()
    loads[13].wait()

    zeros_w = jnp.zeros((HD, 768), bf16)

    def middle(i, carry):
        s = me ^ (3 - i)
        span = rows(s)
        ctx = gather_ctx(s)
        ctx.land_core()
        ctx.land_far()
        left = jnp.concatenate([ctx_all[j, s, 0:B, :] for j in range(4)], axis=1)
        last = jnp.concatenate([ctx_all[j, s, B : B + 128, :] for j in range(4)], axis=1)
        w_left = jnp.concatenate([wo_all[j, 0:128, :] for j in range(4)], axis=0)
        w_tail = [wo_all[j, 128:192, :] for j in range(4)]
        w_upper = jnp.concatenate([piece for w in w_tail for piece in (w, zeros_w)], axis=0)
        w_lower = jnp.concatenate([piece for w in w_tail for piece in (zeros_w, w)], axis=0)
        branch = dot(left, w_left, NN) + jnp.concatenate(
            [dot(last, w_upper, NN), dot(last, w_lower, NN)], axis=0
        )
        h = xp[span, :].astype(f32) + (branch + vec(2))

        @pl.when(i == 3)
        def _():
            block_ref[...] = h

        hat, _ = layer_hat(h)
        act = (hat * vec(3) + vec(4)).astype(bf16)
        a2[span, :] = act
        u = dot(act, wup_ref[...], NN) + vec(5)
        cdf = 0.5 * (1.0 + lax.erf(u * 0.7071067811865476))
        gate[span, :] = (u * cdf).astype(bf16)
        du[span, :] = (cdf + u * (0.3989422804014327 * jnp.exp(-0.5 * (u * u)))).astype(bf16)
        return carry

    lax.fori_loop(0, 4, middle, 0)

    for q in range(4):
        gather_cot(q).forward()
    for q in range(4):
        gather_cot(q).land_core()
        gather_cot(q).land_far()

    blocks = [Reduce(spot, first_y, refs) for first_y, refs in zip(FIRST_Y, block_refs)]
    homes = [down_hbm.at[p] for p in range(3)] + [up_hbm.at[p] for p in range(3)]
    homes += [out_hbm.at[0]] + [qkv_hbm.at[p] for p in range(3)]
    saves = [pltpu.make_async_copy(blocks[p].whole, homes[p], local_sem.at[p]) for p in range(10)]

    def sum_copy(slot, k, device, ref=v_mp):
        view = ref.at[slot]
        return remote(view, view, v_send.at[k], v_recv.at[k], device)

    def sum_y():
        return remote(acc, v_y, v_send.at[3], v_recv.at[3], ypeer)

    def sums(k):
        if k == 0:
            v_mp[me] = acc[...]
            for j in (1, 2, 3):
                sum_copy(me, j - 1, (dp, me ^ j)).start()
        elif k == 1:
            for j in (1, 2, 3):
                sum_copy(me ^ j, j - 1, (dp, me ^ j)).wait_recv()
                sum_copy(me, j - 1, (dp, me ^ j)).wait_send()
            acc[0:8, :] = v_mp[0, 0:8, :] + v_mp[1, 0:8, :] + v_mp[2, 0:8, :] + v_mp[3, 0:8, :]
            sum_y().start()
        elif k == 2:
            sum_y().wait()
            v_z[zi] = acc[...] + v_y[...]
            for j in (1, 2, 3):
                sum_copy(zi, 3 + j, zpeers[j - 1], v_z).start()
        else:
            for j in (1, 2, 3):
                sum_copy(zi ^ j, 3 + j, zpeers[j - 1], v_z).wait_recv()
                sum_copy(zi, 3 + j, zpeers[j - 1], v_z).wait_send()
            sums_ref[...] = v_z[0] + v_z[1] + v_z[2] + v_z[3]

    sum_in = Scatter(place, rs_out, rs_both, rs_far, own, rs_send, rs_recv)
    sum_out = Scatter(place, ms_out, ms_both, ms_far, m_own, ms_send, ms_recv)
    sum_first = Scatter(place, rs_out, rs_both, rs_far, own, rt_send, rt_recv)

    def finish_block(k):
        block_ref[...] = block_ref[...] + (sum_out.finish() + vec(6))

    def finish_input(k):
        grad = sum_first.finish()
        hat, factor = layer_hat(xp[rows(me), :].astype(f32))
        input_ref[...] = input_ref[...] + layer_back(grad * vec(0), hat, factor)

    others = (sums, finish_block, finish_input)

    def poll(name):
        for p, k in POLLS.get(name, ()):
            if p >= len(blocks):
                others[p - len(blocks)](k)
                continue
            blocks[p].stage(k)
            if k == STAGES - 1:
                saves[p].start()

    def poll_at(prefix, index, count):
        for n in range(count):
            if POLLS.get(f"{prefix}{n}"):
                pl.when(index == n)(lambda n=n: poll(f"{prefix}{n}"))

    def stage_grad(p, piece):
        quarter = QUARTER[p]
        for h in range(2):
            for c in range(4):
                part = piece[c * quarter : (c + 1) * quarter, h * 384 : (h + 1) * 384]
                blocks[p].part[h, c] = part.astype(bf16)

    for t in range(3):
        stage_grad(t, dot(gate[:, t * B : (t + 1) * B], cot_all[...], TN))
        poll(f"down{t}")

    def hidden_back(i, carry):
        span = rows(me ^ (3 - i))
        grad_u = (dot(cot_all[span, :], wdn_ref[...], NT) * du[span, :].astype(f32)).astype(bf16)
        du[span, :] = grad_u
        acc[8:9, :] += column_sum(grad_u.astype(f32))
        own[...] = dot(grad_u, wup_ref[...], NT)
        sum_in.step(i, lambda: own[...])
        poll_at("mid", i, 4)
        return carry

    lax.fori_loop(0, 4, hidden_back, 0)

    for t in range(3):
        stage_grad(3 + t, dot(a2[:, t * B : (t + 1) * B], du[...], TN))
        poll(f"up{t}")
    poll("up2b")

    def project_down(i, carry):
        s = me ^ (3 - i)
        m_own[...] = dot(gate[rows(s), :], wdn_ref[...], NN)
        sum_out.step(i, lambda: m_own[...], hold=True)
        poll_at("mlp", i, 4)
        return carry

    lax.fori_loop(0, 4, project_down, 0)

    poll("rs1")
    grad_act = sum_in.finish()
    hat, factor = layer_hat(block_ref[...])
    acc[2:3, :] = column_sum(grad_act * hat)
    acc[3:4, :] = column_sum(grad_act)
    cot_own = cot_all[rows(me), :].astype(f32)
    grad_h = cot_own + layer_back(grad_act * vec(3), hat, factor)
    input_ref[...] = grad_h
    grad_branch = grad_h.astype(bf16)
    do_all[rows(me), :] = grad_branch
    gather_do = Gather(place, lambda s: do_all.at[rows(s)], lambda k: do_send.at[k], lambda k: do_recv.at[k])
    gather_do.start()
    acc[4:5, :] = column_sum(grad_branch.astype(f32))
    acc[5:6, :] = column_sum(cot_own)

    poll("own")
    sum_out.release()

    dk[...] = jnp.zeros(dk.shape, f32)
    dv[...] = jnp.zeros(dv.shape, f32)

    def back_head(s, h, low, high, qlow, qhigh, ref):
        lanes = pl.ds(pl.multiple_of(h * B + qlow, 128), qhigh - qlow)
        head = pl.ds(pl.multiple_of(h * HD, HD), HD)
        weights = ref[low:high, lanes]
        grad_probs = dot(values[low:high, :], dcz_t[:, lanes], NN)
        grad_scores = weights.astype(f32) * (grad_probs - delta[h, 0:1, qlow:qhigh])
        grad_scores = grad_scores.astype(bf16)
        ref[low:high, lanes] = grad_scores
        return dot(keys_t[head, low:high], grad_scores, NN)

    def back_block(i, carry):
        s = me ^ i
        span = rows(s)

        @pl.when(i == 1)
        def _():
            gather_do.land_core()

        @pl.when(i == 2)
        def _():
            poll("do")
            gather_do.forward()

        @pl.when(i == 3)
        def _():
            gather_do.land_far()

        grad_ctx = dot(wo_all[me], do_all[span, :], NT).astype(bf16).astype(f32)
        for h in range(3):
            here = slice(h * HD, (h + 1) * HD)
            scaled = (grad_ctx[here, :] * rinv[s, h, 0:1, :]).astype(bf16)
            delta[h, 0:1, :] = column_sum(scaled.astype(f32) * ctx_t[here, span].astype(f32))
            dcz_t[here, h * B : (h + 1) * B] = scaled
            turned = jnp.concatenate([scaled, jnp.zeros((HD, B), bf16)], axis=0).T.astype(f32)
            wide = jnp.concatenate([turned, turned], axis=1)[:, 0:192]
            if h == 1:
                wide = pltpu.roll(jnp.concatenate([turned, jnp.zeros((B, 128), f32)], axis=1), HD, 1)[:, 0:192]
            dcz[h * B : (h + 1) * B, :] = jnp.where(lane_head == h, wide, 0.0).astype(bf16)

        @pl.when(s != 3)
        def _():
            dv[0:TOP, :] += dot(probs[s], dcz[...], NN)

        @pl.when(s == 3)
        def _():
            dv[...] += dot(probs_last[...], dcz[...], NN)

        def head(h, inner):
            here = pl.ds(pl.multiple_of(h * HD, HD), HD)

            @pl.when(s != 3)
            def _():
                stage[here, 0:B] = back_head(s, h, 0, TOP, 0, B, probs.at[s])

            @pl.when(s == 3)
            def _():
                stage[here, 0:128] = back_head(s, h, 0, 1024, 0, 128, probs_last)
                stage[here, 128:256] = back_head(s, h, 768, 1024, 128, 256, probs_last)

            poll_at("attend", i * 3 + h, 12)
            return inner

        lax.fori_loop(0, 3, head, 0)

        @pl.when(s != 3)
        def _():
            dk[0:TOP, :] += dot(probs[s], qz[s], NN)

        @pl.when(s == 3)
        def _():
            dk[...] += dot(probs_last[...], qz[s], NN)

        dq[span, :] = (stage[0:192, 0:B] * HD**-0.5).T.astype(bf16)
        return carry

    dcz_t[...] = jnp.zeros(dcz_t.shape, bf16)
    lax.fori_loop(0, 4, back_block, 0)

    stage_grad(6, dot(ctx_t[...], do_all[...], NN))
    poll("out")
    dkb[...] = dk[...].astype(bf16)
    dvb[...] = dv[...].astype(bf16)
    for t, ref in enumerate((dq, dkb, dvb)):
        stage_grad(7 + t, dot(ref[...], a1[...], TN))
        poll(f"qkv{t}")
    acc[9:10, 0:192] = column_sum(dq[...].astype(f32))
    acc[9:10, 256:448] = column_sum(dvb[...].astype(f32))

    def project_back(i, carry):
        s = me ^ (3 - i)
        span = rows(s)
        grad = dot(dq[span, :], wqkv_ref[0], NN)
        grad = grad + dot(dkb[span, :], wqkv_ref[1], NN)
        grad = grad + dot(dvb[span, :], wqkv_ref[2], NN)
        hat, _ = layer_hat(xp[span, :].astype(f32))
        acc[0:1, :] += column_sum(grad * hat)
        acc[1:2, :] += column_sum(grad)
        own[...] = grad
        sum_first.step(i, lambda: own[...])
        poll_at("first", i, 4)
        return carry

    lax.fori_loop(0, 4, project_back, 0)

    poll("tail")

    for gather in [gather_wo, gather_do] + [make(s) for s in range(4) for make in (gather_ctx, gather_cot)]:
        gather.close()
    for block in blocks:
        block.close()
    for save in saves:
        save.wait()


def finish_kernel(
    block_hbm, input_hbm, sums_hbm, down_hbm, up_hbm, out_hbm, qkv_hbm,
    block_out, input_grad, gain_first, shift_first, grad_qkv, grad_qv, grad_out, out_bias, gain_second, shift_second,
    grad_up, up_bias, grad_down, down_bias,
    block_v, input_v, sums, down_v, up_v, out_v, qkv_v, block_w, input_w, down_w, up_w, out_w, qkv_w,
    in_sem, out_sem,
):
    share = block_out.shape[0]
    pairs = (
        (down_hbm, down_v), (up_hbm, up_v), (qkv_hbm, qkv_v), (block_hbm, block_v), (input_hbm, input_v),
        (out_hbm, out_v), (sums_hbm, sums),
    )
    loads = [pltpu.make_async_copy(src, dst, in_sem.at[k]) for k, (src, dst) in enumerate(pairs)]
    for load in loads:
        load.start()
    stores = []

    def save(src, dst):
        stores.append(pltpu.make_async_copy(src, dst, out_sem.at[len(stores)]))
        stores[-1].start()

    def widen(source, p, put):
        quarter = source.shape[3]
        for h in range(2):
            for c in range(4):
                put(slice(c * quarter, (c + 1) * quarter), slice(h * 384, (h + 1) * 384), source[p, h, c].astype(f32))

    for k, (source, wide, target) in enumerate(((down_v, down_w, grad_down), (up_v, up_w, grad_up))):
        loads[k].wait()
        for p in range(3):

            def put(r, lanes, value):
                wide[p * B + r.start : p * B + r.stop, lanes] = value

            widen(source, p, put)
        save(wide, target)
    loads[2].wait()
    for p in range(3):

        def put(r, lanes, value):
            qkv_w[p, r, lanes] = value

        widen(qkv_v, p, put)
    save(qkv_w, grad_qkv)
    for k, source, wide, target in ((3, block_v, block_w, block_out), (4, input_v, input_w, input_grad)):
        loads[k].wait()
        wide[...] = source[0:share, :]
        save(wide, target)
    loads[5].wait()

    def put(r, lanes, value):
        out_w[r, lanes] = value

    widen(out_v, 0, put)
    save(out_w, grad_out)
    loads[6].wait()
    for r, ref in enumerate((gain_first, shift_first, gain_second, shift_second, out_bias, down_bias)):
        ref[...] = sums[r, :]
    up_bias[...] = sums[8, :]
    grad_qv[0:1, :] = sums[9:10, 0:192]
    grad_qv[1:2, :] = sums[9:10, 256:448]
    for store in stores:
        store.wait()


def per_device(
    inputs, image_of_row, gain_first, shift_first, qkv_weight, qv_bias, out_weight, out_bias, gain_second,
    shift_second, up_weight, up_bias, down_weight, down_bias, cotangent,
):
    share = cotangent.shape[0]
    vmem, smem, anyspace = (pl.BlockSpec(memory_space=m) for m in (pltpu.VMEM, pltpu.SMEM, pl.ANY))

    def shape(*dims, dtype=bf16):
        return pltpu.VMEM(dims, dtype)

    dma = pltpu.SemaphoreType.DMA

    def block_scratch(first_y, r):
        over = shape(4, r, 384) if first_y else shape(r, 384)
        along = shape(3, r, 384) if first_y else shape(2, 3, r, 384)
        return [shape(2, 4, r, 384), over, along, along, shape(2, 4, r, 384), dma((13,)), dma((13,))]

    scratch = [
        shape(1024, 768), shape(272, 768, dtype=f32), shape(1024, 768),
        shape(1024, 192), shape(1024, 192), shape(192, 1024), shape(192, 1024),
        shape(4, 192, 768), shape(4, 768, 192),
        shape(1024, B, dtype=i32), shape(4, 8, B, dtype=i32),
        shape(3, TOP, 768), shape(1024, 768), shape(4, 3, 8, B, dtype=f32),
        shape(192, 1024), shape(4, 4, 384, 128), shape(4, 192, 768), shape(1024, 768),
        shape(1024, 768), shape(1024, 768), shape(1024, 768), shape(1024, 768),
        shape(192, 768), shape(768, 192), shape(3, 8, B, dtype=f32),
        shape(1024, 192), shape(1024, 192, dtype=f32), shape(1024, 192, dtype=f32),
        shape(1024, 192), shape(1024, 192), shape(B, 768, dtype=f32),
        shape(3, B, 768), shape(2, B, 768), shape(B, 768),
        shape(3, B, 768), shape(2, B, 768), shape(B, 768), shape(B, 768, dtype=f32),
        shape(8, 768, dtype=f32),
        shape(16, 768, dtype=f32), shape(4, 16, 768, dtype=f32), shape(16, 768, dtype=f32), shape(4, 16, 768, dtype=f32),
    ]
    scratch += [dma((3,))] * 2 + [dma((4, 3))] * 4 + [dma((3,))] * 8 + [dma((7,))] * 2 + [dma((10,)), dma((14,))]
    scratch += [shape(4 * share, 768), shape(3, 192, 768), shape(768, 768), shape(768, 768), shape(share, 768)]
    scratch += [[shape(768)] * 7, shape(2, 192)]
    scratch += [[block_scratch(first_y, r) for first_y, r in zip(FIRST_Y, QUARTER)]]
    results = pl.pallas_call(
        layer_kernel,
        out_shape=[
            jax.ShapeDtypeStruct((B, 768), f32),
            jax.ShapeDtypeStruct((B, 768), f32),
            jax.ShapeDtypeStruct((16, 768), f32),
            jax.ShapeDtypeStruct((3, 2, 4, 64, 384), bf16),
            jax.ShapeDtypeStruct((3, 2, 4, 64, 384), bf16),
            jax.ShapeDtypeStruct((1, 2, 4, 48, 384), bf16),
            jax.ShapeDtypeStruct((3, 2, 4, 48, 384), bf16),
        ],
        in_specs=[anyspace, smem] + [anyspace] * 13,
        out_specs=[vmem] * 3 + [anyspace] * 4,
        scratch_shapes=scratch,
        compiler_params=pltpu.CompilerParams(
            collective_id=0, has_side_effects=True, vmem_limit_bytes=60 * 2**20
        ),
        name="layer",
    )(
        inputs, image_of_row, gain_first, shift_first, qv_bias, out_bias, gain_second, shift_second, up_bias, down_bias,
        jnp.swapaxes(qkv_weight, 1, 2), out_weight, up_weight, down_weight, cotangent,
    )

    def out(*dims):
        return jax.ShapeDtypeStruct(dims, f32)

    wide = [shape(share, 768, dtype=f32)] * 2 + [shape(768, 768, dtype=f32)] * 2
    outputs = pl.pallas_call(
        finish_kernel,
        out_shape=[
            out(share, 768), out(share, 768), out(768), out(768), out(3, 192, 768), out(2, 192), out(192, 768),
            out(768), out(768), out(768), out(768, 768), out(768), out(768, 768), out(768),
        ],
        in_specs=[anyspace] * 7,
        out_specs=[anyspace if k in (0, 1, 4, 6, 10, 12) else vmem for k in range(14)],
        scratch_shapes=[pltpu.VMEM(r.shape, r.dtype) for r in results]
        + wide + [shape(192, 768, dtype=f32), shape(3, 192, 768, dtype=f32), dma((7,)), dma((6,))],
        compiler_params=pltpu.CompilerParams(vmem_limit_bytes=60 * 2**20),
        name="finish",
    )(*results)
    return (*outputs[:4], jnp.swapaxes(outputs[4], 1, 2), *outputs[5:])


def solution(mesh):
    return jax.shard_map(
        per_device,
        mesh=mesh,
        in_specs=(
            P("dp", None),
            P("dp"),
            P(),
            P(),
            P(None, None, "mp"),
            P(None, "mp"),
            P("mp", None),
            P(),
            P(),
            P(),
            P(None, "mp"),
            P("mp"),
            P("mp", None),
            P(),
            P(("dp", "mp"), None),
        ),
        out_specs=(
            P(("dp", "mp"), None),
            P(("dp", "mp"), None),
            P(),
            P(),
            P(None, None, "mp"),
            P(None, "mp"),
            P("mp", None),
            P(),
            P(),
            P(),
            P(None, "mp"),
            P("mp"),
            P("mp", None),
            P(),
        ),
        check_vma=False,
    )
```

```python
import functools

import jax
import jax.numpy as jnp
from jax import lax
from jax.experimental import pallas as pl
from jax.experimental.pallas import tpu as pltpu
from jax.sharding import PartitionSpec as P

f32, bf16, i32 = jnp.float32, jnp.bfloat16, jnp.int32
MESH = pl.DeviceIdType.MESH
NN = (((1,), (0,)), ((), ()))
NT = (((1,), (1,)), ((), ()))
TN = (((0,), (0,)), ((), ()))
HD = 64
P_LO = 196
EPSILON = 1e-06
B = 256
TOP = 832
BIG = 4 * P_LO


def dot(left, right, dims):
    return lax.dot_general(left, right, dims, preferred_element_type=f32)


def rows(start, size=B):
    return pl.ds(pl.multiple_of(start * size, size), size)


def layer_hat(values):
    center = values - jnp.mean(values, axis=1, keepdims=True)
    factor = lax.rsqrt(jnp.mean(center * center, axis=1, keepdims=True) + EPSILON)
    return center * factor, factor


def layer_back(grad_hat, normed, factor):
    first = jnp.mean(grad_hat, axis=1, keepdims=True)
    second = jnp.mean(grad_hat * normed, axis=1, keepdims=True)
    return factor * (grad_hat - first - normed * second)


def column_sum(values):
    return jnp.sum(values, axis=0, keepdims=True)


def remote(src, dst, send, recv, device):
    return pltpu.make_async_remote_copy(
        src_ref=src, dst_ref=dst, send_sem=send, recv_sem=recv, device_id=device, device_id_type=MESH
    )


class Gather:
    def __init__(self, place, view, send, recv):
        self.me, self.core, self.across = place
        self.view, self.send, self.recv = view, send, recv

    def copy(self, slot, k, device, part=None):
        view = self.view(slot) if part is None else self.view(slot).at[part]
        return remote(view, view, self.send, self.recv(k), device)

    def start(self):
        self.copy(self.me, 1, self.across).start()
        self.copy(self.me, 0, self.core).start()

    def forward(self):
        slot = self.me ^ 2
        self.copy(slot, 1, self.across).wait_recv()
        self.copy(slot, 2, self.core).start()

    def land_core(self):
        self.copy(self.me ^ 1, 0, self.core).wait_recv()

    def land_far(self):
        self.copy(self.me ^ 3, 2, self.core).wait_recv()


class Scatter:
    def __init__(self, place, out, both, far, own, send, recv):
        self.me, self.core, self.across = place
        self.out, self.both, self.far, self.own = out, both, far, own
        self.send, self.recv = send, recv

    def copy(self, k):
        src = self.out.at[k]
        dst = self.far if k == 1 else self.both.at[k // 2]
        return remote(src, dst, self.send, self.recv.at[k], self.across if k == 1 else self.core)

    def step(self, i, value, hold=False):
        @pl.when(i == 0)
        def _():
            self.out[0] = value().astype(bf16)
            self.copy(0).start()

        @pl.when(i == 1)
        def _():
            if hold:
                self.out[1] = value().astype(bf16)
            else:
                self.copy(0).wait_recv()
                self.out[1] = (value() + self.both[0].astype(f32)).astype(bf16)
                self.copy(1).start()

        @pl.when(i == 2)
        def _():
            self.out[2] = value().astype(bf16)
            self.copy(2).start()

        @pl.when(i == 3)
        def _():
            self.own[...] = value()

    def release(self):
        self.copy(0).wait_recv()
        self.out[1] = (self.out[1].astype(f32) + self.both[0].astype(f32)).astype(bf16)
        self.copy(1).start()

    def finish(self):
        self.copy(2).wait_recv()
        self.copy(1).wait_recv()
        total = self.own[...] + self.both[1].astype(f32) + self.far[...].astype(f32)
        remote(self.out, self.out, self.send, self.recv.at[0], self.core).wait_send()
        return total


class Reduce:
    def __init__(self, spot, first_y, refs):
        self.zi, self.yi, self.over, self.above, self.below = spot
        self.first_y = first_y
        self.part, self.ybuf, self.up, self.down, self.whole, self.send, self.recv = refs

    def copy(self, src, dst, k, slot, device):
        return remote(src, dst, self.send.at[k], self.recv.at[slot], device)

    def begin(self, condition, make):
        if condition is None:
            make().start()
        else:
            pl.when(condition())(lambda: make().start())

    def close(self):
        all_along = self.whole.at[self.yi] if self.first_y else self.whole
        all_over = self.whole if self.first_y else self.whole.at[:, 0]
        pl.when(self.zi < 3)(lambda: self.copy(all_along, all_along, 1, 1, self.above).wait_send())
        pl.when(self.zi > 0)(lambda: self.copy(all_along, all_along, 2, 2, self.below).wait_send())
        self.copy(all_over, all_over, 0, 0, self.over).wait_send()

    def chunks(self, first, count):
        return self.part.at[self.yi if self.first_y else slice(None), pl.ds(first, count)]

    def rising(self, first, count):
        span = pl.ds(first - 1, count)
        return self.up.at[span] if self.first_y else self.up.at[:, span]

    def falling(self, first, count):
        span = pl.ds(first, count)
        return self.down.at[span] if self.first_y else self.down.at[:, span]

    def result(self, chunk):
        return self.whole.at[self.yi if self.first_y else slice(None), chunk]

    def copy_up(self, first, count, src):
        return self.copy(src, self.rising(first, count), 1, 1, self.above)

    def copy_down(self, first, count, src):
        return self.copy(src, self.falling(first, count), 2, 2, self.below)

    def at(self, z):
        return lambda: self.zi == z

    def hop(self, n):
        up_first, down_count = n, 4 - n

        def up_view():
            return self.chunks(n, 4 - n) if n == 1 else self.rising(n, 4 - n)

        def down_view():
            return self.chunks(0, 4 - n) if n == 1 else self.falling(0, 4 - n)

        if n > 1:

            @pl.when(self.zi == n - 1)
            def _():
                came = self.rising(n - 1, 5 - n)
                self.copy_up(n - 1, 5 - n, came).wait_recv()
                view, own = self.rising(n, 4 - n), self.chunks(n, 4 - n)
                view[...] = (view[...].astype(f32) + own[...].astype(f32)).astype(bf16)

            @pl.when(self.zi == 4 - n)
            def _():
                came = self.falling(0, 5 - n)
                self.copy_down(0, 5 - n, came).wait_recv()
                view, own = self.falling(0, 4 - n), self.chunks(0, 4 - n)
                view[...] = (view[...].astype(f32) + own[...].astype(f32)).astype(bf16)

        self.begin(self.at(n - 1), lambda: self.copy_up(up_first, 4 - n, up_view()))
        self.begin(self.at(4 - n), lambda: self.copy_down(0, down_count, down_view()))

    def total(self, store):
        def plain(view):
            return view[...].astype(f32)

        @pl.when(self.zi == 0)
        def _():
            self.copy_down(0, 1, self.falling(0, 1)).wait_recv()
            store(0, plain(self.chunks(0, 1)) + plain(self.falling(0, 1)))

        @pl.when(self.zi == 3)
        def _():
            self.copy_up(3, 1, self.rising(3, 1)).wait_recv()
            store(3, plain(self.chunks(3, 1)) + plain(self.rising(3, 1)))

        for z in (1, 2):

            @pl.when(self.zi == z)
            def _(z=z):
                value = plain(self.chunks(z, 1)) + plain(self.rising(z, 1)) + plain(self.falling(z, 1))
                store(z, value)

    def back(self, d):
        for sign, k, ahead, room in ((-1, 1, self.above, lambda: self.zi < 3), (1, 2, self.below, lambda: self.zi > 0)):

            def here(sign=sign):
                return self.zi >= d if sign < 0 else self.zi <= 3 - d

            def move(sign=sign, k=k, ahead=ahead):
                chunk = self.zi + sign * d
                view = self.result(chunk)
                return self.copy(view, view, k, 3 + chunk, ahead)

            if d > 0:

                @pl.when(here())
                def _():
                    move().wait_recv()

            if d < 3:
                self.begin(lambda room=room, here=here: room() & here(), move)
            if self.first_y and (d > 0 or sign < 0):
                self.begin(here, lambda sign=sign: self.copy_over(self.yi, self.zi + sign * d))

    def copy_over(self, half, chunk):
        view = self.whole.at[half, chunk]
        return self.copy(view, view, 0, 7, self.over)

    def sum_over(self):
        if self.first_y:
            return self.copy(self.part.at[1 - self.yi], self.ybuf, 0, 0, self.over)
        return self.copy(self.part.at[1 - self.yi, self.zi], self.ybuf, 0, 0, self.over)

    def stage(self, k):
        if self.first_y:
            if k == 0:
                self.begin(None, self.sum_over)
            elif k == 1:
                self.sum_over().wait_recv()

                def add(c, carry):
                    value = self.part[self.yi, c].astype(f32) + self.ybuf[c].astype(f32)
                    self.part[self.yi, c] = value.astype(bf16)
                    return carry

                lax.fori_loop(0, 4, add, 0)
                self.hop(1)
            elif k in (2, 3):
                self.hop(k)
            elif k == 4:

                def store(z, value):
                    self.whole[self.yi, z] = value[0].astype(bf16)

                self.total(store)
                self.back(0)
            elif k in (5, 6, 7):
                self.back(k - 4)
            else:
                other = self.whole.at[1 - self.yi]
                self.copy(other, other, 0, 7, self.over).wait_recv()
        else:
            if k in (0, 1, 2):
                self.hop(k + 1)
            elif k == 3:

                def store(z, value):
                    self.part[:, z] = value[:, 0].astype(bf16)

                self.total(store)
                self.begin(None, self.sum_over)
            elif k == 4:
                self.sum_over().wait_recv()
                value = self.part[self.yi, self.zi].astype(f32) + self.ybuf[...].astype(f32)
                self.whole[self.yi, self.zi] = value.astype(bf16)
                self.begin(None, lambda: self.copy_over(self.yi, self.zi))
            elif k == 5:
                self.copy_over(1 - self.yi, self.zi).wait_recv()
                self.back(0)
            else:
                self.back(k - 5)


FIRST_Y = (False, True, True, True, True, True, True, True, True, True)
QUARTER = (64,) * 6 + (48,) * 4
STAGES = 9

POLLS = {
    "down0": ((0, 0),),
    "down1": ((1, 0),),
    "down2": ((2, 0),),
    "up0": ((3, 0), (1, 1),),
    "up1": ((4, 0),),
    "up2": ((0, 1), (5, 0),),
    "rs1": ((2, 1), (1, 2),),
    "own": ((0, 2), (3, 1),),
    "attend0": ((1, 3), (2, 2),),
    "attend3": ((0, 3), (1, 4),),
    "attend4": ((2, 3), (3, 2),),
    "attend5": ((4, 1),),
    "do": ((5, 1), (1, 5), (0, 4),),
    "attend6": ((2, 4), (3, 3),),
    "attend8": ((1, 6), (4, 2),),
    "attend9": ((0, 5), (3, 4),),
    "attend10": ((1, 7), (5, 2),),
    "attend11": ((2, 5), (4, 3),),
    "out": ((6, 0),),
    "qkv0": ((7, 0),),
    "qkv1": ((0, 6), (1, 8),),
    "qkv2": ((8, 0), (9, 0),),
    "first0": ((3, 5),),
    "first2": ((4, 4), (5, 3),),
    "first3": ((2, 6),),
    "tail": ((10, 0), (11, 0), (6, 1), (0, 7), (3, 6), (4, 5), (5, 4), (7, 1), (2, 7), (6, 2), (0, 8), (8, 1), (3, 7), (12, 0), (4, 6), (6, 3), (7, 2), (10, 1), (5, 5), (9, 1), (8, 2), (4, 7), (6, 4), (7, 3), (9, 2), (5, 6), (7, 4), (8, 3), (2, 8), (6, 5), (5, 7), (3, 8), (9, 3), (8, 4), (7, 5), (6, 6), (10, 2), (9, 4), (4, 8), (8, 5), (7, 6), (6, 7), (5, 8), (10, 3), (9, 5), (7, 7), (8, 6), (6, 8), (9, 6), (8, 7), (7, 8), (9, 7), (8, 8), (9, 8),),
}


def layer_kernel(
    x_hbm, ids_hbm, gain_a, shift_a, bias_qv, bias_out, gain_b, shift_b, bias_up, bias_down,
    wqkv_hbm, wo_hbm, wup_hbm, wdn_hbm, cot_hbm,
    block_hbm, input_hbm, sums_hbm, down_hbm, up_hbm, out_hbm, qkv_hbm,
    xp, stage, a1, keys, values, keys_t, values_t, qz_t, qz, kid, qid, probs, probs_last, rinv, ctx_t, ctx_all,
    wo_all, cot_all, a2, gate, du, do_all, dcz_t, dcz, delta, dq, dk, dv, dkb, dvb, own,
    rs_out, rs_both, rs_far, ms_out, ms_both, ms_far, m_own,
    vec_ref, acc, v_mp, v_y, v_z,
    wo_send, wo_recv, cot_send, cot_recv, ctx_send, ctx_recv, do_send, do_recv,
    rs_send, rs_recv, ms_send, ms_recv, rt_send, rt_recv,
    v_send, v_recv, local_sem, load_sem, x_ref, wqkv_ref, wup_ref, wdn_ref, cot_ref, vec_raw, qv_raw,
    block_ref, input_ref, sums_ref, ids_ref, block_refs,
):
    dp, me = lax.axis_index("dp"), lax.axis_index("mp")
    core, across, diagonal = (dp, me ^ 1), (dp, me ^ 2), (dp, me ^ 3)
    yi, zi = dp & 1, (dp >> 1) & 3
    ypeer = (dp ^ 1, me)
    zpeers = [(dp ^ (2 * j), me) for j in (1, 2, 3)]
    place = (me, core, across)
    base = dp & ~7
    above, below = (base + (((zi + 1) & 3) << 1) + yi, me), (base + (((zi + 3) & 3) << 1) + yi, me)
    spot = (zi, yi, ypeer, above, below)
    share = cot_hbm.shape[0]

    barrier = pltpu.get_barrier_semaphore()
    partners = [core, across, diagonal, ypeer] + zpeers
    for partner in partners:
        pl.semaphore_signal(barrier, inc=1, device_id=partner, device_id_type=MESH)

    def vec(r, width=None):
        return vec_ref[r : r + 1, :] if width is None else vec_ref[r : r + 1, width[0] : width[1]]

    pairs = [(wo_hbm, wo_all.at[me]), (cot_hbm, cot_ref), (x_hbm, x_ref), (bias_qv, qv_raw)]
    pairs += list(zip((gain_a, shift_a, bias_out, gain_b, shift_b, bias_up, bias_down), vec_raw))
    pairs += [(wqkv_hbm, wqkv_ref), (wup_hbm, wup_ref), (wdn_hbm, wdn_ref), (ids_hbm, ids_ref)]
    loads = [pltpu.make_async_copy(src, dst, load_sem.at[k]) for k, (src, dst) in enumerate(pairs)]
    for load in loads:
        load.start()
    pl.semaphore_wait(barrier, len(partners))

    gather_wo = Gather(place, lambda s: wo_all.at[s], wo_send.at[0], lambda k: wo_recv.at[k])
    loads[0].wait()
    gather_wo.start()

    gather_cot = Gather(place, lambda s: cot_all.at[rows(s)], cot_send.at[0], lambda k: cot_recv.at[k])

    loads[1].wait()
    stage[240:256, :] = jnp.zeros((16, 768), f32)
    stage[0:share, :] = cot_ref[...].astype(f32)
    cot_all[rows(me), :] = stage[0:B, :].astype(bf16)
    gather_cot.copy(me, 1, across, pl.ds(0, 64)).start()
    gather_cot.copy(me, 0, core).start()
    acc[...] = jnp.zeros(acc.shape, f32)
    for k in range(3, 11):
        loads[k].wait()
    for r, ref in enumerate(vec_raw):
        vec_ref[r : r + 1, :] = ref[...].astype(f32).reshape(1, 768)
    vec_ref[7:8, 0:192] = qv_raw[0:1, :].astype(f32)
    vec_ref[7:8, 256:448] = qv_raw[1:2, :].astype(f32)
    loads[2].wait()

    row_in = lax.broadcasted_iota(i32, (B, 768), 0)
    for s in range(4):
        first = s * share // 16 * 16
        last = min(first + 272, 4 * share)
        stage[0 : last - first, :] = x_ref[first:last, :].astype(f32)
        moved = stage[s * share - first : s * share - first + B, :]
        xp[s * B : (s + 1) * B, :] = jnp.where(row_in < share, moved, 0.0).astype(bf16)

    loads[14].wait()
    two_images = (ids_ref[0] == ids_ref[BIG - 1]).astype(i32)

    def image_of(index, shard, pad):
        place_of = index + shard * share
        small = jnp.zeros_like(index)
        for k in range(1, 5):
            small = small + (place_of >= k * P_LO).astype(i32)
        large = (place_of >= BIG).astype(i32)
        image = small * (1 - two_images) + large * two_images
        return jnp.where(index < share, image, pad)

    def images(s, carry):
        kid[rows(s), :] = image_of(lax.broadcasted_iota(i32, (B, B), 0), s, -1)
        qid[s] = image_of(lax.broadcasted_iota(i32, (8, B), 1), s, -2)
        qz_t[s] = jnp.zeros(qz_t.shape[1:], bf16)
        return carry

    lax.fori_loop(0, 4, images, 0)

    lane_head = lax.broadcasted_iota(i32, (B, 192), 1) // HD

    def project(s, carry):
        span = rows(s)
        hat, _ = layer_hat(xp[span, :].astype(f32))
        act = (hat * vec(0) + vec(1)).astype(bf16)
        a1[span, :] = act
        q = (dot(act, wqkv_ref[0], NT) + vec(7, (0, 192))).astype(bf16)
        k = dot(act, wqkv_ref[1], NT).astype(bf16)
        v = (dot(act, wqkv_ref[2], NT) + vec(7, (256, 448))).astype(bf16)
        keys[span, :] = k
        values[span, :] = v
        keys_t[:, span] = k.T
        values_t[:, span] = v.T
        q = q.astype(f32) * HD**-0.5
        qt = q.astype(bf16).T
        for h in range(3):
            qz_t[s, h * HD : (h + 1) * HD, h * B : (h + 1) * B] = qt[h * HD : (h + 1) * HD, :]
            qz[s, h * B : (h + 1) * B, :] = jnp.where(lane_head == h, q, 0.0).astype(bf16)
        return carry

    loads[11].wait()
    lax.fori_loop(0, 4, project, 0)

    def gather_ctx(s):
        return Gather(
            place, lambda j: ctx_all.at[j, s], ctx_send.at[0], lambda k: ctx_recv.at[s, k]
        )

    def attend(s, h, low, high, qlow, qhigh, store):
        lanes = pl.ds(pl.multiple_of(h * B + qlow, 128), qhigh - qlow)
        scores = dot(keys[low:high, :], qz_t[s, :, lanes], NN)
        same = kid[low:high, qlow:qhigh] == qid[s, 0:1, qlow:qhigh]
        scores = jnp.where(same, scores, -1e30)
        top = jnp.max(scores, axis=0, keepdims=True)
        weights = jnp.exp(scores - top)
        inverse = 1.0 / jnp.sum(weights, axis=0, keepdims=True)
        weights = weights.astype(bf16)
        store(lanes, weights)
        rinv[s, h, 0:1, qlow:qhigh] = inverse
        head = pl.ds(pl.multiple_of(h * HD, HD), HD)
        return (dot(values_t[head, low:high], weights, NN) * inverse).astype(bf16)

    def send_ctx(s):
        span = rows(s)
        block = ctx_t[:, span]
        ctx_all[me, s, 0:B, :] = block[0:128, :].T
        last = jnp.concatenate([block[128:192, 0:128], block[128:192, 128:256]], axis=0)
        ctx_all[me, s, B : B + 128, :] = last.T
        gather_ctx(s).start()

    def attend_top(s, carry):
        def head(h, inner):
            def store(lanes, weights):
                probs[s, :, lanes] = weights

            here = pl.ds(pl.multiple_of(h * HD, HD), HD)
            ctx_t[here, rows(s)] = attend(s, h, 0, TOP, 0, B, store)
            return inner

        lax.fori_loop(0, 3, head, 0)
        send_ctx(s)

        @pl.when(s == 1)
        def _():
            gather_wo.forward()

        return carry

    lax.fori_loop(0, 3, attend_top, 0)

    def attend_last(h, carry):
        here = pl.ds(pl.multiple_of(h * HD, HD), HD)

        def store_left(lanes, weights):
            probs_last[:, lanes] = weights

        def store_right(lanes, weights):
            probs_last[0:768, lanes] = jnp.zeros((768, 128), bf16)
            probs_last[768:1024, lanes] = weights

        ctx_t[here, 768:896] = attend(3, h, 0, 1024, 0, 128, store_left)
        ctx_t[here, 896:1024] = attend(3, h, 768, 1024, 128, 256, store_right)
        return carry

    lax.fori_loop(0, 3, attend_last, 0)
    send_ctx(3)

    for q in (1, 2, 3):
        gather_cot.copy(me, 1, across, pl.ds(q * 64, 64)).start()
    gather_wo.land_core()
    gather_wo.land_far()
    for s in range(4):
        gather_ctx(s).forward()
    loads[12].wait()
    loads[13].wait()

    zeros_w = jnp.zeros((HD, 768), bf16)

    def middle(i, carry):
        s = me ^ (3 - i)
        span = rows(s)
        ctx = gather_ctx(s)
        ctx.land_core()
        ctx.land_far()
        left = jnp.concatenate([ctx_all[j, s, 0:B, :] for j in range(4)], axis=1)
        last = jnp.concatenate([ctx_all[j, s, B : B + 128, :] for j in range(4)], axis=1)
        w_left = jnp.concatenate([wo_all[j, 0:128, :] for j in range(4)], axis=0)
        w_tail = [wo_all[j, 128:192, :] for j in range(4)]
        w_upper = jnp.concatenate([piece for w in w_tail for piece in (w, zeros_w)], axis=0)
        w_lower = jnp.concatenate([piece for w in w_tail for piece in (zeros_w, w)], axis=0)
        branch = dot(left, w_left, NN) + jnp.concatenate(
            [dot(last, w_upper, NN), dot(last, w_lower, NN)], axis=0
        )
        h = xp[span, :].astype(f32) + (branch + vec(2))

        @pl.when(i == 3)
        def _():
            block_ref[...] = h

        hat, _ = layer_hat(h)
        act = (hat * vec(3) + vec(4)).astype(bf16)
        a2[span, :] = act
        u = dot(act, wup_ref[...], NN) + vec(5)
        cdf = 0.5 * (1.0 + lax.erf(u * 0.7071067811865476))
        gate[span, :] = (u * cdf).astype(bf16)
        du[span, :] = (cdf + u * (0.3989422804014327 * jnp.exp(-0.5 * (u * u)))).astype(bf16)
        return carry

    lax.fori_loop(0, 4, middle, 0)

    gather_cot.forward()
    gather_cot.land_core()
    gather_cot.land_far()

    blocks = [Reduce(spot, first_y, refs) for first_y, refs in zip(FIRST_Y, block_refs)]
    homes = [down_hbm.at[p] for p in range(3)] + [up_hbm.at[p] for p in range(3)]
    homes += [out_hbm.at[0]] + [qkv_hbm.at[p] for p in range(3)]
    tensor = (0, 0, 0, 1, 1, 1, 2, 3, 3, 3)
    saves = [pltpu.make_async_copy(blocks[p].whole, homes[p], local_sem.at[tensor[p]]) for p in range(10)]
    save_block = pltpu.make_async_copy(block_ref, block_hbm, local_sem.at[4])
    save_input = pltpu.make_async_copy(input_ref, input_hbm, local_sem.at[5])
    save_sums = pltpu.make_async_copy(sums_ref, sums_hbm, local_sem.at[6])

    def sum_copy(slot, k, device, ref=v_mp):
        view = ref.at[slot]
        return remote(view, view, v_send.at[0 if k < 3 else 2], v_recv.at[k], device)

    def sum_y():
        return remote(acc, v_y, v_send.at[1], v_recv.at[3], ypeer)

    def sums(k):
        if k == 0:
            v_mp[me] = acc[...]
            for j in (1, 2, 3):
                sum_copy(me, j - 1, (dp, me ^ j)).start()
        elif k == 1:
            for j in (1, 2, 3):
                sum_copy(me ^ j, j - 1, (dp, me ^ j)).wait_recv()
            acc[0:8, :] = v_mp[0, 0:8, :] + v_mp[1, 0:8, :] + v_mp[2, 0:8, :] + v_mp[3, 0:8, :]
            sum_y().start()
        elif k == 2:
            sum_y().wait()
            v_z[zi] = acc[...] + v_y[...]
            for j in (1, 2, 3):
                sum_copy(zi, 3 + j, zpeers[j - 1], v_z).start()
        else:
            for j in (1, 2, 3):
                sum_copy(zi ^ j, 3 + j, zpeers[j - 1], v_z).wait_recv()
            sums_ref[...] = v_z[0] + v_z[1] + v_z[2] + v_z[3]
            save_sums.start()
            sum_copy(slice(0, 3), 0, core).wait_send()
            sum_copy(slice(0, 3), 4, core, v_z).wait_send()

    sum_in = Scatter(place, rs_out, rs_both, rs_far, own, rs_send.at[0], rs_recv)
    sum_out = Scatter(place, ms_out, ms_both, ms_far, m_own, ms_send.at[0], ms_recv)
    sum_first = Scatter(place, rs_out, rs_both, rs_far, own, rt_send.at[0], rt_recv)

    def finish_block(k):
        block_ref[...] = block_ref[...] + (sum_out.finish() + vec(6))
        save_block.start()

    def finish_input(k):
        grad = sum_first.finish()
        hat, factor = layer_hat(xp[rows(me), :].astype(f32))
        input_ref[...] = input_ref[...] + layer_back(grad * vec(0), hat, factor)
        save_input.start()

    others = (sums, finish_block, finish_input)

    def poll(name):
        for p, k in POLLS.get(name, ()):
            if p >= len(blocks):
                others[p - len(blocks)](k)
                continue
            blocks[p].stage(k)
            if k == STAGES - 1:
                saves[p].start()

    def poll_at(prefix, index, count):
        for n in range(count):
            if POLLS.get(f"{prefix}{n}"):
                pl.when(index == n)(lambda n=n: poll(f"{prefix}{n}"))

    def stage_grad(p, piece):
        quarter = QUARTER[p]
        for h in range(2):
            for c in range(4):
                part = piece[c * quarter : (c + 1) * quarter, h * 384 : (h + 1) * 384]
                blocks[p].part[h, c] = part.astype(bf16)

    for t in range(3):
        stage_grad(t, dot(gate[:, t * B : (t + 1) * B], cot_all[...], TN))
        poll(f"down{t}")

    def hidden_back(i, carry):
        span = rows(me ^ (3 - i))
        grad_u = (dot(cot_all[span, :], wdn_ref[...], NT) * du[span, :].astype(f32)).astype(bf16)
        du[span, :] = grad_u
        acc[8:9, :] += column_sum(grad_u.astype(f32))
        own[...] = dot(grad_u, wup_ref[...], NT)
        sum_in.step(i, lambda: own[...])
        poll_at("mid", i, 4)
        return carry

    lax.fori_loop(0, 4, hidden_back, 0)

    for t in range(3):
        stage_grad(3 + t, dot(a2[:, t * B : (t + 1) * B], du[...], TN))
        poll(f"up{t}")
    poll("up2b")

    def project_down(i, carry):
        s = me ^ (3 - i)
        m_own[...] = dot(gate[rows(s), :], wdn_ref[...], NN)
        sum_out.step(i, lambda: m_own[...], hold=True)
        poll_at("mlp", i, 4)
        return carry

    lax.fori_loop(0, 4, project_down, 0)

    poll("rs1")
    grad_act = sum_in.finish()
    hat, factor = layer_hat(block_ref[...])
    acc[2:3, :] = column_sum(grad_act * hat)
    acc[3:4, :] = column_sum(grad_act)
    cot_own = cot_all[rows(me), :].astype(f32)
    grad_h = cot_own + layer_back(grad_act * vec(3), hat, factor)
    input_ref[...] = grad_h
    grad_branch = grad_h.astype(bf16)
    do_all[rows(me), :] = grad_branch
    gather_do = Gather(place, lambda s: do_all.at[rows(s)], do_send.at[0], lambda k: do_recv.at[k])
    gather_do.start()
    acc[4:5, :] = column_sum(grad_branch.astype(f32))
    acc[5:6, :] = column_sum(cot_own)

    poll("own")
    sum_out.release()

    dk[...] = jnp.zeros(dk.shape, f32)
    dv[...] = jnp.zeros(dv.shape, f32)

    def back_head(s, h, low, high, qlow, qhigh, ref):
        lanes = pl.ds(pl.multiple_of(h * B + qlow, 128), qhigh - qlow)
        head = pl.ds(pl.multiple_of(h * HD, HD), HD)
        weights = ref[low:high, lanes]
        grad_probs = dot(values[low:high, :], dcz_t[:, lanes], NN)
        grad_scores = weights.astype(f32) * (grad_probs - delta[h, 0:1, qlow:qhigh])
        grad_scores = grad_scores.astype(bf16)
        ref[low:high, lanes] = grad_scores
        return dot(keys_t[head, low:high], grad_scores, NN)

    def back_block(i, carry):
        s = me ^ i
        span = rows(s)

        @pl.when(i == 1)
        def _():
            gather_do.land_core()

        @pl.when(i == 2)
        def _():
            poll("do")
            gather_do.forward()

        @pl.when(i == 3)
        def _():
            gather_do.land_far()

        grad_ctx = dot(wo_all[me], do_all[span, :], NT).astype(bf16).astype(f32)
        for h in range(3):
            here = slice(h * HD, (h + 1) * HD)
            scaled = (grad_ctx[here, :] * rinv[s, h, 0:1, :]).astype(bf16)
            delta[h, 0:1, :] = column_sum(scaled.astype(f32) * ctx_t[here, span].astype(f32))
            dcz_t[here, h * B : (h + 1) * B] = scaled
            turned = jnp.concatenate([scaled, jnp.zeros((HD, B), bf16)], axis=0).T.astype(f32)
            wide = jnp.concatenate([turned, turned], axis=1)[:, 0:192]
            if h == 1:
                wide = pltpu.roll(jnp.concatenate([turned, jnp.zeros((B, 128), f32)], axis=1), HD, 1)[:, 0:192]
            dcz[h * B : (h + 1) * B, :] = jnp.where(lane_head == h, wide, 0.0).astype(bf16)

        @pl.when(s != 3)
        def _():
            dv[0:TOP, :] += dot(probs[s], dcz[...], NN)

        @pl.when(s == 3)
        def _():
            dv[...] += dot(probs_last[...], dcz[...], NN)

        def head(h, inner):
            here = pl.ds(pl.multiple_of(h * HD, HD), HD)

            @pl.when(s != 3)
            def _():
                stage[here, 0:B] = back_head(s, h, 0, TOP, 0, B, probs.at[s])

            @pl.when(s == 3)
            def _():
                stage[here, 0:128] = back_head(s, h, 0, 1024, 0, 128, probs_last)
                stage[here, 128:256] = back_head(s, h, 768, 1024, 128, 256, probs_last)

            poll_at("attend", i * 3 + h, 12)
            return inner

        lax.fori_loop(0, 3, head, 0)

        @pl.when(s != 3)
        def _():
            dk[0:TOP, :] += dot(probs[s], qz[s], NN)

        @pl.when(s == 3)
        def _():
            dk[...] += dot(probs_last[...], qz[s], NN)

        dq[span, :] = (stage[0:192, 0:B] * HD**-0.5).T.astype(bf16)
        return carry

    dcz_t[...] = jnp.zeros(dcz_t.shape, bf16)
    lax.fori_loop(0, 4, back_block, 0)

    stage_grad(6, dot(ctx_t[...], do_all[...], NN))
    poll("out")
    dkb[...] = dk[...].astype(bf16)
    dvb[...] = dv[...].astype(bf16)
    for t, ref in enumerate((dq, dkb, dvb)):
        stage_grad(7 + t, dot(ref[...], a1[...], TN))
        poll(f"qkv{t}")
    acc[9:10, 0:192] = column_sum(dq[...].astype(f32))
    acc[9:10, 256:448] = column_sum(dvb[...].astype(f32))

    def project_back(i, carry):
        s = me ^ (3 - i)
        span = rows(s)
        grad = dot(dq[span, :], wqkv_ref[0], NN)
        grad = grad + dot(dkb[span, :], wqkv_ref[1], NN)
        grad = grad + dot(dvb[span, :], wqkv_ref[2], NN)
        hat, _ = layer_hat(xp[span, :].astype(f32))
        acc[0:1, :] += column_sum(grad * hat)
        acc[1:2, :] += column_sum(grad)
        own[...] = grad
        sum_first.step(i, lambda: own[...])
        poll_at("first", i, 4)
        return carry

    lax.fori_loop(0, 4, project_back, 0)

    poll("tail")

    for gather, total in (
        (gather_wo, wo_all.at[0:3]),
        (gather_cot, cot_all.at[0:768]),
        (gather_do, do_all.at[0:768]),
        (gather_ctx(0), ctx_all.at[0:3]),
    ):
        remote(total, total, gather.send, gather.recv(0), core).wait_send()
    for block in blocks:
        block.close()
    for k, whole in enumerate((down_hbm, up_hbm, out_hbm, qkv_hbm)):
        pltpu.make_async_copy(whole, whole, local_sem.at[k]).wait()
    for save in (save_block, save_input, save_sums):
        save.wait()


def finish_kernel(
    block_hbm, input_hbm, sums_hbm, down_hbm, up_hbm, out_hbm, qkv_hbm,
    block_out, input_grad, gain_first, shift_first, grad_qkv, grad_qv, grad_out, out_bias, gain_second, shift_second,
    grad_up, up_bias, grad_down, down_bias,
    block_v, input_v, sums, down_v, up_v, out_v, qkv_v, block_w, input_w, down_w, up_w, out_w, qkv_w,
    in_sem, out_sem,
):
    share = block_out.shape[0]
    pairs = (
        (down_hbm, down_v), (up_hbm, up_v), (qkv_hbm, qkv_v), (block_hbm, block_v), (input_hbm, input_v),
        (out_hbm, out_v), (sums_hbm, sums),
    )
    loads = [pltpu.make_async_copy(src, dst, in_sem.at[k]) for k, (src, dst) in enumerate(pairs)]
    for load in loads:
        load.start()
    stores = []

    def save(src, dst):
        stores.append(pltpu.make_async_copy(src, dst, out_sem.at[len(stores)]))
        stores[-1].start()

    def widen(source, p, put):
        quarter = source.shape[3]
        for h in range(2):
            for c in range(4):
                put(slice(c * quarter, (c + 1) * quarter), slice(h * 384, (h + 1) * 384), source[p, h, c].astype(f32))

    for k, (source, wide, target) in enumerate(((down_v, down_w, grad_down), (up_v, up_w, grad_up))):
        loads[k].wait()
        for p in range(3):

            def put(r, lanes, value):
                wide[p * B + r.start : p * B + r.stop, lanes] = value

            widen(source, p, put)
        save(wide, target)
    loads[2].wait()
    for p in range(3):

        def put(r, lanes, value):
            qkv_w[p, r, lanes] = value

        widen(qkv_v, p, put)
    save(qkv_w, grad_qkv)
    for k, source, wide, target in ((3, block_v, block_w, block_out), (4, input_v, input_w, input_grad)):
        loads[k].wait()
        wide[...] = source[0:share, :]
        save(wide, target)
    loads[5].wait()

    def put(r, lanes, value):
        out_w[r, lanes] = value

    widen(out_v, 0, put)
    save(out_w, grad_out)
    loads[6].wait()
    for r, ref in enumerate((gain_first, shift_first, gain_second, shift_second, out_bias, down_bias)):
        ref[...] = sums[r, :]
    up_bias[...] = sums[8, :]
    grad_qv[0:1, :] = sums[9:10, 0:192]
    grad_qv[1:2, :] = sums[9:10, 256:448]
    for store in stores:
        store.wait()


def per_device(
    inputs, image_of_row, gain_first, shift_first, qkv_weight, qv_bias, out_weight, out_bias, gain_second,
    shift_second, up_weight, up_bias, down_weight, down_bias, cotangent,
):
    share = cotangent.shape[0]
    vmem, anyspace = (pl.BlockSpec(memory_space=m) for m in (pltpu.VMEM, pl.ANY))

    def shape(*dims, dtype=bf16):
        return pltpu.VMEM(dims, dtype)

    dma = pltpu.SemaphoreType.DMA

    def block_scratch(first_y, r):
        over = shape(4, r, 384) if first_y else shape(r, 384)
        along = shape(3, r, 384) if first_y else shape(2, 3, r, 384)
        return [shape(2, 4, r, 384), over, along, along, shape(2, 4, r, 384), dma((3,)), dma((8,))]

    scratch = [
        shape(1024, 768), shape(272, 768, dtype=f32), shape(1024, 768),
        shape(1024, 192), shape(1024, 192), shape(192, 1024), shape(192, 1024),
        shape(4, 192, 768), shape(4, 768, 192),
        shape(1024, B, dtype=i32), shape(4, 8, B, dtype=i32),
        shape(3, TOP, 768), shape(1024, 768), shape(4, 3, 8, B, dtype=f32),
        shape(192, 1024), shape(4, 4, 384, 128), shape(4, 192, 768), shape(1024, 768),
        shape(1024, 768), shape(1024, 768), shape(1024, 768), shape(1024, 768),
        shape(192, 768), shape(768, 192), shape(3, 8, B, dtype=f32),
        shape(1024, 192), shape(1024, 192, dtype=f32), shape(1024, 192, dtype=f32),
        shape(1024, 192), shape(1024, 192), shape(B, 768, dtype=f32),
        shape(3, B, 768), shape(2, B, 768), shape(B, 768),
        shape(3, B, 768), shape(2, B, 768), shape(B, 768), shape(B, 768, dtype=f32),
        shape(8, 768, dtype=f32),
        shape(16, 768, dtype=f32), shape(4, 16, 768, dtype=f32), shape(16, 768, dtype=f32), shape(4, 16, 768, dtype=f32),
    ]
    one, three = dma((1,)), dma((3,))
    scratch += [one, three, one, three, one, dma((4, 3)), one, three] + [one, three] * 3
    scratch += [three, dma((7,)), dma((7,)), dma((15,))]
    scratch += [shape(4 * share, 768), shape(3, 192, 768), shape(768, 768), shape(768, 768), shape(share, 768)]
    scratch += [[shape(768)] * 7, shape(2, 192), shape(B, 768, dtype=f32), shape(B, 768, dtype=f32)]
    scratch += [shape(16, 768, dtype=f32), pltpu.SMEM(image_of_row.shape, i32)]
    scratch += [[block_scratch(first_y, r) for first_y, r in zip(FIRST_Y, QUARTER)]]
    results = pl.pallas_call(
        layer_kernel,
        out_shape=[
            jax.ShapeDtypeStruct((B, 768), f32),
            jax.ShapeDtypeStruct((B, 768), f32),
            jax.ShapeDtypeStruct((16, 768), f32),
            jax.ShapeDtypeStruct((3, 2, 4, 64, 384), bf16),
            jax.ShapeDtypeStruct((3, 2, 4, 64, 384), bf16),
            jax.ShapeDtypeStruct((1, 2, 4, 48, 384), bf16),
            jax.ShapeDtypeStruct((3, 2, 4, 48, 384), bf16),
        ],
        in_specs=[anyspace] * 15,
        out_specs=[anyspace] * 7,
        scratch_shapes=scratch,
        compiler_params=pltpu.CompilerParams(
            collective_id=0, has_side_effects=True, vmem_limit_bytes=60 * 2**20
        ),
        name="layer",
    )(
        inputs, image_of_row, gain_first, shift_first, qv_bias, out_bias, gain_second, shift_second, up_bias, down_bias,
        jnp.swapaxes(qkv_weight, 1, 2), out_weight, up_weight, down_weight, cotangent,
    )

    def out(*dims):
        return jax.ShapeDtypeStruct(dims, f32)

    wide = [shape(share, 768, dtype=f32)] * 2 + [shape(768, 768, dtype=f32)] * 2
    outputs = pl.pallas_call(
        finish_kernel,
        out_shape=[
            out(share, 768), out(share, 768), out(768), out(768), out(3, 192, 768), out(2, 192), out(192, 768),
            out(768), out(768), out(768), out(768, 768), out(768), out(768, 768), out(768),
        ],
        in_specs=[anyspace] * 7,
        out_specs=[anyspace if k in (0, 1, 4, 6, 10, 12) else vmem for k in range(14)],
        scratch_shapes=[pltpu.VMEM(r.shape, r.dtype) for r in results]
        + wide + [shape(192, 768, dtype=f32), shape(3, 192, 768, dtype=f32), dma((7,)), dma((6,))],
        compiler_params=pltpu.CompilerParams(vmem_limit_bytes=60 * 2**20),
        name="finish",
    )(*results)
    return (*outputs[:4], jnp.swapaxes(outputs[4], 1, 2), *outputs[5:])


def solution(mesh):
    return jax.shard_map(
        per_device,
        mesh=mesh,
        in_specs=(
            P("dp", None),
            P("dp"),
            P(),
            P(),
            P(None, None, "mp"),
            P(None, "mp"),
            P("mp", None),
            P(),
            P(),
            P(),
            P(None, "mp"),
            P("mp"),
            P("mp", None),
            P(),
            P(("dp", "mp"), None),
        ),
        out_specs=(
            P(("dp", "mp"), None),
            P(("dp", "mp"), None),
            P(),
            P(),
            P(None, None, "mp"),
            P(None, "mp"),
            P("mp", None),
            P(),
            P(),
            P(),
            P(None, "mp"),
            P("mp"),
            P("mp", None),
            P(),
        ),
        check_vma=False,
    )
```

```python
import functools

import jax
import jax.numpy as jnp
from jax import lax
from jax.experimental import pallas as pl
from jax.experimental.pallas import tpu as pltpu
from jax.sharding import PartitionSpec as P

f32, bf16, i32 = jnp.float32, jnp.bfloat16, jnp.int32
MESH = pl.DeviceIdType.MESH
NN = (((1,), (0,)), ((), ()))
NT = (((1,), (1,)), ((), ()))
TN = (((0,), (0,)), ((), ()))
HD = 64
P_LO = 196
EPSILON = 1e-06
B = 256
TOP = 832
BIG = 4 * P_LO


def dot(left, right, dims):
    return lax.dot_general(left, right, dims, preferred_element_type=f32)


def rows(start, size=B):
    return pl.ds(pl.multiple_of(start * size, size), size)


def layer_hat(values):
    center = values - jnp.mean(values, axis=1, keepdims=True)
    factor = lax.rsqrt(jnp.mean(center * center, axis=1, keepdims=True) + EPSILON)
    return center * factor, factor


def layer_back(grad_hat, normed, factor):
    first = jnp.mean(grad_hat, axis=1, keepdims=True)
    second = jnp.mean(grad_hat * normed, axis=1, keepdims=True)
    return factor * (grad_hat - first - normed * second)


def column_sum(values):
    return jnp.sum(values, axis=0, keepdims=True)


def remote(src, dst, send, recv, device):
    return pltpu.make_async_remote_copy(
        src_ref=src, dst_ref=dst, send_sem=send, recv_sem=recv, device_id=device, device_id_type=MESH
    )


class Gather:
    def __init__(self, place, view, send, recv):
        self.me, self.core, self.across = place
        self.view, self.send, self.recv = view, send, recv

    def copy(self, slot, k, device, part=None):
        view = self.view(slot) if part is None else self.view(slot).at[part]
        return remote(view, view, self.send, self.recv(k), device)

    def start(self):
        self.copy(self.me, 1, self.across).start()
        self.copy(self.me, 0, self.core).start()

    def forward(self):
        slot = self.me ^ 2
        self.copy(slot, 1, self.across).wait_recv()
        self.copy(slot, 2, self.core).start()

    def land_core(self):
        self.copy(self.me ^ 1, 0, self.core).wait_recv()

    def land_far(self):
        self.copy(self.me ^ 3, 2, self.core).wait_recv()


class Scatter:
    def __init__(self, place, out, both, far, own, send, recv):
        self.me, self.core, self.across = place
        self.out, self.both, self.far, self.own = out, both, far, own
        self.send, self.recv = send, recv

    def copy(self, k):
        src = self.out.at[k]
        dst = self.far if k == 1 else self.both.at[k // 2]
        return remote(src, dst, self.send, self.recv.at[k], self.across if k == 1 else self.core)

    def step(self, i, value, hold=False):
        @pl.when(i == 0)
        def _():
            self.out[0] = value().astype(bf16)
            self.copy(0).start()

        @pl.when(i == 1)
        def _():
            if hold:
                self.out[1] = value().astype(bf16)
            else:
                self.copy(0).wait_recv()
                self.out[1] = (value() + self.both[0].astype(f32)).astype(bf16)
                self.copy(1).start()

        @pl.when(i == 2)
        def _():
            self.out[2] = value().astype(bf16)
            self.copy(2).start()

        @pl.when(i == 3)
        def _():
            self.own[...] = value()

    def release(self):
        self.copy(0).wait_recv()
        self.out[1] = (self.out[1].astype(f32) + self.both[0].astype(f32)).astype(bf16)
        self.copy(1).start()

    def finish(self):
        self.copy(2).wait_recv()
        self.copy(1).wait_recv()
        total = self.own[...] + self.both[1].astype(f32) + self.far[...].astype(f32)
        remote(self.out, self.out, self.send, self.recv.at[0], self.core).wait_send()
        return total


class Reduce:
    def __init__(self, spot, first_y, refs):
        self.zi, self.yi, self.over, self.above, self.below = spot
        self.first_y = first_y
        self.part, self.ybuf, self.up, self.down, self.whole, self.send, self.recv = refs

    def copy(self, src, dst, k, slot, device):
        return remote(src, dst, self.send.at[k], self.recv.at[slot], device)

    def begin(self, condition, make):
        if condition is None:
            make().start()
        else:
            pl.when(condition())(lambda: make().start())

    def close(self):
        all_along = self.whole.at[self.yi] if self.first_y else self.whole
        all_over = self.whole if self.first_y else self.whole.at[:, 0]
        pl.when(self.zi < 3)(lambda: self.copy(all_along, all_along, 1, 1, self.above).wait_send())
        pl.when(self.zi > 0)(lambda: self.copy(all_along, all_along, 2, 2, self.below).wait_send())
        self.copy(all_over, all_over, 0, 0, self.over).wait_send()

    def chunks(self, first, count):
        return self.part.at[self.yi if self.first_y else slice(None), pl.ds(first, count)]

    def rising(self, first, count):
        span = pl.ds(first - 1, count)
        return self.up.at[span] if self.first_y else self.up.at[:, span]

    def falling(self, first, count):
        span = pl.ds(first, count)
        return self.down.at[span] if self.first_y else self.down.at[:, span]

    def result(self, chunk):
        return self.whole.at[self.yi if self.first_y else slice(None), chunk]

    def copy_up(self, first, count, src):
        return self.copy(src, self.rising(first, count), 1, 1, self.above)

    def copy_down(self, first, count, src):
        return self.copy(src, self.falling(first, count), 2, 2, self.below)

    def at(self, z):
        return lambda: self.zi == z

    def hop(self, n):
        up_first, down_count = n, 4 - n

        def up_view():
            return self.chunks(n, 4 - n) if n == 1 else self.rising(n, 4 - n)

        def down_view():
            return self.chunks(0, 4 - n) if n == 1 else self.falling(0, 4 - n)

        if n > 1:

            @pl.when(self.zi == n - 1)
            def _():
                came = self.rising(n - 1, 5 - n)
                self.copy_up(n - 1, 5 - n, came).wait_recv()
                view, own = self.rising(n, 4 - n), self.chunks(n, 4 - n)
                view[...] = (view[...].astype(f32) + own[...].astype(f32)).astype(bf16)

            @pl.when(self.zi == 4 - n)
            def _():
                came = self.falling(0, 5 - n)
                self.copy_down(0, 5 - n, came).wait_recv()
                view, own = self.falling(0, 4 - n), self.chunks(0, 4 - n)
                view[...] = (view[...].astype(f32) + own[...].astype(f32)).astype(bf16)

        self.begin(self.at(n - 1), lambda: self.copy_up(up_first, 4 - n, up_view()))
        self.begin(self.at(4 - n), lambda: self.copy_down(0, down_count, down_view()))

    def total(self, store):
        def plain(view):
            return view[...].astype(f32)

        @pl.when(self.zi == 0)
        def _():
            self.copy_down(0, 1, self.falling(0, 1)).wait_recv()
            store(0, plain(self.chunks(0, 1)) + plain(self.falling(0, 1)))

        @pl.when(self.zi == 3)
        def _():
            self.copy_up(3, 1, self.rising(3, 1)).wait_recv()
            store(3, plain(self.chunks(3, 1)) + plain(self.rising(3, 1)))

        for z in (1, 2):

            @pl.when(self.zi == z)
            def _(z=z):
                value = plain(self.chunks(z, 1)) + plain(self.rising(z, 1)) + plain(self.falling(z, 1))
                store(z, value)

    def back(self, d):
        for sign, k, ahead, room in ((-1, 1, self.above, lambda: self.zi < 3), (1, 2, self.below, lambda: self.zi > 0)):

            def here(sign=sign):
                return self.zi >= d if sign < 0 else self.zi <= 3 - d

            def move(sign=sign, k=k, ahead=ahead):
                chunk = self.zi + sign * d
                view = self.result(chunk)
                return self.copy(view, view, k, 3 + chunk, ahead)

            if d > 0:

                @pl.when(here())
                def _():
                    move().wait_recv()

            if d < 3:
                self.begin(lambda room=room, here=here: room() & here(), move)
            if self.first_y and (d > 0 or sign < 0):
                self.begin(here, lambda sign=sign: self.copy_over(self.yi, self.zi + sign * d))

    def copy_over(self, half, chunk):
        view = self.whole.at[half, chunk]
        return self.copy(view, view, 0, 7, self.over)

    def sum_over(self):
        if self.first_y:
            return self.copy(self.part.at[1 - self.yi], self.ybuf, 0, 0, self.over)
        return self.copy(self.part.at[1 - self.yi, self.zi], self.ybuf, 0, 0, self.over)

    def stage(self, k):
        if self.first_y:
            if k == 0:
                self.begin(None, self.sum_over)
            elif k == 1:
                self.sum_over().wait_recv()

                def add(c, carry):
                    value = self.part[self.yi, c].astype(f32) + self.ybuf[c].astype(f32)
                    self.part[self.yi, c] = value.astype(bf16)
                    return carry

                lax.fori_loop(0, 4, add, 0)
                self.hop(1)
            elif k in (2, 3):
                self.hop(k)
            elif k == 4:

                def store(z, value):
                    self.whole[self.yi, z] = value[0].astype(bf16)

                self.total(store)
                self.back(0)
            elif k in (5, 6, 7):
                self.back(k - 4)
            else:
                other = self.whole.at[1 - self.yi]
                self.copy(other, other, 0, 7, self.over).wait_recv()
        else:
            if k in (0, 1, 2):
                self.hop(k + 1)
            elif k == 3:

                def store(z, value):
                    self.part[:, z] = value[:, 0].astype(bf16)

                self.total(store)
                self.begin(None, self.sum_over)
            elif k == 4:
                self.sum_over().wait_recv()
                value = self.part[self.yi, self.zi].astype(f32) + self.ybuf[...].astype(f32)
                self.whole[self.yi, self.zi] = value.astype(bf16)
                self.begin(None, lambda: self.copy_over(self.yi, self.zi))
            elif k == 5:
                self.copy_over(1 - self.yi, self.zi).wait_recv()
                self.back(0)
            else:
                self.back(k - 5)


FIRST_Y = (True, False, True, True, True, True, True, True, True, False)
QUARTER = (64,) * 6 + (48,) * 4
STAGES = 9

POLLS = {
    "down0": ((0, 0),),
    "down1": ((1, 0),),
    "down2": ((2, 0),),
    "mid3": ((0, 1),),
    "up0": ((3, 0),),
    "up1": ((4, 0),),
    "up2": ((5, 0), (1, 1),),
    "mlp2": ((2, 1),),
    "rs1": ((0, 2),),
    "own": ((3, 1), (2, 2), (1, 2),),
    "attend0": ((0, 3),),
    "after0": ((4, 1),),
    "prep1": ((3, 2), (2, 3), (1, 3),),
    "attend1": ((0, 4),),
    "after1": ((5, 1),),
    "do": ((2, 4), (4, 2), (1, 4), (3, 3),),
    "prep2": ((0, 5),),
    "attend2": ((3, 4), (1, 5), (5, 2),),
    "after2": ((4, 3), (2, 5),),
    "prep3": ((0, 6),),
    "attend3": ((3, 5),),
    "out": ((6, 0), (1, 6),),
    "qkv0": ((7, 0),),
    "qkv1": ((8, 0), (4, 4),),
    "qkv2": ((9, 0),),
    "first0": ((5, 3),),
    "first1": ((2, 6), (0, 7), (3, 6),),
    "tail": ((11, 0), (10, 0), (1, 7), (6, 1), (4, 5), (5, 4), (9, 1), (2, 7), (7, 1), (3, 7), (6, 2), (1, 8), (8, 1), (4, 6), (12, 0), (9, 2), (7, 2), (5, 5), (0, 8), (10, 1), (6, 3), (4, 7), (8, 2), (9, 3), (2, 8), (7, 3), (3, 8), (5, 6), (6, 4), (7, 4), (8, 3), (5, 7), (6, 5), (4, 8), (10, 2), (7, 5), (9, 4), (8, 4), (6, 6), (5, 8), (9, 5), (10, 3), (7, 6), (6, 7), (8, 5), (9, 6), (7, 7), (6, 8), (8, 6), (9, 7), (7, 8), (8, 7), (9, 8), (8, 8),),
}


def layer_kernel(
    x_hbm, ids_hbm, gain_a, shift_a, bias_qv, bias_out, gain_b, shift_b, bias_up, bias_down,
    wqkv_hbm, wo_hbm, wup_hbm, wdn_hbm, cot_hbm,
    block_hbm, input_hbm, sums_hbm, down_hbm, up_hbm, out_hbm, qkv_hbm,
    xp, stage, a1, keys, values, keys_t, values_t, qz_t, qz, kid, qid, probs, probs_last, rinv, ctx_t, ctx_all,
    wo_all, cot_all, a2, gate, du, do_all, dcz_t, dcz, delta, dk, dv, own,
    rs_out, rs_both, rs_far, ms_out, ms_both, ms_far, m_own,
    vec_ref, acc, v_mp, v_y, v_z,
    wo_send, wo_recv, cot_send, cot_recv, ctx_send, ctx_recv, do_send, do_recv,
    rs_send, rs_recv, ms_send, ms_recv, rt_send, rt_recv,
    v_send, v_recv, local_sem, load_sem, x_ref, wqkv_ref, wup_ref, wdn_ref, cot_ref, vec_raw, qv_raw,
    block_ref, input_ref, sums_ref, ids_ref, block_refs,
):
    dp, me = lax.axis_index("dp"), lax.axis_index("mp")
    core, across, diagonal = (dp, me ^ 1), (dp, me ^ 2), (dp, me ^ 3)
    yi, zi = dp & 1, (dp >> 1) & 3
    ypeer = (dp ^ 1, me)
    zpeers = [(dp ^ (2 * j), me) for j in (1, 2, 3)]
    place = (me, core, across)
    base = dp & ~7
    above, below = (base + (((zi + 1) & 3) << 1) + yi, me), (base + (((zi + 3) & 3) << 1) + yi, me)
    spot = (zi, yi, ypeer, above, below)
    share = cot_hbm.shape[0]

    barrier = pltpu.get_barrier_semaphore()
    partners = [core, across, diagonal, ypeer] + zpeers
    for partner in partners:
        pl.semaphore_signal(barrier, inc=1, device_id=partner, device_id_type=MESH)

    def vec(r, width=None):
        return vec_ref[r : r + 1, :] if width is None else vec_ref[r : r + 1, width[0] : width[1]]

    pairs = [(wo_hbm, wo_all.at[me]), (cot_hbm, cot_ref), (x_hbm, x_ref), (bias_qv, qv_raw)]
    pairs += list(zip((gain_a, shift_a, bias_out, gain_b, shift_b, bias_up, bias_down), vec_raw))
    pairs += [(wqkv_hbm, wqkv_ref), (wup_hbm, wup_ref), (wdn_hbm, wdn_ref), (ids_hbm, ids_ref)]
    loads = [pltpu.make_async_copy(src, dst, load_sem.at[k]) for k, (src, dst) in enumerate(pairs)]
    for load in loads:
        load.start()
    pl.semaphore_wait(barrier, len(partners))

    gather_wo = Gather(place, lambda s: wo_all.at[s], wo_send.at[0], lambda k: wo_recv.at[k])
    loads[0].wait()
    gather_wo.start()

    gather_cot = Gather(place, lambda s: cot_all.at[rows(s)], cot_send.at[0], lambda k: cot_recv.at[k])

    loads[1].wait()
    stage[240:256, :] = jnp.zeros((16, 768), f32)
    stage[0:share, :] = cot_ref[...].astype(f32)
    cot_all[rows(me), :] = stage[0:B, :].astype(bf16)
    gather_cot.copy(me, 0, core).start()
    acc[...] = jnp.zeros(acc.shape, f32)
    for k in range(3, 11):
        loads[k].wait()
    for r, ref in enumerate(vec_raw):
        vec_ref[r : r + 1, :] = ref[...].astype(f32).reshape(1, 768)
    vec_ref[7:8, 0:192] = qv_raw[0:1, :].astype(f32)
    vec_ref[7:8, 256:448] = qv_raw[1:2, :].astype(f32)
    loads[2].wait()

    row_in = lax.broadcasted_iota(i32, (B, 768), 0)
    for s in range(4):
        first = s * share // 16 * 16
        last = min(first + 272, 4 * share)
        stage[0 : last - first, :] = x_ref[first:last, :].astype(f32)
        moved = stage[s * share - first : s * share - first + B, :]
        xp[s * B : (s + 1) * B, :] = jnp.where(row_in < share, moved, 0.0).astype(bf16)

    loads[14].wait()
    two_images = (ids_ref[0] == ids_ref[BIG - 1]).astype(i32)

    def image_of(index, shard, pad):
        place_of = index + shard * share
        small = jnp.zeros_like(index)
        for k in range(1, 5):
            small = small + (place_of >= k * P_LO).astype(i32)
        large = (place_of >= BIG).astype(i32)
        image = small * (1 - two_images) + large * two_images
        return jnp.where(index < share, image, pad)

    def images(s, carry):
        kid[rows(s), :] = image_of(lax.broadcasted_iota(i32, (B, B), 0), s, -1)
        qid[s] = image_of(lax.broadcasted_iota(i32, (8, B), 1), s, -2)
        qz_t[s] = jnp.zeros(qz_t.shape[1:], bf16)
        return carry

    lax.fori_loop(0, 4, images, 0)

    lane_head = lax.broadcasted_iota(i32, (B, 192), 1) // HD

    def project(s, carry):
        span = rows(s)
        hat, _ = layer_hat(xp[span, :].astype(f32))
        act = (hat * vec(0) + vec(1)).astype(bf16)
        a1[span, :] = act
        q = (dot(act, wqkv_ref[0], NT) + vec(7, (0, 192))).astype(bf16)
        k = dot(act, wqkv_ref[1], NT).astype(bf16)
        v = (dot(act, wqkv_ref[2], NT) + vec(7, (256, 448))).astype(bf16)
        keys[span, :] = k
        values[span, :] = v
        keys_t[:, span] = k.T
        values_t[:, span] = v.T
        q = q.astype(f32) * HD**-0.5
        qt = q.astype(bf16).T
        for h in range(3):
            qz_t[s, h * HD : (h + 1) * HD, h * B : (h + 1) * B] = qt[h * HD : (h + 1) * HD, :]
            qz[s, h * B : (h + 1) * B, :] = jnp.where(lane_head == h, q, 0.0).astype(bf16)
        return carry

    loads[11].wait()
    lax.fori_loop(0, 4, project, 0)

    def gather_ctx(s):
        return Gather(
            place, lambda j: ctx_all.at[j, s], ctx_send.at[0], lambda k: ctx_recv.at[s, k]
        )

    def attend(s, low, high, qlow, qhigh):
        width = qhigh - qlow
        wanted = qz_t[s]
        if width < B:
            wanted = jnp.concatenate([wanted[:, h * B + qlow : h * B + qhigh] for h in range(3)], axis=1)
        scores = dot(keys[low:high, :], wanted, NN)
        same = kid[low:high, qlow:qhigh] == qid[s, 0:1, qlow:qhigh]
        scores = jnp.where(jnp.concatenate([same] * 3, axis=1), scores, -1e30)
        weights = jnp.exp(scores - jnp.max(scores, axis=0, keepdims=True))
        inverse = 1.0 / jnp.sum(weights, axis=0, keepdims=True)
        weights = weights.astype(bf16)
        mixed = dot(values_t[:, low:high], weights, NN) * inverse
        for h in range(3):
            rinv[s, h, 0:1, qlow:qhigh] = inverse[:, h * width : (h + 1) * width]
        heads = [mixed[h * HD : (h + 1) * HD, h * width : (h + 1) * width] for h in range(3)]
        return weights, jnp.concatenate(heads, axis=0).astype(bf16)

    def send_ctx(s):
        span = rows(s)
        block = ctx_t[:, span]
        ctx_all[me, s, 0:B, :] = block[0:128, :].T
        last = jnp.concatenate([block[128:192, 0:128], block[128:192, 128:256]], axis=0)
        ctx_all[me, s, B : B + 128, :] = last.T
        gather_ctx(s).start()

    def attend_top(s, carry):
        probs[s], ctx_t[:, rows(s)] = attend(s, 0, TOP, 0, B)
        send_ctx(s)

        @pl.when(s == 1)
        def _():
            gather_wo.forward()

        return carry

    lax.fori_loop(0, 3, attend_top, 0)

    left, ctx_t[:, 768:896] = attend(3, 0, 1024, 0, 128)
    right, ctx_t[:, 896:1024] = attend(3, 768, 1024, 128, 256)
    for h in range(3):
        probs_last[:, h * B : h * B + 128] = left[:, h * 128 : (h + 1) * 128]
        probs_last[0:768, h * B + 128 : (h + 1) * B] = jnp.zeros((768, 128), bf16)
        probs_last[768:1024, h * B + 128 : (h + 1) * B] = right[:, h * 128 : (h + 1) * 128]
    send_ctx(3)

    for q in range(4):
        gather_cot.copy(me, 1, across, pl.ds(q * 64, 64)).start()
    gather_wo.land_core()
    gather_wo.land_far()
    for s in range(4):
        gather_ctx(s).forward()
    loads[12].wait()
    loads[13].wait()

    zeros_w = jnp.zeros((HD, 768), bf16)

    def middle(i, carry):
        s = me ^ (3 - i)
        span = rows(s)
        ctx = gather_ctx(s)
        ctx.land_core()
        ctx.land_far()
        left = jnp.concatenate([ctx_all[j, s, 0:B, :] for j in range(4)], axis=1)
        last = jnp.concatenate([ctx_all[j, s, B : B + 128, :] for j in range(4)], axis=1)
        w_left = jnp.concatenate([wo_all[j, 0:128, :] for j in range(4)], axis=0)
        w_tail = [wo_all[j, 128:192, :] for j in range(4)]
        w_upper = jnp.concatenate([piece for w in w_tail for piece in (w, zeros_w)], axis=0)
        w_lower = jnp.concatenate([piece for w in w_tail for piece in (zeros_w, w)], axis=0)
        branch = dot(left, w_left, NN) + jnp.concatenate(
            [dot(last, w_upper, NN), dot(last, w_lower, NN)], axis=0
        )
        h = xp[span, :].astype(f32) + (branch + vec(2))

        @pl.when(i == 3)
        def _():
            block_ref[...] = h

        hat, _ = layer_hat(h)
        act = (hat * vec(3) + vec(4)).astype(bf16)
        a2[span, :] = act
        u = dot(act, wup_ref[...], NN) + vec(5)
        cdf = 0.5 * (1.0 + lax.erf(u * 0.7071067811865476))
        gate[span, :] = (u * cdf).astype(bf16)
        du[span, :] = (cdf + u * (0.3989422804014327 * jnp.exp(-0.5 * (u * u)))).astype(bf16)
        return carry

    lax.fori_loop(0, 4, middle, 0)

    gather_cot.forward()
    gather_cot.land_core()
    gather_cot.land_far()

    blocks = [Reduce(spot, first_y, refs) for first_y, refs in zip(FIRST_Y, block_refs)]
    homes = [down_hbm.at[p] for p in range(3)] + [up_hbm.at[p] for p in range(3)]
    homes += [out_hbm.at[0]] + [qkv_hbm.at[p] for p in range(3)]
    tensor = (0, 0, 0, 1, 1, 1, 2, 3, 3, 3)
    saves = [pltpu.make_async_copy(blocks[p].whole, homes[p], local_sem.at[tensor[p]]) for p in range(10)]
    save_block = pltpu.make_async_copy(block_ref, block_hbm, local_sem.at[4])
    save_input = pltpu.make_async_copy(input_ref, input_hbm, local_sem.at[5])
    save_sums = pltpu.make_async_copy(sums_ref, sums_hbm, local_sem.at[6])

    def sum_copy(slot, k, device, ref=v_mp):
        view = ref.at[slot]
        return remote(view, view, v_send.at[0 if k < 3 else 2], v_recv.at[k], device)

    def sum_y():
        return remote(acc, v_y, v_send.at[1], v_recv.at[3], ypeer)

    def sums(k):
        if k == 0:
            v_mp[me] = acc[...]
            for j in (1, 2, 3):
                sum_copy(me, j - 1, (dp, me ^ j)).start()
        elif k == 1:
            for j in (1, 2, 3):
                sum_copy(me ^ j, j - 1, (dp, me ^ j)).wait_recv()
            acc[0:8, :] = v_mp[0, 0:8, :] + v_mp[1, 0:8, :] + v_mp[2, 0:8, :] + v_mp[3, 0:8, :]
            sum_y().start()
        elif k == 2:
            sum_y().wait()
            v_z[zi] = acc[...] + v_y[...]
            for j in (1, 2, 3):
                sum_copy(zi, 3 + j, zpeers[j - 1], v_z).start()
        else:
            for j in (1, 2, 3):
                sum_copy(zi ^ j, 3 + j, zpeers[j - 1], v_z).wait_recv()
            sums_ref[...] = v_z[0] + v_z[1] + v_z[2] + v_z[3]
            save_sums.start()
            sum_copy(slice(0, 3), 0, core).wait_send()
            sum_copy(slice(0, 3), 4, core, v_z).wait_send()

    sum_in = Scatter(place, rs_out, rs_both, rs_far, own, rs_send.at[0], rs_recv)
    sum_out = Scatter(place, ms_out, ms_both, ms_far, m_own, ms_send.at[0], ms_recv)
    sum_first = Scatter(place, rs_out, rs_both, rs_far, own, rt_send.at[0], rt_recv)

    def finish_block(k):
        block_ref[...] = block_ref[...] + (sum_out.finish() + vec(6))
        save_block.start()

    def finish_input(k):
        grad = sum_first.finish()
        hat, factor = layer_hat(xp[rows(me), :].astype(f32))
        input_ref[...] = input_ref[...] + layer_back(grad * vec(0), hat, factor)
        save_input.start()

    others = (sums, finish_block, finish_input)

    def poll(name):
        for p, k in POLLS.get(name, ()):
            if p >= len(blocks):
                others[p - len(blocks)](k)
                continue
            blocks[p].stage(k)
            if k == STAGES - 1:
                saves[p].start()

    def poll_at(prefix, index, count):
        for n in range(count):
            if POLLS.get(f"{prefix}{n}"):
                pl.when(index == n)(lambda n=n: poll(f"{prefix}{n}"))

    def stage_grad(p, piece):
        quarter = QUARTER[p]
        for h in range(2):
            for c in range(4):
                part = piece[c * quarter : (c + 1) * quarter, h * 384 : (h + 1) * 384]
                blocks[p].part[h, c] = part.astype(bf16)

    for t in range(3):
        stage_grad(t, dot(gate[:, t * B : (t + 1) * B], cot_all[...], TN))
        poll(f"down{t}")

    def hidden_back(i, carry):
        span = rows(me ^ (3 - i))
        grad_u = (dot(cot_all[span, :], wdn_ref[...], NT) * du[span, :].astype(f32)).astype(bf16)
        du[span, :] = grad_u
        acc[8:9, :] += column_sum(grad_u.astype(f32))
        own[...] = dot(grad_u, wup_ref[...], NT)
        sum_in.step(i, lambda: own[...])
        poll_at("mid", i, 4)
        return carry

    lax.fori_loop(0, 4, hidden_back, 0)

    for t in range(3):
        stage_grad(3 + t, dot(a2[:, t * B : (t + 1) * B], du[...], TN))
        poll(f"up{t}")
    poll("up2b")

    def project_down(i, carry):
        s = me ^ (3 - i)
        m_own[...] = dot(gate[rows(s), :], wdn_ref[...], NN)
        sum_out.step(i, lambda: m_own[...], hold=True)
        poll_at("mlp", i, 4)
        return carry

    lax.fori_loop(0, 4, project_down, 0)

    poll("rs1")
    grad_act = sum_in.finish()
    hat, factor = layer_hat(block_ref[...])
    acc[2:3, :] = column_sum(grad_act * hat)
    acc[3:4, :] = column_sum(grad_act)
    cot_own = cot_all[rows(me), :].astype(f32)
    grad_h = cot_own + layer_back(grad_act * vec(3), hat, factor)
    input_ref[...] = grad_h
    grad_branch = grad_h.astype(bf16)
    do_all[rows(me), :] = grad_branch
    gather_do = Gather(place, lambda s: do_all.at[rows(s)], do_send.at[0], lambda k: do_recv.at[k])
    gather_do.start()
    acc[4:5, :] = column_sum(grad_branch.astype(f32))
    acc[5:6, :] = column_sum(cot_own)

    poll("own")
    sum_out.release()

    dq, dkb, dvb = (slice(256 * k, 256 * k + 192) for k in range(3))
    dk[...] = jnp.zeros(dk.shape, f32)
    dv[...] = jnp.zeros(dv.shape, f32)

    def back_heads(weights, low, high, wanted, center):
        width = weights.shape[1] // 3
        grad_scores = weights.astype(f32) * (dot(values[low:high, :], wanted, NN) - center)
        grad_scores = grad_scores.astype(bf16)
        mixed = dot(keys_t[:, low:high], grad_scores, NN)
        heads = [mixed[h * HD : (h + 1) * HD, h * width : (h + 1) * width] for h in range(3)]
        return grad_scores, jnp.concatenate(heads, axis=0)

    def back_block(i, carry):
        s = me ^ i
        span = rows(s)

        @pl.when(i == 1)
        def _():
            gather_do.land_core()

        @pl.when(i == 2)
        def _():
            poll("do")
            gather_do.forward()

        @pl.when(i == 3)
        def _():
            gather_do.land_far()

        grad_ctx = dot(wo_all[me], do_all[span, :], NT).astype(bf16).astype(f32)
        for h in range(3):
            here = slice(h * HD, (h + 1) * HD)
            scaled = (grad_ctx[here, :] * rinv[s, h, 0:1, :]).astype(bf16)
            delta[0:1, h * B : (h + 1) * B] = column_sum(scaled.astype(f32) * ctx_t[here, span].astype(f32))
            dcz_t[here, h * B : (h + 1) * B] = scaled
            turned = jnp.concatenate([scaled, jnp.zeros((HD, B), bf16)], axis=0).T.astype(f32)
            wide = jnp.concatenate([turned, turned], axis=1)[:, 0:192]
            if h == 1:
                wide = pltpu.roll(jnp.concatenate([turned, jnp.zeros((B, 128), f32)], axis=1), HD, 1)[:, 0:192]
            dcz[h * B : (h + 1) * B, :] = jnp.where(lane_head == h, wide, 0.0).astype(bf16)

        @pl.when(s != 3)
        def _():
            dv[0:TOP, :] += dot(probs[s], dcz[...], NN)

        @pl.when(s == 3)
        def _():
            dv[...] += dot(probs_last[...], dcz[...], NN)

        poll_at("prep", i, 4)

        @pl.when(s != 3)
        def _():
            probs[s], stage[0:192, 0:B] = back_heads(probs[s], 0, TOP, dcz_t[...], delta[0:1, :])

        @pl.when(s == 3)
        def _():
            def side(ref, low, high, qlow):
                parts = [ref[low:high, h * B + qlow : h * B + qlow + 128] for h in range(3)]
                return jnp.concatenate(parts, axis=1)

            for low, qlow in ((0, 0), (768, 128)):
                wanted, center = side(dcz_t, 0, 192, qlow), side(delta, 0, 1, qlow)
                grad_scores, grad_q = back_heads(side(probs_last, low, 1024, qlow), low, 1024, wanted, center)
                stage[0:192, qlow : qlow + 128] = grad_q
                for h in range(3):
                    lanes = slice(h * B + qlow, h * B + qlow + 128)
                    probs_last[low:1024, lanes] = grad_scores[:, h * 128 : (h + 1) * 128]

        poll_at("attend", i, 4)

        @pl.when(s != 3)
        def _():
            dk[0:TOP, :] += dot(probs[s], qz[s], NN)

        @pl.when(s == 3)
        def _():
            dk[...] += dot(probs_last[...], qz[s], NN)

        a2[span, dq] = (stage[0:192, 0:B] * HD**-0.5).T.astype(bf16)
        poll_at("after", i, 4)
        return carry

    dcz_t[...] = jnp.zeros(dcz_t.shape, bf16)
    lax.fori_loop(0, 4, back_block, 0)

    stage_grad(6, dot(ctx_t[...], do_all[...], NN))
    poll("out")
    a2[:, dkb] = dk[...].astype(bf16)
    a2[:, dvb] = dv[...].astype(bf16)
    for t, lanes in enumerate((dq, dkb, dvb)):
        stage_grad(7 + t, dot(a2[:, lanes], a1[...], TN))
        poll(f"qkv{t}")
    acc[9:10, 0:192] = column_sum(a2[:, dq].astype(f32))
    acc[9:10, 256:448] = column_sum(a2[:, dvb].astype(f32))

    def project_back(i, carry):
        s = me ^ (3 - i)
        span = rows(s)
        grad = dot(a2[span, dq], wqkv_ref[0], NN)
        grad = grad + dot(a2[span, dkb], wqkv_ref[1], NN)
        grad = grad + dot(a2[span, dvb], wqkv_ref[2], NN)
        hat, _ = layer_hat(xp[span, :].astype(f32))
        acc[0:1, :] += column_sum(grad * hat)
        acc[1:2, :] += column_sum(grad)
        own[...] = grad
        sum_first.step(i, lambda: own[...])
        poll_at("first", i, 4)
        return carry

    lax.fori_loop(0, 4, project_back, 0)

    poll("tail")

    for gather, total in (
        (gather_wo, wo_all.at[0:3]),
        (gather_cot, cot_all.at[0:768]),
        (gather_do, do_all.at[0:768]),
        (gather_ctx(0), ctx_all.at[0:3]),
    ):
        remote(total, total, gather.send, gather.recv(0), core).wait_send()
    for block in blocks:
        block.close()
    for k, whole in enumerate((down_hbm, up_hbm, out_hbm, qkv_hbm)):
        pltpu.make_async_copy(whole, whole, local_sem.at[k]).wait()
    for save in (save_block, save_input, save_sums):
        save.wait()


def finish_kernel(
    block_hbm, input_hbm, sums_hbm, down_hbm, up_hbm, out_hbm, qkv_hbm,
    block_out, input_grad, gain_first, shift_first, grad_qkv, grad_qv, grad_out, out_bias, gain_second, shift_second,
    grad_up, up_bias, grad_down, down_bias,
    block_v, input_v, sums, down_v, up_v, out_v, qkv_v, block_w, input_w, down_w, up_w, out_w, qkv_w,
    in_sem, out_sem,
):
    share = block_out.shape[0]
    pairs = (
        (down_hbm, down_v), (up_hbm, up_v), (qkv_hbm, qkv_v), (block_hbm, block_v), (input_hbm, input_v),
        (out_hbm, out_v), (sums_hbm, sums),
    )
    loads = [pltpu.make_async_copy(src, dst, in_sem.at[k]) for k, (src, dst) in enumerate(pairs)]
    for load in loads:
        load.start()
    stores = []

    def save(src, dst):
        stores.append(pltpu.make_async_copy(src, dst, out_sem.at[len(stores)]))
        stores[-1].start()

    def widen(source, p, put):
        quarter = source.shape[3]
        for h in range(2):
            for c in range(4):
                put(slice(c * quarter, (c + 1) * quarter), slice(h * 384, (h + 1) * 384), source[p, h, c].astype(f32))

    for k, (source, wide, target) in enumerate(((down_v, down_w, grad_down), (up_v, up_w, grad_up))):
        loads[k].wait()
        for p in range(3):

            def put(r, lanes, value):
                wide[p * B + r.start : p * B + r.stop, lanes] = value

            widen(source, p, put)
        save(wide, target)
    loads[2].wait()
    for p in range(3):

        def put(r, lanes, value):
            qkv_w[p, r, lanes] = value

        widen(qkv_v, p, put)
    save(qkv_w, grad_qkv)
    for k, source, wide, target in ((3, block_v, block_w, block_out), (4, input_v, input_w, input_grad)):
        loads[k].wait()
        wide[...] = source[0:share, :]
        save(wide, target)
    loads[5].wait()

    def put(r, lanes, value):
        out_w[r, lanes] = value

    widen(out_v, 0, put)
    save(out_w, grad_out)
    loads[6].wait()
    for r, ref in enumerate((gain_first, shift_first, gain_second, shift_second, out_bias, down_bias)):
        ref[...] = sums[r, :]
    up_bias[...] = sums[8, :]
    grad_qv[0:1, :] = sums[9:10, 0:192]
    grad_qv[1:2, :] = sums[9:10, 256:448]
    for store in stores:
        store.wait()


def per_device(
    inputs, image_of_row, gain_first, shift_first, qkv_weight, qv_bias, out_weight, out_bias, gain_second,
    shift_second, up_weight, up_bias, down_weight, down_bias, cotangent,
):
    share = cotangent.shape[0]
    vmem, anyspace = (pl.BlockSpec(memory_space=m) for m in (pltpu.VMEM, pl.ANY))

    def shape(*dims, dtype=bf16):
        return pltpu.VMEM(dims, dtype)

    dma = pltpu.SemaphoreType.DMA

    def block_scratch(first_y, r):
        over = shape(4, r, 384) if first_y else shape(r, 384)
        along = shape(3, r, 384) if first_y else shape(2, 3, r, 384)
        return [shape(2, 4, r, 384), over, along, along, shape(2, 4, r, 384), dma((3,)), dma((8,))]

    scratch = [
        shape(1024, 768), shape(272, 768, dtype=f32), shape(1024, 768),
        shape(1024, 192), shape(1024, 192), shape(192, 1024), shape(192, 1024),
        shape(4, 192, 768), shape(4, 768, 192),
        shape(1024, B, dtype=i32), shape(4, 8, B, dtype=i32),
        shape(3, TOP, 768), shape(1024, 768), shape(4, 3, 8, B, dtype=f32),
        shape(192, 1024), shape(4, 4, 384, 128), shape(4, 192, 768), shape(1024, 768),
        shape(1024, 768), shape(1024, 768), shape(1024, 768), shape(1024, 768),
        shape(192, 768), shape(768, 192), shape(8, 768, dtype=f32),
        shape(1024, 192, dtype=f32), shape(1024, 192, dtype=f32), shape(B, 768, dtype=f32),
        shape(3, B, 768), shape(2, B, 768), shape(B, 768),
        shape(3, B, 768), shape(2, B, 768), shape(B, 768), shape(B, 768, dtype=f32),
        shape(8, 768, dtype=f32),
        shape(16, 768, dtype=f32), shape(4, 16, 768, dtype=f32), shape(16, 768, dtype=f32), shape(4, 16, 768, dtype=f32),
    ]
    one, three = dma((1,)), dma((3,))
    scratch += [one, three, one, three, one, dma((4, 3)), one, three] + [one, three] * 3
    scratch += [three, dma((7,)), dma((7,)), dma((15,))]
    scratch += [shape(4 * share, 768), shape(3, 192, 768), shape(768, 768), shape(768, 768), shape(share, 768)]
    scratch += [[shape(768)] * 7, shape(2, 192), shape(B, 768, dtype=f32), shape(B, 768, dtype=f32)]
    scratch += [shape(16, 768, dtype=f32), pltpu.SMEM(image_of_row.shape, i32)]
    scratch += [[block_scratch(first_y, r) for first_y, r in zip(FIRST_Y, QUARTER)]]
    results = pl.pallas_call(
        layer_kernel,
        out_shape=[
            jax.ShapeDtypeStruct((B, 768), f32),
            jax.ShapeDtypeStruct((B, 768), f32),
            jax.ShapeDtypeStruct((16, 768), f32),
            jax.ShapeDtypeStruct((3, 2, 4, 64, 384), bf16),
            jax.ShapeDtypeStruct((3, 2, 4, 64, 384), bf16),
            jax.ShapeDtypeStruct((1, 2, 4, 48, 384), bf16),
            jax.ShapeDtypeStruct((3, 2, 4, 48, 384), bf16),
        ],
        in_specs=[anyspace] * 15,
        out_specs=[anyspace] * 7,
        scratch_shapes=scratch,
        compiler_params=pltpu.CompilerParams(
            collective_id=0, has_side_effects=True, vmem_limit_bytes=60 * 2**20
        ),
        name="layer",
    )(
        inputs, image_of_row, gain_first, shift_first, qv_bias, out_bias, gain_second, shift_second, up_bias, down_bias,
        jnp.swapaxes(qkv_weight, 1, 2), out_weight, up_weight, down_weight, cotangent,
    )

    def out(*dims):
        return jax.ShapeDtypeStruct(dims, f32)

    wide = [shape(share, 768, dtype=f32)] * 2 + [shape(768, 768, dtype=f32)] * 2
    outputs = pl.pallas_call(
        finish_kernel,
        out_shape=[
            out(share, 768), out(share, 768), out(768), out(768), out(3, 192, 768), out(2, 192), out(192, 768),
            out(768), out(768), out(768), out(768, 768), out(768), out(768, 768), out(768),
        ],
        in_specs=[anyspace] * 7,
        out_specs=[anyspace if k in (0, 1, 4, 6, 10, 12) else vmem for k in range(14)],
        scratch_shapes=[pltpu.VMEM(r.shape, r.dtype) for r in results]
        + wide + [shape(192, 768, dtype=f32), shape(3, 192, 768, dtype=f32), dma((7,)), dma((6,))],
        compiler_params=pltpu.CompilerParams(vmem_limit_bytes=60 * 2**20),
        name="finish",
    )(*results)
    return (*outputs[:4], jnp.swapaxes(outputs[4], 1, 2), *outputs[5:])


def solution(mesh):
    return jax.shard_map(
        per_device,
        mesh=mesh,
        in_specs=(
            P("dp", None),
            P("dp"),
            P(),
            P(),
            P(None, None, "mp"),
            P(None, "mp"),
            P("mp", None),
            P(),
            P(),
            P(),
            P(None, "mp"),
            P("mp"),
            P("mp", None),
            P(),
            P(("dp", "mp"), None),
        ),
        out_specs=(
            P(("dp", "mp"), None),
            P(("dp", "mp"), None),
            P(),
            P(),
            P(None, None, "mp"),
            P(None, "mp"),
            P("mp", None),
            P(),
            P(),
            P(),
            P(None, "mp"),
            P("mp"),
            P("mp", None),
            P(),
        ),
        check_vma=False,
    )
```

```python
import functools

import jax
import jax.numpy as jnp
from jax import lax
from jax.experimental import pallas as pl
from jax.experimental.pallas import tpu as pltpu
from jax.sharding import PartitionSpec as P

f32, bf16, i32 = jnp.float32, jnp.bfloat16, jnp.int32
MESH = pl.DeviceIdType.MESH
NN = (((1,), (0,)), ((), ()))
NT = (((1,), (1,)), ((), ()))
TN = (((0,), (0,)), ((), ()))
HD = 64
P_LO = 196
EPSILON = 1e-06
B = 256
TOP = 832
BIG = 4 * P_LO


def dot(left, right, dims):
    return lax.dot_general(left, right, dims, preferred_element_type=f32)


def rows(start, size=B):
    return pl.ds(pl.multiple_of(start * size, size), size)


def layer_hat(values):
    center = values - jnp.mean(values, axis=1, keepdims=True)
    factor = lax.rsqrt(jnp.mean(center * center, axis=1, keepdims=True) + EPSILON)
    return center * factor, factor


def layer_back(grad_hat, normed, factor):
    first = jnp.mean(grad_hat, axis=1, keepdims=True)
    second = jnp.mean(grad_hat * normed, axis=1, keepdims=True)
    return factor * (grad_hat - first - normed * second)


def column_sum(values):
    return jnp.sum(values, axis=0, keepdims=True)


def remote(src, dst, send, recv, device):
    return pltpu.make_async_remote_copy(
        src_ref=src, dst_ref=dst, send_sem=send, recv_sem=recv, device_id=device, device_id_type=MESH
    )


class Gather:
    def __init__(self, place, view, send, recv):
        self.me, self.core, self.across = place
        self.view, self.send, self.recv = view, send, recv

    def copy(self, slot, k, device, part=None):
        view = self.view(slot) if part is None else self.view(slot).at[part]
        return remote(view, view, self.send, self.recv(k), device)

    def start(self):
        self.copy(self.me, 1, self.across).start()
        self.copy(self.me, 0, self.core).start()

    def forward(self):
        slot = self.me ^ 2
        self.copy(slot, 1, self.across).wait_recv()
        self.copy(slot, 2, self.core).start()

    def land_core(self):
        self.copy(self.me ^ 1, 0, self.core).wait_recv()

    def land_far(self):
        self.copy(self.me ^ 3, 2, self.core).wait_recv()


class Scatter:
    def __init__(self, place, out, both, far, own, send, recv):
        self.me, self.core, self.across = place
        self.out, self.both, self.far, self.own = out, both, far, own
        self.send, self.recv = send, recv

    def copy(self, k):
        src = self.out.at[k]
        dst = self.far if k == 1 else self.both.at[k // 2]
        return remote(src, dst, self.send, self.recv.at[k], self.across if k == 1 else self.core)

    def step(self, i, value, hold=False):
        @pl.when(i == 0)
        def _():
            self.out[0] = value().astype(bf16)
            self.copy(0).start()

        @pl.when(i == 1)
        def _():
            if hold:
                self.out[1] = value().astype(bf16)
            else:
                self.copy(0).wait_recv()
                self.out[1] = (value() + self.both[0].astype(f32)).astype(bf16)
                self.copy(1).start()

        @pl.when(i == 2)
        def _():
            self.out[2] = value().astype(bf16)
            self.copy(2).start()

        @pl.when(i == 3)
        def _():
            self.own[...] = value()

    def release(self):
        self.copy(0).wait_recv()
        self.out[1] = (self.out[1].astype(f32) + self.both[0].astype(f32)).astype(bf16)
        self.copy(1).start()

    def finish(self):
        self.copy(2).wait_recv()
        self.copy(1).wait_recv()
        total = self.own[...] + self.both[1].astype(f32) + self.far[...].astype(f32)
        remote(self.out, self.out, self.send, self.recv.at[0], self.core).wait_send()
        return total


class Reduce:
    def __init__(self, spot, first_y, refs):
        self.zi, self.yi, self.over, self.above, self.below = spot
        self.first_y = first_y
        self.part, self.ybuf, self.up, self.down, self.whole, self.send, self.recv = refs

    def copy(self, src, dst, k, slot, device):
        return remote(src, dst, self.send.at[k], self.recv.at[slot], device)

    def begin(self, condition, make):
        if condition is None:
            make().start()
        else:
            pl.when(condition())(lambda: make().start())

    def close(self):
        all_along = self.whole.at[self.yi] if self.first_y else self.whole
        all_over = self.whole if self.first_y else self.whole.at[:, 0]
        pl.when(self.zi < 3)(lambda: self.copy(all_along, all_along, 1, 1, self.above).wait_send())
        pl.when(self.zi > 0)(lambda: self.copy(all_along, all_along, 2, 2, self.below).wait_send())
        self.copy(all_over, all_over, 0, 0, self.over).wait_send()

    def chunks(self, first, count):
        return self.part.at[self.yi if self.first_y else slice(None), pl.ds(first, count)]

    def rising(self, first, count):
        span = pl.ds(first - 1, count)
        return self.up.at[span] if self.first_y else self.up.at[:, span]

    def falling(self, first, count):
        span = pl.ds(first, count)
        return self.down.at[span] if self.first_y else self.down.at[:, span]

    def result(self, chunk):
        return self.whole.at[self.yi if self.first_y else slice(None), chunk]

    def copy_up(self, first, count, src):
        return self.copy(src, self.rising(first, count), 1, 1, self.above)

    def copy_down(self, first, count, src):
        return self.copy(src, self.falling(first, count), 2, 2, self.below)

    def at(self, z):
        return lambda: self.zi == z

    def hop(self, n):
        up_first, down_count = n, 4 - n

        def up_view():
            return self.chunks(n, 4 - n) if n == 1 else self.rising(n, 4 - n)

        def down_view():
            return self.chunks(0, 4 - n) if n == 1 else self.falling(0, 4 - n)

        if n > 1:

            @pl.when(self.zi == n - 1)
            def _():
                came = self.rising(n - 1, 5 - n)
                self.copy_up(n - 1, 5 - n, came).wait_recv()
                view, own = self.rising(n, 4 - n), self.chunks(n, 4 - n)
                view[...] = (view[...].astype(f32) + own[...].astype(f32)).astype(bf16)

            @pl.when(self.zi == 4 - n)
            def _():
                came = self.falling(0, 5 - n)
                self.copy_down(0, 5 - n, came).wait_recv()
                view, own = self.falling(0, 4 - n), self.chunks(0, 4 - n)
                view[...] = (view[...].astype(f32) + own[...].astype(f32)).astype(bf16)

        self.begin(self.at(n - 1), lambda: self.copy_up(up_first, 4 - n, up_view()))
        self.begin(self.at(4 - n), lambda: self.copy_down(0, down_count, down_view()))

    def total(self, store):
        def plain(view):
            return view[...].astype(f32)

        @pl.when(self.zi == 0)
        def _():
            self.copy_down(0, 1, self.falling(0, 1)).wait_recv()
            store(0, plain(self.chunks(0, 1)) + plain(self.falling(0, 1)))

        @pl.when(self.zi == 3)
        def _():
            self.copy_up(3, 1, self.rising(3, 1)).wait_recv()
            store(3, plain(self.chunks(3, 1)) + plain(self.rising(3, 1)))

        for z in (1, 2):

            @pl.when(self.zi == z)
            def _(z=z):
                value = plain(self.chunks(z, 1)) + plain(self.rising(z, 1)) + plain(self.falling(z, 1))
                store(z, value)

    def back(self, d):
        for sign, k, ahead, room in ((-1, 1, self.above, lambda: self.zi < 3), (1, 2, self.below, lambda: self.zi > 0)):

            def here(sign=sign):
                return self.zi >= d if sign < 0 else self.zi <= 3 - d

            def move(sign=sign, k=k, ahead=ahead):
                chunk = self.zi + sign * d
                view = self.result(chunk)
                return self.copy(view, view, k, 3 + chunk, ahead)

            if d > 0:

                @pl.when(here())
                def _():
                    move().wait_recv()

            if d < 3:
                self.begin(lambda room=room, here=here: room() & here(), move)
            if self.first_y and (d > 0 or sign < 0):
                self.begin(here, lambda sign=sign: self.copy_over(self.yi, self.zi + sign * d))

    def copy_over(self, half, chunk):
        view = self.whole.at[half, chunk]
        return self.copy(view, view, 0, 7, self.over)

    def sum_over(self):
        if self.first_y:
            return self.copy(self.part.at[1 - self.yi], self.ybuf, 0, 0, self.over)
        return self.copy(self.part.at[1 - self.yi, self.zi], self.ybuf, 0, 0, self.over)

    def stage(self, k):
        if self.first_y:
            if k == 0:
                self.begin(None, self.sum_over)
            elif k == 1:
                self.sum_over().wait_recv()

                def add(c, carry):
                    value = self.part[self.yi, c].astype(f32) + self.ybuf[c].astype(f32)
                    self.part[self.yi, c] = value.astype(bf16)
                    return carry

                lax.fori_loop(0, 4, add, 0)
                self.hop(1)
            elif k in (2, 3):
                self.hop(k)
            elif k == 4:

                def store(z, value):
                    self.whole[self.yi, z] = value[0].astype(bf16)

                self.total(store)
                self.back(0)
            elif k in (5, 6, 7):
                self.back(k - 4)
            else:
                other = self.whole.at[1 - self.yi]
                self.copy(other, other, 0, 7, self.over).wait_recv()
        else:
            if k in (0, 1, 2):
                self.hop(k + 1)
            elif k == 3:

                def store(z, value):
                    self.part[:, z] = value[:, 0].astype(bf16)

                self.total(store)
                self.begin(None, self.sum_over)
            elif k == 4:
                self.sum_over().wait_recv()
                value = self.part[self.yi, self.zi].astype(f32) + self.ybuf[...].astype(f32)
                self.whole[self.yi, self.zi] = value.astype(bf16)
                self.begin(None, lambda: self.copy_over(self.yi, self.zi))
            elif k == 5:
                self.copy_over(1 - self.yi, self.zi).wait_recv()
                self.back(0)
            else:
                self.back(k - 5)


FIRST_Y = (True, False, True, True, True, True, True, True, True, False)
QUARTER = (64,) * 6 + (48,) * 4
STAGES = 9

POLLS = {
    "down0": ((0, 0),),
    "down1": ((1, 0),),
    "down2": ((2, 0),),
    "mid3": ((0, 1),),
    "up0": ((3, 0),),
    "up1": ((4, 0),),
    "up2": ((5, 0), (1, 1),),
    "mlp2": ((2, 1),),
    "rs1": ((0, 2),),
    "own": ((3, 1), (2, 2), (1, 2),),
    "attend0": ((0, 3),),
    "after0": ((4, 1),),
    "prep1": ((3, 2), (2, 3), (1, 3),),
    "attend1": ((0, 4),),
    "after1": ((5, 1),),
    "do": ((2, 4), (4, 2), (1, 4), (3, 3),),
    "prep2": ((0, 5),),
    "attend2": ((3, 4), (1, 5), (5, 2),),
    "after2": ((4, 3), (2, 5),),
    "prep3": ((0, 6),),
    "attend3": ((3, 5),),
    "out": ((6, 0), (1, 6),),
    "qkv0": ((7, 0),),
    "qkv1": ((8, 0), (4, 4),),
    "qkv2": ((9, 0),),
    "first0": ((5, 3),),
    "first1": ((2, 6), (0, 7), (3, 6),),
    "tail": ((11, 0), (10, 0), (1, 7), (6, 1), (4, 5), (5, 4), (9, 1), (2, 7), (7, 1), (3, 7), (6, 2), (1, 8), (8, 1), (4, 6), (12, 0), (9, 2), (7, 2), (5, 5), (0, 8), (10, 1), (6, 3), (4, 7), (8, 2), (9, 3), (2, 8), (7, 3), (3, 8), (5, 6), (6, 4), (7, 4), (8, 3), (5, 7), (6, 5), (4, 8), (10, 2), (7, 5), (9, 4), (8, 4), (6, 6), (5, 8), (9, 5), (10, 3), (7, 6), (6, 7), (8, 5), (9, 6), (7, 7), (6, 8), (8, 6), (9, 7), (7, 8), (8, 7), (9, 8), (8, 8),),
}


def layer_kernel(
    x_hbm, ids_hbm, gain_a, shift_a, bias_qv, bias_out, gain_b, shift_b, bias_up, bias_down,
    wqkv_hbm, wo_hbm, wup_hbm, wdn_hbm, cot_hbm,
    block_hbm, input_hbm, sums_hbm, down_hbm, up_hbm, out_hbm, qkv_hbm,
    xp, stage, a1, keys, values, keys_t, values_t, qz_t, qz, kid, qid, probs, probs_last, rinv, ctx_t, ctx_all,
    wo_all, cot_all, a2, gate, du, do_all, dcz_t, dcz, delta, dk, dv, own,
    rs_out, rs_both, rs_far, ms_out, ms_both, ms_far, m_own,
    vec_ref, acc, v_mp, v_y, v_z,
    wo_send, wo_recv, cot_send, cot_recv, ctx_send, ctx_recv, do_send, do_recv,
    rs_send, rs_recv, ms_send, ms_recv, rt_send, rt_recv,
    v_send, v_recv, local_sem, load_sem, x_ref, wqkv_ref, wup_ref, wdn_ref, cot_ref, vec_raw, qv_raw,
    block_ref, input_ref, sums_ref, ids_ref, block_refs,
):
    dp, me = lax.axis_index("dp"), lax.axis_index("mp")
    core, across, diagonal = (dp, me ^ 1), (dp, me ^ 2), (dp, me ^ 3)
    yi, zi = dp & 1, (dp >> 1) & 3
    ypeer = (dp ^ 1, me)
    zpeers = [(dp ^ (2 * j), me) for j in (1, 2, 3)]
    place = (me, core, across)
    base = dp & ~7
    above, below = (base + (((zi + 1) & 3) << 1) + yi, me), (base + (((zi + 3) & 3) << 1) + yi, me)
    spot = (zi, yi, ypeer, above, below)
    share = cot_hbm.shape[0]

    barrier = pltpu.get_barrier_semaphore()
    partners = [core, across, diagonal, ypeer] + zpeers
    for partner in partners:
        pl.semaphore_signal(barrier, inc=1, device_id=partner, device_id_type=MESH)

    def vec(r, width=None):
        return vec_ref[r : r + 1, :] if width is None else vec_ref[r : r + 1, width[0] : width[1]]

    pairs = [(wo_hbm, wo_all.at[me]), (cot_hbm, cot_ref), (x_hbm, x_ref), (bias_qv, qv_raw)]
    pairs += list(zip((gain_a, shift_a, bias_out, gain_b, shift_b, bias_up, bias_down), vec_raw))
    pairs += [(wqkv_hbm, wqkv_ref), (wup_hbm, wup_ref), (wdn_hbm, wdn_ref), (ids_hbm, ids_ref)]
    loads = [pltpu.make_async_copy(src, dst, load_sem.at[k]) for k, (src, dst) in enumerate(pairs)]
    for load in loads:
        load.start()
    pl.semaphore_wait(barrier, len(partners))

    gather_wo = Gather(place, lambda s: wo_all.at[s], wo_send.at[0], lambda k: wo_recv.at[k])
    loads[0].wait()
    gather_wo.start()

    gather_cot = Gather(place, lambda s: cot_all.at[rows(s)], cot_send.at[0], lambda k: cot_recv.at[k])

    loads[1].wait()
    stage[240:256, :] = jnp.zeros((16, 768), f32)
    stage[0:share, :] = cot_ref[...].astype(f32)
    cot_all[rows(me), :] = stage[0:B, :].astype(bf16)
    gather_cot.copy(me, 0, core).start()
    acc[...] = jnp.zeros(acc.shape, f32)
    for k in range(3, 11):
        loads[k].wait()
    for r, ref in enumerate(vec_raw):
        vec_ref[r : r + 1, :] = ref[...].astype(f32).reshape(1, 768)
    vec_ref[7:8, 0:192] = qv_raw[0:1, :].astype(f32)
    vec_ref[7:8, 256:448] = qv_raw[1:2, :].astype(f32)
    loads[2].wait()

    row_in = lax.broadcasted_iota(i32, (B, 768), 0)
    for s in range(4):
        first = s * share // 16 * 16
        last = min(first + 272, 4 * share)
        stage[0 : last - first, :] = x_ref[first:last, :].astype(f32)
        moved = stage[s * share - first : s * share - first + B, :]
        xp[s * B : (s + 1) * B, :] = jnp.where(row_in < share, moved, 0.0).astype(bf16)

    loads[14].wait()
    two_images = (ids_ref[0] == ids_ref[BIG - 1]).astype(i32)

    def image_of(index, shard, pad):
        place_of = index + shard * share
        small = jnp.zeros_like(index)
        for k in range(1, 5):
            small = small + (place_of >= k * P_LO).astype(i32)
        large = (place_of >= BIG).astype(i32)
        image = small * (1 - two_images) + large * two_images
        return jnp.where(index < share, image, pad)

    def images(s, carry):
        kid[rows(s), :] = image_of(lax.broadcasted_iota(i32, (B, B), 0), s, -1)
        qid[s] = image_of(lax.broadcasted_iota(i32, (8, B), 1), s, -2)
        qz_t[s] = jnp.zeros(qz_t.shape[1:], bf16)
        return carry

    lax.fori_loop(0, 4, images, 0)

    lane_head = lax.broadcasted_iota(i32, (B, 192), 1) // HD

    def project(s, carry):
        span = rows(s)
        hat, _ = layer_hat(xp[span, :].astype(f32))
        act = (hat * vec(0) + vec(1)).astype(bf16)
        a1[span, :] = act
        q = (dot(act, wqkv_ref[0], NT) + vec(7, (0, 192))).astype(bf16)
        k = dot(act, wqkv_ref[1], NT).astype(bf16)
        v = (dot(act, wqkv_ref[2], NT) + vec(7, (256, 448))).astype(bf16)
        keys[span, :] = k
        values[span, :] = v
        keys_t[:, span] = k.T
        values_t[:, span] = v.T
        q = q.astype(f32) * HD**-0.5
        qt = q.astype(bf16).T
        for h in range(3):
            qz_t[s, h * HD : (h + 1) * HD, h * B : (h + 1) * B] = qt[h * HD : (h + 1) * HD, :]
            qz[s, h * B : (h + 1) * B, :] = jnp.where(lane_head == h, q, 0.0).astype(bf16)
        return carry

    loads[11].wait()
    lax.fori_loop(0, 4, project, 0)

    def gather_ctx(s):
        return Gather(
            place, lambda j: ctx_all.at[j, s], ctx_send.at[0], lambda k: ctx_recv.at[s, k]
        )

    def attend(s, low, high, qlow, qhigh):
        width = qhigh - qlow
        wanted = qz_t[s]
        if width < B:
            wanted = jnp.concatenate([wanted[:, h * B + qlow : h * B + qhigh] for h in range(3)], axis=1)
        scores = dot(keys[low:high, :], wanted, NN)
        same = kid[low:high, qlow:qhigh] == qid[s, 0:1, qlow:qhigh]
        scores = jnp.where(jnp.concatenate([same] * 3, axis=1), scores, -1e30)
        weights = jnp.exp(scores - jnp.max(scores, axis=0, keepdims=True))
        inverse = 1.0 / jnp.sum(weights, axis=0, keepdims=True)
        weights = weights.astype(bf16)
        mixed = dot(values_t[:, low:high], weights, NN) * inverse
        for h in range(3):
            rinv[s, h, 0:1, qlow:qhigh] = inverse[:, h * width : (h + 1) * width]
        heads = [mixed[h * HD : (h + 1) * HD, h * width : (h + 1) * width] for h in range(3)]
        return weights, jnp.concatenate(heads, axis=0).astype(bf16)

    def send_ctx(s):
        span = rows(s)
        block = ctx_t[:, span]
        ctx_all[me, s, 0:B, :] = block[0:128, :].T
        last = jnp.concatenate([block[128:192, 0:128], block[128:192, 128:256]], axis=0)
        ctx_all[me, s, B : B + 128, :] = last.T
        gather_ctx(s).start()

    def attend_top(s, carry):
        probs[s], ctx_t[:, rows(s)] = attend(s, 0, TOP, 0, B)
        send_ctx(s)

        @pl.when(s == 1)
        def _():
            gather_wo.forward()

        return carry

    lax.fori_loop(0, 3, attend_top, 0)

    left, ctx_t[:, 768:896] = attend(3, 0, 1024, 0, 128)
    right, ctx_t[:, 896:1024] = attend(3, 768, 1024, 128, 256)
    for h in range(3):
        probs_last[:, h * B : h * B + 128] = left[:, h * 128 : (h + 1) * 128]
        probs_last[0:768, h * B + 128 : (h + 1) * B] = jnp.zeros((768, 128), bf16)
        probs_last[768:1024, h * B + 128 : (h + 1) * B] = right[:, h * 128 : (h + 1) * 128]
    send_ctx(3)

    for q in range(4):
        gather_cot.copy(me, 1, across, pl.ds(q * 64, 64)).start()
    gather_wo.land_core()
    gather_wo.land_far()
    loads[12].wait()
    loads[13].wait()

    zeros_w = jnp.zeros((HD, 768), bf16)

    def middle(s, carry):
        span = rows(s)
        ctx = gather_ctx(s)
        ctx.forward()
        ctx.land_core()
        ctx.land_far()
        left = jnp.concatenate([ctx_all[j, s, 0:B, :] for j in range(4)], axis=1)
        last = jnp.concatenate([ctx_all[j, s, B : B + 128, :] for j in range(4)], axis=1)
        w_left = jnp.concatenate([wo_all[j, 0:128, :] for j in range(4)], axis=0)
        w_tail = [wo_all[j, 128:192, :] for j in range(4)]
        w_upper = jnp.concatenate([piece for w in w_tail for piece in (w, zeros_w)], axis=0)
        w_lower = jnp.concatenate([piece for w in w_tail for piece in (zeros_w, w)], axis=0)
        branch = dot(left, w_left, NN) + jnp.concatenate(
            [dot(last, w_upper, NN), dot(last, w_lower, NN)], axis=0
        )
        h = xp[span, :].astype(f32) + (branch + vec(2))

        @pl.when(s == me)
        def _():
            block_ref[...] = h

        hat, _ = layer_hat(h)
        act = (hat * vec(3) + vec(4)).astype(bf16)
        a2[span, :] = act
        u = dot(act, wup_ref[...], NN) + vec(5)
        cdf = 0.5 * (1.0 + lax.erf(u * 0.7071067811865476))
        gate[span, :] = (u * cdf).astype(bf16)
        du[span, :] = (cdf + u * (0.3989422804014327 * jnp.exp(-0.5 * (u * u)))).astype(bf16)
        return carry

    lax.fori_loop(0, 4, middle, 0)

    gather_cot.forward()
    gather_cot.land_core()
    gather_cot.land_far()

    blocks = [Reduce(spot, first_y, refs) for first_y, refs in zip(FIRST_Y, block_refs)]
    homes = [down_hbm.at[p] for p in range(3)] + [up_hbm.at[p] for p in range(3)]
    homes += [out_hbm.at[0]] + [qkv_hbm.at[p] for p in range(3)]
    tensor = (0, 0, 0, 1, 1, 1, 2, 3, 3, 3)
    saves = [pltpu.make_async_copy(blocks[p].whole, homes[p], local_sem.at[tensor[p]]) for p in range(10)]
    save_block = pltpu.make_async_copy(block_ref, block_hbm, local_sem.at[4])
    save_input = pltpu.make_async_copy(input_ref, input_hbm, local_sem.at[5])
    save_sums = pltpu.make_async_copy(sums_ref, sums_hbm, local_sem.at[6])

    def sum_copy(slot, k, device, ref=v_mp):
        view = ref.at[slot]
        return remote(view, view, v_send.at[0 if k < 3 else 2], v_recv.at[k], device)

    def sum_y():
        return remote(acc, v_y, v_send.at[1], v_recv.at[3], ypeer)

    def sums(k):
        if k == 0:
            v_mp[me] = acc[...]
            for j in (1, 2, 3):
                sum_copy(me, j - 1, (dp, me ^ j)).start()
        elif k == 1:
            for j in (1, 2, 3):
                sum_copy(me ^ j, j - 1, (dp, me ^ j)).wait_recv()
            acc[0:8, :] = v_mp[0, 0:8, :] + v_mp[1, 0:8, :] + v_mp[2, 0:8, :] + v_mp[3, 0:8, :]
            sum_y().start()
        elif k == 2:
            sum_y().wait()
            v_z[zi] = acc[...] + v_y[...]
            for j in (1, 2, 3):
                sum_copy(zi, 3 + j, zpeers[j - 1], v_z).start()
        else:
            for j in (1, 2, 3):
                sum_copy(zi ^ j, 3 + j, zpeers[j - 1], v_z).wait_recv()
            sums_ref[...] = v_z[0] + v_z[1] + v_z[2] + v_z[3]
            save_sums.start()
            sum_copy(slice(0, 3), 0, core).wait_send()
            sum_copy(slice(0, 3), 4, core, v_z).wait_send()

    sum_in = Scatter(place, rs_out, rs_both, rs_far, own, rs_send.at[0], rs_recv)
    sum_out = Scatter(place, ms_out, ms_both, ms_far, m_own, ms_send.at[0], ms_recv)
    sum_first = Scatter(place, rs_out, rs_both, rs_far, own, rt_send.at[0], rt_recv)

    def finish_block(k):
        block_ref[...] = block_ref[...] + (sum_out.finish() + vec(6))
        save_block.start()

    def finish_input(k):
        grad = sum_first.finish()
        hat, factor = layer_hat(xp[rows(me), :].astype(f32))
        input_ref[...] = input_ref[...] + layer_back(grad * vec(0), hat, factor)
        save_input.start()

    others = (sums, finish_block, finish_input)

    def poll(name):
        for p, k in POLLS.get(name, ()):
            if p >= len(blocks):
                others[p - len(blocks)](k)
                continue
            blocks[p].stage(k)
            if k == STAGES - 1:
                saves[p].start()

    def poll_at(prefix, index, count):
        for n in range(count):
            if POLLS.get(f"{prefix}{n}"):
                pl.when(index == n)(lambda n=n: poll(f"{prefix}{n}"))

    def stage_grad(p, piece):
        quarter = QUARTER[p]
        for h in range(2):
            for c in range(4):
                part = piece[c * quarter : (c + 1) * quarter, h * 384 : (h + 1) * 384]
                blocks[p].part[h, c] = part.astype(bf16)

    for t in range(3):
        stage_grad(t, dot(gate[:, t * B : (t + 1) * B], cot_all[...], TN))
        poll(f"down{t}")

    def hidden_back(i, carry):
        span = rows(me ^ (3 - i))
        grad_u = (dot(cot_all[span, :], wdn_ref[...], NT) * du[span, :].astype(f32)).astype(bf16)
        du[span, :] = grad_u
        acc[8:9, :] += column_sum(grad_u.astype(f32))
        own[...] = dot(grad_u, wup_ref[...], NT)
        sum_in.step(i, lambda: own[...])
        poll_at("mid", i, 4)
        return carry

    lax.fori_loop(0, 4, hidden_back, 0)

    for t in range(3):
        stage_grad(3 + t, dot(a2[:, t * B : (t + 1) * B], du[...], TN))
        poll(f"up{t}")
    poll("up2b")

    def project_down(i, carry):
        s = me ^ (3 - i)
        m_own[...] = dot(gate[rows(s), :], wdn_ref[...], NN)
        sum_out.step(i, lambda: m_own[...], hold=True)
        poll_at("mlp", i, 4)
        return carry

    lax.fori_loop(0, 4, project_down, 0)

    poll("rs1")
    grad_act = sum_in.finish()
    hat, factor = layer_hat(block_ref[...])
    acc[2:3, :] = column_sum(grad_act * hat)
    acc[3:4, :] = column_sum(grad_act)
    cot_own = cot_all[rows(me), :].astype(f32)
    grad_h = cot_own + layer_back(grad_act * vec(3), hat, factor)
    input_ref[...] = grad_h
    grad_branch = grad_h.astype(bf16)
    do_all[rows(me), :] = grad_branch
    gather_do = Gather(place, lambda s: do_all.at[rows(s)], do_send.at[0], lambda k: do_recv.at[k])
    gather_do.start()
    acc[4:5, :] = column_sum(grad_branch.astype(f32))
    acc[5:6, :] = column_sum(cot_own)

    poll("own")
    sum_out.release()

    dq, dkb, dvb = (slice(256 * k, 256 * k + 192) for k in range(3))
    dk[...] = jnp.zeros(dk.shape, f32)
    dv[...] = jnp.zeros(dv.shape, f32)

    def back_heads(weights, low, high, wanted, center):
        width = weights.shape[1] // 3
        grad_scores = weights.astype(f32) * (dot(values[low:high, :], wanted, NN) - center)
        grad_scores = grad_scores.astype(bf16)
        mixed = dot(keys_t[:, low:high], grad_scores, NN)
        heads = [mixed[h * HD : (h + 1) * HD, h * width : (h + 1) * width] for h in range(3)]
        return grad_scores, jnp.concatenate(heads, axis=0)

    def back_block(i, carry):
        s = me ^ i
        span = rows(s)

        @pl.when(i == 1)
        def _():
            gather_do.land_core()

        @pl.when(i == 2)
        def _():
            poll("do")
            gather_do.forward()

        @pl.when(i == 3)
        def _():
            gather_do.land_far()

        grad_ctx = dot(wo_all[me], do_all[span, :], NT).astype(bf16).astype(f32)
        for h in range(3):
            here = slice(h * HD, (h + 1) * HD)
            scaled = (grad_ctx[here, :] * rinv[s, h, 0:1, :]).astype(bf16)
            delta[0:1, h * B : (h + 1) * B] = column_sum(scaled.astype(f32) * ctx_t[here, span].astype(f32))
            dcz_t[here, h * B : (h + 1) * B] = scaled
            turned = jnp.concatenate([scaled, jnp.zeros((HD, B), bf16)], axis=0).T.astype(f32)
            wide = jnp.concatenate([turned, turned], axis=1)[:, 0:192]
            if h == 1:
                wide = pltpu.roll(jnp.concatenate([turned, jnp.zeros((B, 128), f32)], axis=1), HD, 1)[:, 0:192]
            dcz[h * B : (h + 1) * B, :] = jnp.where(lane_head == h, wide, 0.0).astype(bf16)

        @pl.when(s != 3)
        def _():
            dv[0:TOP, :] += dot(probs[s], dcz[...], NN)

        @pl.when(s == 3)
        def _():
            dv[...] += dot(probs_last[...], dcz[...], NN)

        poll_at("prep", i, 4)

        @pl.when(s != 3)
        def _():
            probs[s], stage[0:192, 0:B] = back_heads(probs[s], 0, TOP, dcz_t[...], delta[0:1, :])

        @pl.when(s == 3)
        def _():
            def side(ref, low, high, qlow):
                parts = [ref[low:high, h * B + qlow : h * B + qlow + 128] for h in range(3)]
                return jnp.concatenate(parts, axis=1)

            for low, qlow in ((0, 0), (768, 128)):
                wanted, center = side(dcz_t, 0, 192, qlow), side(delta, 0, 1, qlow)
                grad_scores, grad_q = back_heads(side(probs_last, low, 1024, qlow), low, 1024, wanted, center)
                stage[0:192, qlow : qlow + 128] = grad_q
                for h in range(3):
                    lanes = slice(h * B + qlow, h * B + qlow + 128)
                    probs_last[low:1024, lanes] = grad_scores[:, h * 128 : (h + 1) * 128]

        poll_at("attend", i, 4)

        @pl.when(s != 3)
        def _():
            dk[0:TOP, :] += dot(probs[s], qz[s], NN)

        @pl.when(s == 3)
        def _():
            dk[...] += dot(probs_last[...], qz[s], NN)

        a2[span, dq] = (stage[0:192, 0:B] * HD**-0.5).T.astype(bf16)
        poll_at("after", i, 4)
        return carry

    dcz_t[...] = jnp.zeros(dcz_t.shape, bf16)
    lax.fori_loop(0, 4, back_block, 0)

    stage_grad(6, dot(ctx_t[...], do_all[...], NN))
    poll("out")
    a2[:, dkb] = dk[...].astype(bf16)
    a2[:, dvb] = dv[...].astype(bf16)
    for t, lanes in enumerate((dq, dkb, dvb)):
        stage_grad(7 + t, dot(a2[:, lanes], a1[...], TN))
        poll(f"qkv{t}")
    acc[9:10, 0:192] = column_sum(a2[:, dq].astype(f32))
    acc[9:10, 256:448] = column_sum(a2[:, dvb].astype(f32))

    def project_back(i, carry):
        s = me ^ (3 - i)
        span = rows(s)
        grad = dot(a2[span, dq], wqkv_ref[0], NN)
        grad = grad + dot(a2[span, dkb], wqkv_ref[1], NN)
        grad = grad + dot(a2[span, dvb], wqkv_ref[2], NN)
        hat, _ = layer_hat(xp[span, :].astype(f32))
        acc[0:1, :] += column_sum(grad * hat)
        acc[1:2, :] += column_sum(grad)
        own[...] = grad
        sum_first.step(i, lambda: own[...])
        poll_at("first", i, 4)
        return carry

    lax.fori_loop(0, 4, project_back, 0)

    poll("tail")

    for gather, total in (
        (gather_wo, wo_all.at[0:3]),
        (gather_cot, cot_all.at[0:768]),
        (gather_do, do_all.at[0:768]),
        (gather_ctx(0), ctx_all.at[0:3]),
    ):
        remote(total, total, gather.send, gather.recv(0), core).wait_send()
    for block in blocks:
        block.close()
    for k, whole in enumerate((down_hbm, up_hbm, out_hbm, qkv_hbm)):
        pltpu.make_async_copy(whole, whole, local_sem.at[k]).wait()
    for save in (save_block, save_input, save_sums):
        save.wait()


def finish_kernel(
    block_hbm, input_hbm, sums_hbm, down_hbm, up_hbm, out_hbm, qkv_hbm,
    block_out, input_grad, gain_first, shift_first, grad_qkv, grad_qv, grad_out, out_bias, gain_second, shift_second,
    grad_up, up_bias, grad_down, down_bias,
    block_v, input_v, sums, down_v, up_v, out_v, qkv_v, block_w, input_w, down_w, up_w, out_w, qkv_w,
    in_sem, out_sem,
):
    share = block_out.shape[0]
    pairs = [(down_hbm.at[p], down_v.at[p]) for p in range(3)] + [(up_hbm.at[p], up_v.at[p]) for p in range(3)]
    pairs += [(qkv_hbm.at[p], qkv_v.at[p]) for p in range(3)]
    pairs += [(block_hbm, block_v), (input_hbm, input_v), (out_hbm, out_v), (sums_hbm, sums)]
    loads = [pltpu.make_async_copy(src, dst, in_sem.at[k]) for k, (src, dst) in enumerate(pairs)]
    for load in loads:
        load.start()
    stores = []

    def save(src, dst):
        stores.append(pltpu.make_async_copy(src, dst, out_sem.at[len(stores)]))
        stores[-1].start()

    def widen(source, p, put):
        quarter = source.shape[3]
        for h in range(2):
            for c in range(4):
                put(slice(c * quarter, (c + 1) * quarter), slice(h * 384, (h + 1) * 384), source[p, h, c].astype(f32))

    for k, (source, wide, target) in enumerate(((down_v, down_w, grad_down), (up_v, up_w, grad_up))):
        for p in range(3):
            loads[3 * k + p].wait()

            def put(r, lanes, value):
                wide[p * B + r.start : p * B + r.stop, lanes] = value

            widen(source, p, put)
            save(wide.at[p * B : (p + 1) * B], target.at[p * B : (p + 1) * B])
    for p in range(3):
        loads[6 + p].wait()

        def put(r, lanes, value):
            qkv_w[p, r, lanes] = value

        widen(qkv_v, p, put)
        save(qkv_w.at[p], grad_qkv.at[p])
    for k, source, wide, target in ((9, block_v, block_w, block_out), (10, input_v, input_w, input_grad)):
        loads[k].wait()
        wide[...] = source[0:share, :]
        save(wide, target)
    loads[11].wait()

    def put(r, lanes, value):
        out_w[r, lanes] = value

    widen(out_v, 0, put)
    save(out_w, grad_out)
    loads[12].wait()
    for r, ref in enumerate((gain_first, shift_first, gain_second, shift_second, out_bias, down_bias)):
        ref[...] = sums[r, :]
    up_bias[...] = sums[8, :]
    grad_qv[0:1, :] = sums[9:10, 0:192]
    grad_qv[1:2, :] = sums[9:10, 256:448]
    for store in stores:
        store.wait()


def per_device(
    inputs, image_of_row, gain_first, shift_first, qkv_weight, qv_bias, out_weight, out_bias, gain_second,
    shift_second, up_weight, up_bias, down_weight, down_bias, cotangent,
):
    share = cotangent.shape[0]
    vmem, anyspace = (pl.BlockSpec(memory_space=m) for m in (pltpu.VMEM, pl.ANY))

    def shape(*dims, dtype=bf16):
        return pltpu.VMEM(dims, dtype)

    dma = pltpu.SemaphoreType.DMA

    def block_scratch(first_y, r):
        over = shape(4, r, 384) if first_y else shape(r, 384)
        along = shape(3, r, 384) if first_y else shape(2, 3, r, 384)
        return [shape(2, 4, r, 384), over, along, along, shape(2, 4, r, 384), dma((3,)), dma((8,))]

    scratch = [
        shape(1024, 768), shape(272, 768, dtype=f32), shape(1024, 768),
        shape(1024, 192), shape(1024, 192), shape(192, 1024), shape(192, 1024),
        shape(4, 192, 768), shape(4, 768, 192),
        shape(1024, B, dtype=i32), shape(4, 8, B, dtype=i32),
        shape(3, TOP, 768), shape(1024, 768), shape(4, 3, 8, B, dtype=f32),
        shape(192, 1024), shape(4, 4, 384, 128), shape(4, 192, 768), shape(1024, 768),
        shape(1024, 768), shape(1024, 768), shape(1024, 768), shape(1024, 768),
        shape(192, 768), shape(768, 192), shape(8, 768, dtype=f32),
        shape(1024, 192, dtype=f32), shape(1024, 192, dtype=f32), shape(B, 768, dtype=f32),
        shape(3, B, 768), shape(2, B, 768), shape(B, 768),
        shape(3, B, 768), shape(2, B, 768), shape(B, 768), shape(B, 768, dtype=f32),
        shape(8, 768, dtype=f32),
        shape(16, 768, dtype=f32), shape(4, 16, 768, dtype=f32), shape(16, 768, dtype=f32), shape(4, 16, 768, dtype=f32),
    ]
    one, three = dma((1,)), dma((3,))
    scratch += [one, three, one, three, one, dma((4, 3)), one, three] + [one, three] * 3
    scratch += [three, dma((7,)), dma((7,)), dma((15,))]
    scratch += [shape(4 * share, 768), shape(3, 192, 768), shape(768, 768), shape(768, 768), shape(share, 768)]
    scratch += [[shape(768)] * 7, shape(2, 192), shape(B, 768, dtype=f32), shape(B, 768, dtype=f32)]
    scratch += [shape(16, 768, dtype=f32), pltpu.SMEM(image_of_row.shape, i32)]
    scratch += [[block_scratch(first_y, r) for first_y, r in zip(FIRST_Y, QUARTER)]]
    results = pl.pallas_call(
        layer_kernel,
        out_shape=[
            jax.ShapeDtypeStruct((B, 768), f32),
            jax.ShapeDtypeStruct((B, 768), f32),
            jax.ShapeDtypeStruct((16, 768), f32),
            jax.ShapeDtypeStruct((3, 2, 4, 64, 384), bf16),
            jax.ShapeDtypeStruct((3, 2, 4, 64, 384), bf16),
            jax.ShapeDtypeStruct((1, 2, 4, 48, 384), bf16),
            jax.ShapeDtypeStruct((3, 2, 4, 48, 384), bf16),
        ],
        in_specs=[anyspace] * 15,
        out_specs=[anyspace] * 7,
        scratch_shapes=scratch,
        compiler_params=pltpu.CompilerParams(
            collective_id=0, has_side_effects=True, vmem_limit_bytes=60 * 2**20
        ),
        name="layer",
    )(
        inputs, image_of_row, gain_first, shift_first, qv_bias, out_bias, gain_second, shift_second, up_bias, down_bias,
        jnp.swapaxes(qkv_weight, 1, 2), out_weight, up_weight, down_weight, cotangent,
    )

    def out(*dims):
        return jax.ShapeDtypeStruct(dims, f32)

    wide = [shape(share, 768, dtype=f32)] * 2 + [shape(768, 768, dtype=f32)] * 2
    outputs = pl.pallas_call(
        finish_kernel,
        out_shape=[
            out(share, 768), out(share, 768), out(768), out(768), out(3, 192, 768), out(2, 192), out(192, 768),
            out(768), out(768), out(768), out(768, 768), out(768), out(768, 768), out(768),
        ],
        in_specs=[anyspace] * 7,
        out_specs=[anyspace if k in (0, 1, 4, 6, 10, 12) else vmem for k in range(14)],
        scratch_shapes=[pltpu.VMEM(r.shape, r.dtype) for r in results]
        + wide + [shape(192, 768, dtype=f32), shape(3, 192, 768, dtype=f32), dma((13,)), dma((12,))],
        compiler_params=pltpu.CompilerParams(vmem_limit_bytes=60 * 2**20),
        name="finish",
    )(*results)
    return (*outputs[:4], jnp.swapaxes(outputs[4], 1, 2), *outputs[5:])


def solution(mesh):
    return jax.shard_map(
        per_device,
        mesh=mesh,
        in_specs=(
            P("dp", None),
            P("dp"),
            P(),
            P(),
            P(None, None, "mp"),
            P(None, "mp"),
            P("mp", None),
            P(),
            P(),
            P(),
            P(None, "mp"),
            P("mp"),
            P("mp", None),
            P(),
            P(("dp", "mp"), None),
        ),
        out_specs=(
            P(("dp", "mp"), None),
            P(("dp", "mp"), None),
            P(),
            P(),
            P(None, None, "mp"),
            P(None, "mp"),
            P("mp", None),
            P(),
            P(),
            P(),
            P(None, "mp"),
            P("mp"),
            P("mp", None),
            P(),
        ),
        check_vma=False,
    )
```
